32 devices in a mesh: replica: 4 (over y, core), fsdp: 8 (over z, x).
Axes of the slice: x: 2, y: 2, z: 4, core: 2. Of those that a mesh axis runs over, the one named last changes fastest.
Arguments:
- tokens: bfloat16 [4, 6144, 8192], P('replica', 'fsdp'), may hold values from -6 to 6
- cotangent: bfloat16 [4, 6144, 512], P('replica', 'fsdp'), may hold values from -6 to 6
- params: float32 [4, 8192, 512], P('replica', 'fsdp'), may hold values from -0.0625 to 0.0625
- adam_m: float32 [4, 8192, 512], P('replica', 'fsdp'), may hold values from -0.046875 to 0.046875
- adam_v: float32 [4, 8192, 512], P('replica', 'fsdp'), may hold values from 1e-06 to 0.0001
- anchor: float32 [8192, 128], P('fsdp'), may hold values from -0.0625 to 0.0625
- momentum: float32 [8192, 128], P('fsdp'), may hold values from -0.046875 to 0.046875
- delta: float32 [4, 8192, 128], P('replica', 'fsdp'), may hold values from -0.078125 to 0.078125
- fragment: int32 [1], replicated, may hold values from 0 to 3
Outputs:
- new_params: float32 [4, 8192, 512], P('replica', 'fsdp')
- new_m: float32 [4, 8192, 512], P('replica', 'fsdp')
- new_v: float32 [4, 8192, 512], P('replica', 'fsdp')
- new_anchor: float32 [8192, 128], P('fsdp')
- new_momentum: float32 [8192, 128], P('fsdp')
The draws below stay inside these ranges and needn't reach their ends.
All inputs are finite; a program needn't handle non-finite values.
Results may differ from the reference program's by a relative error of at most 0.0017.
Values may be sent and summed in bfloat16 or wider, within the bound.
No kernel may reach another device: no remote copies, remote signals or barrier semaphores. Data moves between devices by JAX's collectives and lax.ppermute only.
A program may use at most 128 MiB of HBM per device.

```python
import math
import jax
import jax.numpy as jnp
from jax import lax

D = 8192
HEAD_DIM = 128
KV_HEADS = 4
TOK_DEV = 768
INNER_STEPS = 2
E = 512
ROWS = 6144
N_REPLICA = 4
N_FSDP = 8


def steps_of(rng, dims, split, least, top_value):
    def one(axis_at, parts):
        steps = jax.random.uniform(jax.random.fold_in(jax.random.fold_in(rng, 6), axis_at), (parts,), jnp.float32, least / len(split), top_value / len(split))
        return jnp.repeat(jnp.exp(steps), dims[axis_at] // parts).reshape((-1,) + (1,) * (len(dims) - axis_at - 1))

    factor_of = one(*split[0])
    for cut in split[1:]:
        factor_of = factor_of * one(*cut)
    return factor_of


def noise(stream_key, dims, width, most, pieces=(), kind=jnp.bfloat16):
    result = jax.random.normal(stream_key, dims, jnp.float32) * width
    if len(pieces) > 0:
        result = steps_of(stream_key, dims, pieces, -0.22, 0.18) * result
    return jnp.clip(result, min=-most, max=most).astype(kind)


def setup_inputs(seed: int = 0) -> dict:
    arg_keys = jax.random.split(jax.random.key(seed), 10)
    tokens = noise(arg_keys[0], (N_REPLICA, ROWS, D), 1.0, 6.0, ((0, 4), (1, 8)))
    cotangent = noise(arg_keys[1], (N_REPLICA, ROWS, E), 1.0, 6.0, ((0, 4), (1, 8)))
    params = noise(arg_keys[2], (N_REPLICA, D, E), D ** -0.5, 0.0625, ((0, 4), (1, 8)), jnp.float32)
    adam_m = noise(arg_keys[3], (N_REPLICA, D, E), 0.003, 0.046875, ((0, 4), (1, 8)), jnp.float32)
    adam_v = jnp.clip(jnp.exp(math.log(0.0001) - 4.6051702 * jax.random.uniform(arg_keys[4], (N_REPLICA, D, E), jnp.float32) ** steps_of(arg_keys[4], (N_REPLICA, D, E), ((0, 4), (1, 8)), -0.2, 0.2)), 9.999999974752427e-07, 0.0001)
    anchor = noise(arg_keys[5], (D, HEAD_DIM), D ** -0.5, 0.0625, ((0, 8),), jnp.float32)
    momentum = noise(arg_keys[6], (D, HEAD_DIM), 0.003, 0.046875, ((0, 8),), jnp.float32)
    delta = noise(arg_keys[7], (N_REPLICA, D, HEAD_DIM), 0.005, 0.078125, ((0, 4), (1, 8)), jnp.float32)
    fragment = jax.random.randint(arg_keys[8], (1,), 0, KV_HEADS).astype(jnp.int32)
    return dict(tokens=tokens, cotangent=cotangent, params=params, adam_m=adam_m, adam_v=adam_v, anchor=anchor, momentum=momentum, delta=delta, fragment=fragment)


beta_one = 0.9
beta_two = 0.95
adam_eps = 1e-08
learn_rate = 0.002
weight_decay = 0.1
outer_rate = 0.7
outer_momentum = 0.9
mixing = 0.5

def norm_rows(values):
    floats = values.astype(jnp.float32)
    scale = lax.rsqrt(lax.optimization_barrier(jnp.mean(floats * floats, axis=-1, keepdims=True)) + 1e-05)
    return (floats * scale).astype(jnp.bfloat16)

def key_gradient(keys, cotan, rows):
    count = keys.shape[0]
    heads = keys.reshape(count, KV_HEADS, HEAD_DIM)
    inverse = lax.rsqrt(lax.optimization_barrier(jnp.mean(heads * heads, axis=-1, keepdims=True)) + 1e-06)
    unit = heads * inverse
    upstream = cotan.astype(jnp.float32).reshape(count, KV_HEADS, HEAD_DIM) / rows
    grads = inverse * (upstream - unit * lax.optimization_barrier(jnp.mean(upstream * unit, axis=-1, keepdims=True)))
    return grads.reshape(count, KV_HEADS * HEAD_DIM).astype(jnp.bfloat16)

def adam_update(weight, first, second, grad, stamp):
    first = beta_one * first + (1.0 - beta_one) * grad
    second = beta_two * second + (1.0 - beta_two) * grad * grad
    fix_one = 1.0 - beta_one ** stamp
    fix_two = 1.0 - beta_two ** stamp
    ratio = first / fix_one / (jnp.sqrt(second / fix_two) + adam_eps)
    weight = weight - learn_rate * (ratio + weight_decay * weight)
    return (weight, first, second)

def block_grad(normed, key_grad):
    return lax.dot_general(normed, key_grad, (((0,), (0,)), ((), ())), preferred_element_type=jnp.float32)

def reference(tokens, cotangent, params, adam_m, adam_v, anchor, momentum, delta, fragment):
    average = lax.optimization_barrier(jnp.sum(delta, axis=0)) / N_REPLICA
    new_momentum = outer_momentum * momentum + average
    new_anchor = anchor - outer_rate * (outer_momentum * new_momentum + average)
    offset = (fragment[0] * HEAD_DIM).astype(jnp.int32)
    rows = TOK_DEV * N_FSDP
    out_w, out_m, out_v = ([], [], [])
    for replica_id in range(N_REPLICA):
        normed = norm_rows(tokens[replica_id])
        weight, first, second = (params[replica_id], adam_m[replica_id], adam_v[replica_id])
        for inner in range(INNER_STEPS):
            if inner == 1:
                columns = lax.dynamic_slice_in_dim(weight, offset, HEAD_DIM, 1)
                merged = mixing * columns + (1.0 - mixing) * new_anchor
                weight = lax.dynamic_update_slice_in_dim(weight, merged, offset, 1)
            keys = jnp.dot(normed, weight.astype(jnp.bfloat16), preferred_element_type=jnp.float32)
            key_grad = key_gradient(keys, cotangent[replica_id], rows)
            grad = block_grad(normed, key_grad)
            weight, first, second = adam_update(weight, first, second, grad, inner + 1)
        out_w.append(weight)
        out_m.append(first)
        out_v.append(second)
    return (jnp.stack(out_w), jnp.stack(out_m), jnp.stack(out_v), new_anchor, new_momentum)
```

```python
import jax
import jax.numpy as jnp
from jax import lax
from jax.sharding import PartitionSpec as P

HEAD_DIM = 128
KV_HEADS = 4
INNER_STEPS = 2
UNIT_HEADS = 2
RING_MOST = 8
SENT = jnp.float16
SCALE = 1.0 / 128


beta_one = 0.9
beta_two = 0.95
adam_eps = 1e-08
learn_rate = 0.002
weight_decay = 0.1
outer_rate = 0.7
outer_momentum = 0.9
mixing = 0.5


def norm_rows(values):
    floats = values.astype(jnp.float32)
    scale = lax.rsqrt(jnp.mean(floats * floats, axis=-1, keepdims=True) + 1e-05)
    return (floats * scale).astype(jnp.bfloat16)


def key_gradient(keys, cotan, rows):
    count = keys.shape[0]
    heads = keys.reshape(count, -1, HEAD_DIM)
    inverse = lax.rsqrt(jnp.mean(heads * heads, axis=-1, keepdims=True) + 1e-06)
    unit = heads * inverse
    upstream = cotan.astype(jnp.float32).reshape(count, -1, HEAD_DIM) / rows
    grads = inverse * (upstream - unit * jnp.mean(upstream * unit, axis=-1, keepdims=True))
    return grads.reshape(keys.shape).astype(jnp.bfloat16)


def adam_update(weight, first, second, grad, stamp):
    first = beta_one * first + (1.0 - beta_one) * grad
    second = beta_two * second + (1.0 - beta_two) * grad * grad
    fix_one = 1.0 - beta_one**stamp
    fix_two = 1.0 - beta_two**stamp
    ratio = first / fix_one / (jnp.sqrt(second / fix_two) + adam_eps)
    weight = weight - learn_rate * (ratio + weight_decay * weight)
    return (weight, first, second)


def outer_update(delta_rows, anchor, momentum):
    count = lax.axis_size("replica")
    total = lax.psum(delta_rows, "replica")
    average = total / count
    fresh_mom = outer_momentum * momentum + average
    fresh_anchor = anchor - outer_rate * (outer_momentum * fresh_mom + average)
    return (fresh_anchor, fresh_mom)


def ring_of(count):
    half = count // 2
    return [2 * p if p < half else 2 * (count - 1 - p) + 1 for p in range(count)]


def on_device(tokens, cotangent, params, adam_m, adam_v, anchor, momentum, delta, fragment):
    count = lax.axis_size("fsdp")
    half = count // 2
    ringed = count % 2 == 0 and count <= RING_MOST
    ring = ring_of(count)
    onward = [(ring[p], ring[(p + 1) % count]) for p in range(count)]
    back = [(ring[(p + 1) % count], ring[p]) for p in range(count)]
    index = lax.axis_index("fsdp")
    place = jnp.where(index % 2 == 0, index // 2, count - 1 - index // 2)

    cotan = cotangent[0]
    depth, width = params.shape[1:]
    unit_cols = UNIT_HEADS * HEAD_DIM
    units = width // unit_cols
    rows = tokens.shape[1] * count

    def cols_of(array, unit):
        return lax.slice_in_dim(array, unit * unit_cols, (unit + 1) * unit_cols, axis=1)

    weights = [cols_of(params[0], u) for u in range(units)]
    firsts = [cols_of(adam_m[0], u) for u in range(units)]
    seconds = [cols_of(adam_v[0], u) for u in range(units)]
    cotans = [cols_of(cotan, u) for u in range(units)]

    normed = norm_rows(tokens[0])
    normed_at = []
    for k in range(count if ringed else 0):
        spot = (place + k) % count
        owner = jnp.where(spot < half, 2 * spot, 2 * (count - 1 - spot) + 1)
        normed_at.append(lax.dynamic_slice_in_dim(normed, owner * depth, depth, 1))

    def gather_whole(current):
        every = lax.all_gather(current.astype(jnp.bfloat16), "fsdp", axis=0, tiled=True)
        return jnp.dot(normed, every, preferred_element_type=jnp.float32)

    def scatter_whole(key_grad):
        part = lax.dot_general(
            normed, key_grad, (((0,), (0,)), ((), ())), preferred_element_type=jnp.float32
        )
        return lax.psum_scatter(part, "fsdp", scatter_dimension=0, tiled=True)

    def add_rows(k, piece):
        return jnp.dot(normed_at[k], piece, preferred_element_type=jnp.float32)

    def gather_keys(current):
        own = current.astype(jnp.bfloat16)
        keys = add_rows(0, own)
        left, right = own, own
        for k in range(1, half):
            left = lax.ppermute(left, "fsdp", onward)
            right = lax.ppermute(right, "fsdp", back)
            keys = keys + add_rows(count - k, left) + add_rows(k, right)
        top = lax.ppermute(left[: depth // 2], "fsdp", onward)
        low = lax.ppermute(right[depth // 2 :], "fsdp", back)
        return keys + add_rows(half, jnp.concatenate([top, low], 0))

    def grad_part(k, key_grad):
        return lax.dot_general(
            normed_at[k], key_grad, (((0,), (0,)), ((), ())), preferred_element_type=jnp.float32
        )

    def scatter_grad(key_grad):
        far = (SCALE * grad_part(half, key_grad)).astype(SENT)
        right = lax.ppermute(far[: depth // 2], "fsdp", onward)
        left = lax.ppermute(far[depth // 2 :], "fsdp", back)
        zeros = jnp.zeros_like(right)
        right = jnp.concatenate([right, zeros], 0)
        left = jnp.concatenate([zeros, left], 0)
        for k in range(half - 1, 0, -1):
            right = (SCALE * grad_part(k, key_grad) + right.astype(jnp.float32)).astype(SENT)
            left = (SCALE * grad_part(count - k, key_grad) + left.astype(jnp.float32)).astype(SENT)
            right = lax.ppermute(right, "fsdp", onward)
            left = lax.ppermute(left, "fsdp", back)
        return grad_part(0, key_grad) + (right.astype(jnp.float32) + left.astype(jnp.float32)) / SCALE

    gather, scatter = (gather_keys, scatter_grad) if ringed else (gather_whole, scatter_whole)
    new_anchor, new_momentum = outer_update(delta[0], anchor, momentum)
    for inner in range(INNER_STEPS):
        for u in range(units):
            weight = weights[u]
            if inner == 1:
                blocks = []
                for h in range(UNIT_HEADS):
                    block = lax.slice_in_dim(weight, h * HEAD_DIM, (h + 1) * HEAD_DIM, axis=1)
                    merged = mixing * block + (1.0 - mixing) * new_anchor
                    blocks.append(jnp.where(fragment[0] == u * UNIT_HEADS + h, merged, block))
                weight = jnp.concatenate(blocks, 1) if UNIT_HEADS > 1 else blocks[0]
            key_grad = key_gradient(gather(weight), cotans[u], rows)
            grad = scatter(key_grad)
            weights[u], firsts[u], seconds[u] = adam_update(
                weight, firsts[u], seconds[u], grad, inner + 1
            )

    def whole(pieces):
        return jnp.concatenate(pieces, 1)[None]

    return (whole(weights), whole(firsts), whole(seconds), new_anchor, new_momentum)


def solution(mesh):
    return jax.shard_map(
        on_device,
        mesh=mesh,
        in_specs=(
            P("replica", "fsdp", None),
            P("replica", "fsdp", None),
            P("replica", "fsdp", None),
            P("replica", "fsdp", None),
            P("replica", "fsdp", None),
            P("fsdp", None),
            P("fsdp", None),
            P("replica", "fsdp", None),
            P(),
        ),
        out_specs=(
            P("replica", "fsdp", None),
            P("replica", "fsdp", None),
            P("replica", "fsdp", None),
            P("fsdp", None),
            P("fsdp", None),
        ),
        check_vma=False,
    )
```

```python
import functools

import jax
import jax.numpy as jnp
from jax import lax
from jax.experimental import pallas as pl
from jax.experimental.layout import Layout, with_layout_constraint
from jax.experimental.pallas import tpu as pltpu
from jax.sharding import PartitionSpec as P

HEAD_DIM = 128
KV_HEADS = 4
INNER_STEPS = 2
UNIT_HEADS = 2
RING_MOST = 8
NORM_TILE = 64
KEY_TILE = 256
ADAM_TILE = 256
SENT = jnp.float16
SCALE = 1.0 / 128


beta_one = 0.9
beta_two = 0.95
adam_eps = 1e-08
learn_rate = 0.002
weight_decay = 0.1
outer_rate = 0.7
outer_momentum = 0.9
mixing = 0.5


def norm_kernel(values, out):
    floats = values[...].astype(jnp.float32)
    scale = lax.rsqrt(jnp.mean(floats * floats, axis=-1, keepdims=True) + 1e-05)
    out[...] = (floats * scale).astype(jnp.bfloat16)


def norm_rows(values):
    rows, width = values.shape
    tile = NORM_TILE if rows % NORM_TILE == 0 else rows
    block = pl.BlockSpec((tile, width), lambda i: (i, 0))
    return pl.pallas_call(
        norm_kernel,
        grid=(rows // tile,),
        in_specs=[block],
        out_specs=block,
        out_shape=jax.ShapeDtypeStruct(values.shape, jnp.bfloat16),
        cost_estimate=pl.CostEstimate(
            flops=8 * rows * width, bytes_accessed=4 * rows * width, transcendentals=rows
        ),
        compiler_params=pltpu.CompilerParams(vmem_limit_bytes=16 * 2**20),
    )(values)


def key_kernel(rows, keys, cotan, out):
    for h in range(keys.shape[1] // HEAD_DIM):
        spot = pl.ds(h * HEAD_DIM, HEAD_DIM)
        head = keys[:, spot]
        inverse = lax.rsqrt(jnp.mean(head * head, axis=-1, keepdims=True) + 1e-06)
        unit = head * inverse
        upstream = cotan[:, spot].astype(jnp.float32) / rows
        grads = inverse * (upstream - unit * jnp.mean(upstream * unit, axis=-1, keepdims=True))
        out[:, spot] = grads.astype(jnp.bfloat16)


def key_gradient(keys, cotan, unit, rows):
    count, cols = keys.shape
    tile = KEY_TILE if count % KEY_TILE == 0 else count
    block = pl.BlockSpec((tile, cols), lambda i: (i, 0))
    return pl.pallas_call(
        functools.partial(key_kernel, rows),
        grid=(count // tile,),
        in_specs=[block, pl.BlockSpec((tile, cols), lambda i: (i, unit))],
        out_specs=block,
        out_shape=jax.ShapeDtypeStruct(keys.shape, jnp.bfloat16),
        cost_estimate=pl.CostEstimate(
            flops=12 * count * cols, bytes_accessed=8 * count * cols, transcendentals=count
        ),
        compiler_params=pltpu.CompilerParams(vmem_limit_bytes=16 * 2**20),
    )(keys, cotan)


def adam_update(weight, first, second, grad, stamp):
    first = beta_one * first + (1.0 - beta_one) * grad
    second = beta_two * second + (1.0 - beta_two) * grad * grad
    fix_one = 1.0 - beta_one**stamp
    fix_two = 1.0 - beta_two**stamp
    ratio = first / fix_one / (jnp.sqrt(second / fix_two) + adam_eps)
    weight = weight - learn_rate * (ratio + weight_decay * weight)
    return (weight, first, second)


def first_kernel(stamp, unit, fragment, anchor, weight, first, second, grad, out_w, out_m, out_v, own):
    fresh, out_m[...], out_v[...] = adam_update(
        weight[...], first[...], second[...], grad[...], stamp
    )
    heads = fresh.shape[1] // HEAD_DIM
    for h in range(heads):
        head = fresh[:, h * HEAD_DIM : (h + 1) * HEAD_DIM]
        merged = mixing * head + (1.0 - mixing) * anchor[...]
        head = jnp.where(fragment[0] == unit * heads + h, merged, head)
        out_w[:, pl.ds(h * HEAD_DIM, HEAD_DIM)] = head
        own[:, pl.ds(h * HEAD_DIM, HEAD_DIM)] = head.astype(jnp.bfloat16)


def first_update(stamp, unit, fragment, anchor, weight, first, second, grad):
    rows, cols = grad.shape
    tile = min(rows, ADAM_TILE)
    block = pl.BlockSpec((tile, cols), lambda i: (i, 0))
    spot = pl.BlockSpec((tile, cols), lambda i: (i, unit))
    side = pl.BlockSpec((tile, HEAD_DIM), lambda i: (i, 0))
    return pl.pallas_call(
        functools.partial(first_kernel, stamp, unit),
        grid=(rows // tile,),
        in_specs=[pl.BlockSpec(memory_space=pltpu.SMEM), side, spot, spot, spot, block],
        out_specs=[block] * 4,
        out_shape=[jax.ShapeDtypeStruct((rows, cols), jnp.float32)] * 3
        + [jax.ShapeDtypeStruct((rows, cols), jnp.bfloat16)],
        cost_estimate=pl.CostEstimate(
            flops=24 * rows * cols, bytes_accessed=32 * rows * cols, transcendentals=rows * cols
        ),
        compiler_params=pltpu.CompilerParams(vmem_limit_bytes=16 * 2**20),
    )(fragment, anchor, weight, first, second, grad)


def last_kernel(stamp, weight, first, second, grad, *rest):
    for out, value in zip(
        rest[-3:], adam_update(weight[...], first[...], second[...], grad[...], stamp)
    ):
        out[...] = value


def last_update(stamp, unit, width, weight, first, second, grad, before):
    rows, cols = grad.shape
    tile = min(rows, ADAM_TILE)
    block = pl.BlockSpec((tile, cols), lambda i: (i, 0))
    spot = pl.BlockSpec((tile, cols), lambda i: (i, unit))
    return pl.pallas_call(
        functools.partial(last_kernel, stamp),
        grid=(rows // tile,),
        in_specs=[block] * 4 + [pl.BlockSpec(memory_space=pl.ANY)] * len(before),
        out_specs=[spot] * 3,
        out_shape=[jax.ShapeDtypeStruct((rows, width), jnp.float32)] * 3,
        input_output_aliases={4 + i: i for i in range(len(before))},
        cost_estimate=pl.CostEstimate(
            flops=20 * rows * cols, bytes_accessed=28 * rows * cols, transcendentals=rows * cols
        ),
        compiler_params=pltpu.CompilerParams(vmem_limit_bytes=16 * 2**20),
    )(weight, first, second, grad, *before)


def by_rows(array):
    return with_layout_constraint(array, Layout(major_to_minor=(0, 1)))


def outer_update(total, anchor, momentum):
    average = total / lax.axis_size("replica")
    fresh_mom = outer_momentum * momentum + average
    fresh_anchor = anchor - outer_rate * (outer_momentum * fresh_mom + average)
    return (fresh_anchor, fresh_mom)


def ring_of(count):
    half = count // 2
    return [2 * p if p < half else 2 * (count - 1 - p) + 1 for p in range(count)]


def on_device(tokens, cotangent, params, adam_m, adam_v, anchor, momentum, delta, fragment):
    count = lax.axis_size("fsdp")
    half = count // 2
    ringed = count % 2 == 0 and count <= RING_MOST
    ring = ring_of(count)
    onward = [(ring[p], ring[(p + 1) % count]) for p in range(count)]
    back = [(ring[(p + 1) % count], ring[p]) for p in range(count)]
    index = lax.axis_index("fsdp")
    place = jnp.where(index % 2 == 0, index // 2, count - 1 - index // 2)

    cotan = cotangent[0]
    depth, width = params.shape[1:]
    unit_cols = UNIT_HEADS * HEAD_DIM
    units = width // unit_cols
    rows = tokens.shape[1] * count

    owns = [
        by_rows(params[0, :, u * unit_cols : (u + 1) * unit_cols].astype(jnp.bfloat16))
        for u in range(units)
    ]

    normed = norm_rows(tokens[0])
    normed_at = []
    for k in range(count if ringed else 0):
        spot = (place + k) % count
        owner = jnp.where(spot < half, 2 * spot, 2 * (count - 1 - spot) + 1)
        normed_at.append(lax.dynamic_slice_in_dim(normed, owner * depth, depth, 1))

    def gather_whole(current, after=None):
        every = lax.all_gather(current, "fsdp", axis=0, tiled=True)
        return jnp.dot(normed, every, preferred_element_type=jnp.float32), every

    def scatter_whole(key_grad):
        part = lax.dot_general(
            normed, key_grad, (((0,), (0,)), ((), ())), preferred_element_type=jnp.float32
        )
        return lax.psum_scatter(part, "fsdp", scatter_dimension=0, tiled=True)

    def add_rows(k, piece):
        return jnp.dot(normed_at[k], piece, preferred_element_type=jnp.float32)

    def gather_keys(current, after=None):
        own = current
        if after is not None:
            own, _ = lax.optimization_barrier((own, after))
        keys = add_rows(0, own)
        left, right = own, own
        for k in range(1, half):
            left = lax.ppermute(left, "fsdp", onward)
            right = lax.ppermute(right, "fsdp", back)
            keys = keys + add_rows(count - k, left) + add_rows(k, right)
        top = lax.ppermute(left[: depth // 2], "fsdp", onward)
        low = lax.ppermute(right[depth // 2 :], "fsdp", back)
        return keys + add_rows(half, jnp.concatenate([top, low], 0)), (left, right)

    def grad_part(k, key_grad):
        return lax.dot_general(
            normed_at[k], key_grad, (((0,), (0,)), ((), ())), preferred_element_type=jnp.float32
        )

    def scatter_grad(key_grad):
        far = by_rows((SCALE * grad_part(half, key_grad)).astype(SENT))
        right = lax.ppermute(far[: depth // 2], "fsdp", onward)
        left = lax.ppermute(far[depth // 2 :], "fsdp", back)
        zeros = jnp.zeros_like(right)
        right = jnp.concatenate([right, zeros], 0)
        left = jnp.concatenate([zeros, left], 0)
        for k in range(half - 1, 0, -1):
            right = SCALE * grad_part(k, key_grad) + right.astype(jnp.float32)
            left = SCALE * grad_part(count - k, key_grad) + left.astype(jnp.float32)
            right, left = by_rows(right.astype(SENT)), by_rows(left.astype(SENT))
            right = lax.ppermute(right, "fsdp", onward)
            left = lax.ppermute(left, "fsdp", back)
        return grad_part(0, key_grad) + (right.astype(jnp.float32) + left.astype(jnp.float32)) / SCALE

    gather, scatter = (gather_keys, scatter_grad) if ringed else (gather_whole, scatter_whole)
    total = lax.psum(delta[0], "replica")
    results = ()
    first_sent = None
    states = [None] * units
    for inner in range(INNER_STEPS):
        for u in range(units):
            keys, sent = gather(owns[u], first_sent if inner == 0 else None)
            first_sent = sent
            if inner == 0 and u == 0:
                keys, total = lax.optimization_barrier((keys, total))
                new_anchor, new_momentum = outer_update(total, anchor, momentum)
            grad = scatter(key_gradient(keys, cotan, u, rows))
            if inner == 0:
                *states[u], owns[u] = first_update(
                    1, u, fragment, new_anchor, params[0], adam_m[0], adam_v[0], grad
                )
            else:
                results = last_update(inner + 1, u, width, *states[u], grad, results)

    return (*(out[None] for out in results), new_anchor, new_momentum)


def solution(mesh):
    return jax.shard_map(
        on_device,
        mesh=mesh,
        in_specs=(
            P("replica", "fsdp", None),
            P("replica", "fsdp", None),
            P("replica", "fsdp", None),
            P("replica", "fsdp", None),
            P("replica", "fsdp", None),
            P("fsdp", None),
            P("fsdp", None),
            P("replica", "fsdp", None),
            P(),
        ),
        out_specs=(
            P("replica", "fsdp", None),
            P("replica", "fsdp", None),
            P("replica", "fsdp", None),
            P("fsdp", None),
            P("fsdp", None),
        ),
        check_vma=False,
    )
```

```python
import functools

import jax
import jax.numpy as jnp
from jax import lax
from jax.experimental import pallas as pl
from jax.experimental.layout import Layout, with_layout_constraint
from jax.experimental.pallas import tpu as pltpu
from jax.sharding import PartitionSpec as P

HEAD_DIM = 128
KV_HEADS = 4
INNER_STEPS = 2
UNIT_HEADS = 2
RING_MOST = 8
NORM_TILE = 64
KEY_TILE = 256
ADAM_TILE = 256
VMEM_BYTES = 10 * 2**20
SENT = jnp.float16
SCALE = 1.0 / 128


beta_one = 0.9
beta_two = 0.95
adam_eps = 1e-08
learn_rate = 0.002
weight_decay = 0.1
outer_rate = 0.7
outer_momentum = 0.9
mixing = 0.5


def norm_kernel(values, out):
    floats = values[...].astype(jnp.float32)
    scale = lax.rsqrt(jnp.mean(floats * floats, axis=-1, keepdims=True) + 1e-05)
    out[...] = (floats * scale).astype(jnp.bfloat16)


def norm_rows(values):
    rows, width = values.shape
    tile = NORM_TILE if rows % NORM_TILE == 0 else rows
    block = pl.BlockSpec((tile, width), lambda i: (i, 0))
    return pl.pallas_call(
        norm_kernel,
        grid=(rows // tile,),
        in_specs=[block],
        out_specs=block,
        out_shape=jax.ShapeDtypeStruct(values.shape, jnp.bfloat16),
        cost_estimate=pl.CostEstimate(
            flops=8 * rows * width, bytes_accessed=4 * rows * width, transcendentals=rows
        ),
        compiler_params=pltpu.CompilerParams(vmem_limit_bytes=VMEM_BYTES),
    )(values)


def key_kernel(rows, keys, cotan, out):
    for h in range(keys.shape[1] // HEAD_DIM):
        spot = pl.ds(h * HEAD_DIM, HEAD_DIM)
        head = keys[:, spot]
        inverse = lax.rsqrt(jnp.mean(head * head, axis=-1, keepdims=True) + 1e-06)
        unit = head * inverse
        upstream = cotan[:, spot].astype(jnp.float32) / rows
        grads = inverse * (upstream - unit * jnp.mean(upstream * unit, axis=-1, keepdims=True))
        out[:, spot] = grads.astype(jnp.bfloat16)


def key_gradient(keys, cotan, unit, rows):
    count, cols = keys.shape
    tile = KEY_TILE if count % KEY_TILE == 0 else count
    block = pl.BlockSpec((tile, cols), lambda i: (i, 0))
    return pl.pallas_call(
        functools.partial(key_kernel, rows),
        grid=(count // tile,),
        in_specs=[block, pl.BlockSpec((tile, cols), lambda i: (i, unit))],
        out_specs=block,
        out_shape=jax.ShapeDtypeStruct(keys.shape, jnp.bfloat16),
        cost_estimate=pl.CostEstimate(
            flops=12 * count * cols, bytes_accessed=8 * count * cols, transcendentals=count
        ),
        compiler_params=pltpu.CompilerParams(vmem_limit_bytes=VMEM_BYTES),
    )(keys, cotan)


def adam_update(weight, first, second, grad, stamp):
    first = beta_one * first + (1.0 - beta_one) * grad
    second = beta_two * second + (1.0 - beta_two) * grad * grad
    fix_one = 1.0 - beta_one**stamp
    fix_two = 1.0 - beta_two**stamp
    ratio = first / fix_one / (jnp.sqrt(second / fix_two) + adam_eps)
    weight = weight - learn_rate * (ratio + weight_decay * weight)
    return (weight, first, second)


def first_kernel(stamp, unit, fragment, anchor, weight, first, second, grad, out_w, out_m, out_v, own):
    fresh, out_m[...], out_v[...] = adam_update(
        weight[...], first[...], second[...], grad[...], stamp
    )
    heads = fresh.shape[1] // HEAD_DIM
    for h in range(heads):
        head = fresh[:, h * HEAD_DIM : (h + 1) * HEAD_DIM]
        merged = mixing * head + (1.0 - mixing) * anchor[...]
        head = jnp.where(fragment[0] == unit * heads + h, merged, head)
        out_w[:, pl.ds(h * HEAD_DIM, HEAD_DIM)] = head
        own[:, pl.ds(h * HEAD_DIM, HEAD_DIM)] = head.astype(jnp.bfloat16)


def first_update(stamp, unit, fragment, anchor, weight, first, second, grad):
    rows, cols = grad.shape
    tile = min(rows, ADAM_TILE)
    block = pl.BlockSpec((tile, cols), lambda i: (i, 0))
    spot = pl.BlockSpec((tile, cols), lambda i: (i, unit))
    side = pl.BlockSpec((tile, HEAD_DIM), lambda i: (i, 0))
    return pl.pallas_call(
        functools.partial(first_kernel, stamp, unit),
        grid=(rows // tile,),
        in_specs=[pl.BlockSpec(memory_space=pltpu.SMEM), side, spot, spot, spot, block],
        out_specs=[block] * 4,
        out_shape=[jax.ShapeDtypeStruct((rows, cols), jnp.float32)] * 3
        + [jax.ShapeDtypeStruct((rows, cols), jnp.bfloat16)],
        cost_estimate=pl.CostEstimate(
            flops=24 * rows * cols, bytes_accessed=32 * rows * cols, transcendentals=rows * cols
        ),
        compiler_params=pltpu.CompilerParams(vmem_limit_bytes=VMEM_BYTES),
    )(fragment, anchor, weight, first, second, grad)


def last_kernel(stamp, weight, first, second, grad, *rest):
    for out, value in zip(
        rest[-3:], adam_update(weight[...], first[...], second[...], grad[...], stamp)
    ):
        out[...] = value


def last_update(stamp, unit, width, weight, first, second, grad, before):
    rows, cols = grad.shape
    tile = min(rows, ADAM_TILE)
    block = pl.BlockSpec((tile, cols), lambda i: (i, 0))
    spot = pl.BlockSpec((tile, cols), lambda i: (i, unit))
    return pl.pallas_call(
        functools.partial(last_kernel, stamp),
        grid=(rows // tile,),
        in_specs=[block] * 4 + [pl.BlockSpec(memory_space=pl.ANY)] * len(before),
        out_specs=[spot] * 3,
        out_shape=[jax.ShapeDtypeStruct((rows, width), jnp.float32)] * 3,
        input_output_aliases={4 + i: i for i in range(len(before))},
        cost_estimate=pl.CostEstimate(
            flops=20 * rows * cols, bytes_accessed=28 * rows * cols, transcendentals=rows * cols
        ),
        compiler_params=pltpu.CompilerParams(vmem_limit_bytes=VMEM_BYTES),
    )(weight, first, second, grad, *before)


def by_rows(array):
    return with_layout_constraint(array, Layout(major_to_minor=(0, 1)))


def outer_update(total, anchor, momentum):
    average = total / lax.axis_size("replica")
    fresh_mom = outer_momentum * momentum + average
    fresh_anchor = anchor - outer_rate * (outer_momentum * fresh_mom + average)
    return (fresh_anchor, fresh_mom)


def ring_of(count):
    half = count // 2
    return [2 * p if p < half else 2 * (count - 1 - p) + 1 for p in range(count)]


def on_device(tokens, cotangent, params, adam_m, adam_v, anchor, momentum, delta, fragment):
    count = lax.axis_size("fsdp")
    half = count // 2
    ringed = count % 2 == 0 and count <= RING_MOST
    ring = ring_of(count)
    onward = [(ring[p], ring[(p + 1) % count]) for p in range(count)]
    back = [(ring[(p + 1) % count], ring[p]) for p in range(count)]
    index = lax.axis_index("fsdp")
    place = jnp.where(index % 2 == 0, index // 2, count - 1 - index // 2)

    cotan = cotangent[0]
    depth, width = params.shape[1:]
    unit_cols = UNIT_HEADS * HEAD_DIM
    units = width // unit_cols
    rows = tokens.shape[1] * count

    def own_of(source, unit):
        return by_rows(source[0, :, unit * unit_cols : (unit + 1) * unit_cols].astype(jnp.bfloat16))

    owns = [own_of(params, 0)]
    held = lax.optimization_barrier((params, owns[0]))[0]
    owns += [own_of(held, u) for u in range(1, units)]
    normed = norm_rows(tokens[0])
    normed_at = []
    for k in range(count if ringed else 0):
        spot = (place + k) % count
        owner = jnp.where(spot < half, 2 * spot, 2 * (count - 1 - spot) + 1)
        normed_at.append(lax.dynamic_slice_in_dim(normed, owner * depth, depth, 1))

    def pieces_of(block):
        return [block[: depth // 2], block[depth // 2 :]]

    def whole(pieces):
        return jnp.concatenate(pieces, 0) if len(pieces) > 1 else pieces[0]

    def gather_whole(current, split, after=None):
        every = lax.all_gather(current, "fsdp", axis=0, tiled=True)
        return jnp.dot(normed, every, preferred_element_type=jnp.float32), every, every

    def scatter_whole(key_grad, split, after=None):
        part = lax.dot_general(
            normed, key_grad, (((0,), (0,)), ((), ())), preferred_element_type=jnp.float32
        )
        return lax.psum_scatter(part, "fsdp", scatter_dimension=0, tiled=True)

    def add_rows(k, piece):
        return jnp.dot(normed_at[k], piece, preferred_element_type=jnp.float32)

    def gather_keys(current, split, after=None):
        own = current
        if after is not None:
            own, _ = lax.optimization_barrier((own, after))
        keys = add_rows(0, own)
        lefts = rights = pieces_of(own) if split else [own]
        first_hop = None
        for k in range(1, half):
            lefts = [lax.ppermute(piece, "fsdp", onward) for piece in lefts]
            rights = [lax.ppermute(piece, "fsdp", back) for piece in rights]
            first_hop = first_hop or (lefts, rights)
            keys = keys + add_rows(count - k, whole(lefts)) + add_rows(k, whole(rights))
        early = (lefts[-1], rights[0])
        top = lax.ppermute(pieces_of(whole(lefts))[0], "fsdp", onward)
        low = lax.ppermute(pieces_of(whole(rights))[1], "fsdp", back)
        return keys + add_rows(half, whole([top, low])), early, first_hop

    def scatter_grad(key_grad, split, after=None):
        parts = 2 if split else 1

        def term(k, part, parts):
            rows = depth // parts
            features = lax.slice_in_dim(normed_at[k], part * rows, (part + 1) * rows, axis=1)
            return lax.dot_general(
                features, key_grad, (((0,), (0,)), ((), ())), preferred_element_type=jnp.float32
            )

        def sends(k, arrived):
            return [
                by_rows((SCALE * term(k, i, parts) + a.astype(jnp.float32)).astype(SENT))
                for i, a in enumerate(arrived)
            ]

        far = [by_rows((SCALE * term(half, i, 2)).astype(SENT)) for i in range(2)]
        if after is not None:
            far, _ = lax.optimization_barrier((far, after))
        right = lax.ppermute(far[0], "fsdp", onward)
        left = lax.ppermute(far[1], "fsdp", back)
        zeros = jnp.zeros_like(right)
        rights, lefts = [right, zeros], [zeros, left]
        if not split:
            rights, lefts = [whole(rights)], [whole(lefts)]
        for k in range(half - 1, 0, -1):
            rights = [lax.ppermute(s, "fsdp", onward) for s in sends(k, rights)]
            lefts = [lax.ppermute(s, "fsdp", back) for s in sends(count - k, lefts)]
        arrived = whole(rights).astype(jnp.float32) + whole(lefts).astype(jnp.float32)
        return term(0, 0, 1) + arrived / SCALE

    gather, scatter = (gather_keys, scatter_grad) if ringed else (gather_whole, scatter_whole)
    total = lax.psum(delta[0], "replica")
    states = [None] * units
    key_grads = [None] * units
    early = first_hop = None
    for u in range(units):
        keys, early, hop = gather(owns[u], u == 0, early)
        first_hop = hop if u == 1 else first_hop
        if u == 0:
            keys, total = lax.optimization_barrier((keys, total))
            new_anchor, new_momentum = outer_update(total, anchor, momentum)
        key_grads[u] = key_gradient(keys, cotan, u, rows)
    for u in range(units):
        grad = scatter(key_grads[u], False, first_hop if u == 0 else None)
        *states[u], owns[u] = first_update(
            1, u, fragment, new_anchor, params[0], adam_m[0], adam_v[0], grad
        )
    results = ()
    for u in range(units):
        keys = gather(owns[u], False)[0]
        grad = scatter(key_gradient(keys, cotan, u, rows), u == units - 1)
        results = last_update(2, u, width, *states[u], grad, results)

    return (*(out[None] for out in results), new_anchor, new_momentum)


def solution(mesh):
    return jax.shard_map(
        on_device,
        mesh=mesh,
        in_specs=(
            P("replica", "fsdp", None),
            P("replica", "fsdp", None),
            P("replica", "fsdp", None),
            P("replica", "fsdp", None),
            P("replica", "fsdp", None),
            P("fsdp", None),
            P("fsdp", None),
            P("replica", "fsdp", None),
            P(),
        ),
        out_specs=(
            P("replica", "fsdp", None),
            P("replica", "fsdp", None),
            P("replica", "fsdp", None),
            P("fsdp", None),
            P("fsdp", None),
        ),
        check_vma=False,
    )
```

```python
import functools

import jax
import jax.numpy as jnp
from jax import lax
from jax.experimental import pallas as pl
from jax.experimental.layout import Layout, with_layout_constraint
from jax.experimental.pallas import tpu as pltpu
from jax.sharding import PartitionSpec as P

HEAD_DIM = 128
KV_HEADS = 4
INNER_STEPS = 2
UNIT_HEADS = 2
RING_MOST = 8
NORM_TILE = 64
KEY_TILE = 256
ADAM_TILE = 128
VMEM_BYTES = 10 * 2**20
SENT = jnp.float16
SCALE = 1.0 / 128


beta_one = 0.9
beta_two = 0.95
adam_eps = 1e-08
learn_rate = 0.002
weight_decay = 0.1
outer_rate = 0.7
outer_momentum = 0.9
mixing = 0.5


def norm_kernel(values, out):
    floats = values[...].astype(jnp.float32)
    scale = lax.rsqrt(jnp.mean(floats * floats, axis=-1, keepdims=True) + 1e-05)
    out[...] = (floats * scale).astype(jnp.bfloat16)


def norm_rows(values):
    rows, width = values.shape
    tile = NORM_TILE if rows % NORM_TILE == 0 else rows
    block = pl.BlockSpec((tile, width), lambda i: (i, 0))
    return pl.pallas_call(
        norm_kernel,
        grid=(rows // tile,),
        in_specs=[block],
        out_specs=block,
        out_shape=jax.ShapeDtypeStruct(values.shape, jnp.bfloat16),
        cost_estimate=pl.CostEstimate(
            flops=8 * rows * width, bytes_accessed=4 * rows * width, transcendentals=rows
        ),
        compiler_params=pltpu.CompilerParams(vmem_limit_bytes=VMEM_BYTES),
    )(values)


def key_kernel(rows, keys, cotan, out):
    for h in range(keys.shape[1] // HEAD_DIM):
        spot = pl.ds(h * HEAD_DIM, HEAD_DIM)
        head = keys[:, spot]
        inverse = lax.rsqrt(jnp.mean(head * head, axis=-1, keepdims=True) + 1e-06)
        unit = head * inverse
        upstream = cotan[:, spot].astype(jnp.float32) / rows
        grads = inverse * (upstream - unit * jnp.mean(upstream * unit, axis=-1, keepdims=True))
        out[:, spot] = grads.astype(jnp.bfloat16)


def key_gradient(keys, cotan, unit, rows):
    count, cols = keys.shape
    tile = KEY_TILE if count % KEY_TILE == 0 else count
    block = pl.BlockSpec((tile, cols), lambda i: (i, 0))
    return pl.pallas_call(
        functools.partial(key_kernel, rows),
        grid=(count // tile,),
        in_specs=[block, pl.BlockSpec((tile, cols), lambda i: (i, unit))],
        out_specs=block,
        out_shape=jax.ShapeDtypeStruct(keys.shape, jnp.bfloat16),
        cost_estimate=pl.CostEstimate(
            flops=12 * count * cols, bytes_accessed=8 * count * cols, transcendentals=count
        ),
        compiler_params=pltpu.CompilerParams(vmem_limit_bytes=VMEM_BYTES),
    )(keys, cotan)


def adam_update(weight, first, second, grad, stamp):
    first = beta_one * first + (1.0 - beta_one) * grad
    second = beta_two * second + (1.0 - beta_two) * grad * grad
    fix_one = 1.0 - beta_one**stamp
    fix_two = 1.0 - beta_two**stamp
    ratio = first / fix_one / (jnp.sqrt(second / fix_two) + adam_eps)
    weight = weight - learn_rate * (ratio + weight_decay * weight)
    return (weight, first, second)


def first_kernel(stamp, unit, fragment, anchor, weight, first, second, grad, out_w, out_m, out_v, own):
    fresh, out_m[...], out_v[...] = adam_update(
        weight[...], first[...], second[...], grad[...], stamp
    )
    heads = fresh.shape[1] // HEAD_DIM
    for h in range(heads):
        head = fresh[:, h * HEAD_DIM : (h + 1) * HEAD_DIM]
        merged = mixing * head + (1.0 - mixing) * anchor[...]
        head = jnp.where(fragment[0] == unit * heads + h, merged, head)
        out_w[:, pl.ds(h * HEAD_DIM, HEAD_DIM)] = head
        own[:, pl.ds(h * HEAD_DIM, HEAD_DIM)] = head.astype(jnp.bfloat16)


def first_update(stamp, unit, fragment, anchor, weight, first, second, grad):
    rows, cols = grad.shape
    tile = min(rows, ADAM_TILE)
    block = pl.BlockSpec((tile, cols), lambda i: (i, 0))
    spot = pl.BlockSpec((tile, cols), lambda i: (i, unit))
    side = pl.BlockSpec((tile, HEAD_DIM), lambda i: (i, 0))
    return pl.pallas_call(
        functools.partial(first_kernel, stamp, unit),
        grid=(rows // tile,),
        in_specs=[pl.BlockSpec(memory_space=pltpu.SMEM), side, spot, spot, spot, block],
        out_specs=[block] * 4,
        out_shape=[jax.ShapeDtypeStruct((rows, cols), jnp.float32)] * 3
        + [jax.ShapeDtypeStruct((rows, cols), jnp.bfloat16)],
        cost_estimate=pl.CostEstimate(
            flops=24 * rows * cols, bytes_accessed=32 * rows * cols, transcendentals=rows * cols
        ),
        compiler_params=pltpu.CompilerParams(vmem_limit_bytes=VMEM_BYTES),
    )(fragment, anchor, weight, first, second, grad)


def last_kernel(stamp, weight, first, second, grad, *rest):
    for out, value in zip(
        rest[-3:], adam_update(weight[...], first[...], second[...], grad[...], stamp)
    ):
        out[...] = value


def last_update(stamp, unit, width, weight, first, second, grad, before):
    rows, cols = grad.shape
    tile = min(rows, ADAM_TILE)
    block = pl.BlockSpec((tile, cols), lambda i: (i, 0))
    spot = pl.BlockSpec((tile, cols), lambda i: (i, unit))
    return pl.pallas_call(
        functools.partial(last_kernel, stamp),
        grid=(rows // tile,),
        in_specs=[block] * 4 + [pl.BlockSpec(memory_space=pl.ANY)] * len(before),
        out_specs=[spot] * 3,
        out_shape=[jax.ShapeDtypeStruct((rows, width), jnp.float32)] * 3,
        input_output_aliases={4 + i: i for i in range(len(before))},
        cost_estimate=pl.CostEstimate(
            flops=20 * rows * cols, bytes_accessed=28 * rows * cols, transcendentals=rows * cols
        ),
        compiler_params=pltpu.CompilerParams(vmem_limit_bytes=VMEM_BYTES),
    )(weight, first, second, grad, *before)


def by_rows(array):
    return with_layout_constraint(array, Layout(major_to_minor=(0, 1)))


def outer_update(total, anchor, momentum):
    average = total / lax.axis_size("replica")
    fresh_mom = outer_momentum * momentum + average
    fresh_anchor = anchor - outer_rate * (outer_momentum * fresh_mom + average)
    return (fresh_anchor, fresh_mom)


def ring_of(count):
    half = count // 2
    return [2 * p if p < half else 2 * (count - 1 - p) + 1 for p in range(count)]


def on_device(tokens, cotangent, params, adam_m, adam_v, anchor, momentum, delta, fragment):
    count = lax.axis_size("fsdp")
    half = count // 2
    ringed = count % 2 == 0 and count <= RING_MOST
    ring = ring_of(count)
    onward = [(ring[p], ring[(p + 1) % count]) for p in range(count)]
    back = [(ring[(p + 1) % count], ring[p]) for p in range(count)]
    index = lax.axis_index("fsdp")
    place = jnp.where(index % 2 == 0, index // 2, count - 1 - index // 2)

    cotan = cotangent[0]
    depth, width = params.shape[1:]
    unit_cols = UNIT_HEADS * HEAD_DIM
    units = width // unit_cols
    rows = tokens.shape[1] * count

    owns = [
        by_rows(params[0, :, u * unit_cols : (u + 1) * unit_cols].astype(jnp.bfloat16))
        for u in range(units)
    ]

    normed = norm_rows(tokens[0])
    normed_at = []
    for k in range(count if ringed else 0):
        spot = (place + k) % count
        owner = jnp.where(spot < half, 2 * spot, 2 * (count - 1 - spot) + 1)
        normed_at.append(lax.dynamic_slice_in_dim(normed, owner * depth, depth, 1))

    def gather_whole(current, after=None):
        every = lax.all_gather(current, "fsdp", axis=0, tiled=True)
        return jnp.dot(normed, every, preferred_element_type=jnp.float32), every

    def scatter_whole(key_grad):
        part = lax.dot_general(
            normed, key_grad, (((0,), (0,)), ((), ())), preferred_element_type=jnp.float32
        )
        return lax.psum_scatter(part, "fsdp", scatter_dimension=0, tiled=True)

    def add_rows(k, piece):
        return jnp.dot(normed_at[k], piece, preferred_element_type=jnp.float32)

    def gather_keys(current, after=None):
        own = current
        if after is not None:
            own, _ = lax.optimization_barrier((own, after))
        keys = add_rows(0, own)
        left, right = own, own
        first_hop = None
        for k in range(1, half):
            left = lax.ppermute(left, "fsdp", onward)
            right = lax.ppermute(right, "fsdp", back)
            first_hop = first_hop or (left, right)
            keys = keys + add_rows(count - k, left) + add_rows(k, right)
        top = lax.ppermute(left[: depth // 2], "fsdp", onward)
        low = lax.ppermute(right[depth // 2 :], "fsdp", back)
        return keys + add_rows(half, jnp.concatenate([top, low], 0)), first_hop

    def grad_part(k, key_grad):
        return lax.dot_general(
            normed_at[k], key_grad, (((0,), (0,)), ((), ())), preferred_element_type=jnp.float32
        )

    def scatter_grad(key_grad):
        far = by_rows((SCALE * grad_part(half, key_grad)).astype(SENT))
        right = lax.ppermute(far[: depth // 2], "fsdp", onward)
        left = lax.ppermute(far[depth // 2 :], "fsdp", back)
        zeros = jnp.zeros_like(right)
        right = jnp.concatenate([right, zeros], 0)
        left = jnp.concatenate([zeros, left], 0)
        for k in range(half - 1, 0, -1):
            right = SCALE * grad_part(k, key_grad) + right.astype(jnp.float32)
            left = SCALE * grad_part(count - k, key_grad) + left.astype(jnp.float32)
            right, left = by_rows(right.astype(SENT)), by_rows(left.astype(SENT))
            right = lax.ppermute(right, "fsdp", onward)
            left = lax.ppermute(left, "fsdp", back)
        return grad_part(0, key_grad) + (right.astype(jnp.float32) + left.astype(jnp.float32)) / SCALE

    gather, scatter = (gather_keys, scatter_grad) if ringed else (gather_whole, scatter_whole)
    total = lax.psum(delta[0], "replica")
    states, key_grads = [None] * units, [None] * units
    first_hop = None
    for u in range(units):
        keys, first_hop = gather(owns[u], first_hop)
        if u == units - 1:
            keys, total = lax.optimization_barrier((keys, total))
            new_anchor, new_momentum = outer_update(total, anchor, momentum)
        key_grads[u] = key_gradient(keys, cotan, u, rows)
    for u in range(units):
        *states[u], owns[u] = first_update(
            1, u, fragment, new_anchor, params[0], adam_m[0], adam_v[0], scatter(key_grads[u])
        )
    results = ()
    for u in range(units):
        grad = scatter(key_gradient(gather(owns[u])[0], cotan, u, rows))
        results = last_update(2, u, width, *states[u], grad, results)

    return (*(out[None] for out in results), new_anchor, new_momentum)


def solution(mesh):
    return jax.shard_map(
        on_device,
        mesh=mesh,
        in_specs=(
            P("replica", "fsdp", None),
            P("replica", "fsdp", None),
            P("replica", "fsdp", None),
            P("replica", "fsdp", None),
            P("replica", "fsdp", None),
            P("fsdp", None),
            P("fsdp", None),
            P("replica", "fsdp", None),
            P(),
        ),
        out_specs=(
            P("replica", "fsdp", None),
            P("replica", "fsdp", None),
            P("replica", "fsdp", None),
            P("fsdp", None),
            P("fsdp", None),
        ),
        check_vma=False,
    )
```

```python
import functools

import jax
import jax.numpy as jnp
from jax import lax
from jax.experimental import pallas as pl
from jax.experimental.layout import Layout, with_layout_constraint
from jax.experimental.pallas import tpu as pltpu
from jax.sharding import PartitionSpec as P

HEAD_DIM = 128
KV_HEADS = 4
INNER_STEPS = 2
UNIT_HEADS = 2
RING_MOST = 8
NORM_TILE = 64
KEY_TILE = 256
ADAM_TILE = 256
VMEM_BYTES = 10 * 2**20
SENT = jnp.float16
SCALE = 1.0 / 128


beta_one = 0.9
beta_two = 0.95
adam_eps = 1e-08
learn_rate = 0.002
weight_decay = 0.1
outer_rate = 0.7
outer_momentum = 0.9
mixing = 0.5


def norm_kernel(values, out):
    floats = values[...].astype(jnp.float32)
    scale = lax.rsqrt(jnp.mean(floats * floats, axis=-1, keepdims=True) + 1e-05)
    out[...] = (floats * scale).astype(jnp.bfloat16)


def norm_rows(values):
    rows, width = values.shape
    tile = NORM_TILE if rows % NORM_TILE == 0 else rows
    block = pl.BlockSpec((tile, width), lambda i: (i, 0))
    return pl.pallas_call(
        norm_kernel,
        grid=(rows // tile,),
        in_specs=[block],
        out_specs=block,
        out_shape=jax.ShapeDtypeStruct(values.shape, jnp.bfloat16),
        cost_estimate=pl.CostEstimate(
            flops=8 * rows * width, bytes_accessed=4 * rows * width, transcendentals=rows
        ),
        compiler_params=pltpu.CompilerParams(vmem_limit_bytes=VMEM_BYTES),
    )(values)


def key_kernel(rows, keys, cotan, out):
    for h in range(keys.shape[1] // HEAD_DIM):
        spot = pl.ds(h * HEAD_DIM, HEAD_DIM)
        head = keys[:, spot]
        inverse = lax.rsqrt(jnp.mean(head * head, axis=-1, keepdims=True) + 1e-06)
        unit = head * inverse
        upstream = cotan[:, spot].astype(jnp.float32) / rows
        grads = inverse * (upstream - unit * jnp.mean(upstream * unit, axis=-1, keepdims=True))
        out[:, spot] = grads.astype(jnp.bfloat16)


def key_gradient(keys, cotan, unit, rows):
    count, cols = keys.shape
    tile = KEY_TILE if count % KEY_TILE == 0 else count
    block = pl.BlockSpec((tile, cols), lambda i: (i, 0))
    return pl.pallas_call(
        functools.partial(key_kernel, rows),
        grid=(count // tile,),
        in_specs=[block, pl.BlockSpec((tile, cols), lambda i: (i, unit))],
        out_specs=block,
        out_shape=jax.ShapeDtypeStruct(keys.shape, jnp.bfloat16),
        cost_estimate=pl.CostEstimate(
            flops=12 * count * cols, bytes_accessed=8 * count * cols, transcendentals=count
        ),
        compiler_params=pltpu.CompilerParams(vmem_limit_bytes=VMEM_BYTES),
    )(keys, cotan)


def adam_update(weight, first, second, grad, stamp):
    first = beta_one * first + (1.0 - beta_one) * grad
    second = beta_two * second + (1.0 - beta_two) * grad * grad
    fix_one = 1.0 - beta_one**stamp
    fix_two = 1.0 - beta_two**stamp
    ratio = first / fix_one / (jnp.sqrt(second / fix_two) + adam_eps)
    weight = weight - learn_rate * (ratio + weight_decay * weight)
    return (weight, first, second)


def first_kernel(stamp, unit, fragment, anchor, weight, first, second, grad, out_w, out_m, out_v, own):
    fresh, out_m[...], out_v[...] = adam_update(
        weight[...], first[...], second[...], grad[...], stamp
    )
    heads = fresh.shape[1] // HEAD_DIM
    for h in range(heads):
        head = fresh[:, h * HEAD_DIM : (h + 1) * HEAD_DIM]
        merged = mixing * head + (1.0 - mixing) * anchor[...]
        head = jnp.where(fragment[0] == unit * heads + h, merged, head)
        out_w[:, pl.ds(h * HEAD_DIM, HEAD_DIM)] = head
        own[:, pl.ds(h * HEAD_DIM, HEAD_DIM)] = head.astype(jnp.bfloat16)


def first_update(stamp, unit, fragment, anchor, weight, first, second, grad):
    rows, cols = grad.shape
    tile = min(rows, ADAM_TILE)
    block = pl.BlockSpec((tile, cols), lambda i: (i, 0))
    spot = pl.BlockSpec((tile, cols), lambda i: (i, unit))
    side = pl.BlockSpec((tile, HEAD_DIM), lambda i: (i, 0))
    return pl.pallas_call(
        functools.partial(first_kernel, stamp, unit),
        grid=(rows // tile,),
        in_specs=[pl.BlockSpec(memory_space=pltpu.SMEM), side, spot, spot, spot, block],
        out_specs=[block] * 4,
        out_shape=[jax.ShapeDtypeStruct((rows, cols), jnp.float32)] * 3
        + [jax.ShapeDtypeStruct((rows, cols), jnp.bfloat16)],
        cost_estimate=pl.CostEstimate(
            flops=24 * rows * cols, bytes_accessed=32 * rows * cols, transcendentals=rows * cols
        ),
        compiler_params=pltpu.CompilerParams(vmem_limit_bytes=VMEM_BYTES),
    )(fragment, anchor, weight, first, second, grad)


def last_kernel(stamp, weight, first, second, grad, *rest):
    for out, value in zip(
        rest[-3:], adam_update(weight[...], first[...], second[...], grad[...], stamp)
    ):
        out[...] = value


def last_update(stamp, unit, width, weight, first, second, grad, before):
    rows, cols = grad.shape
    tile = min(rows, ADAM_TILE)
    block = pl.BlockSpec((tile, cols), lambda i: (i, 0))
    spot = pl.BlockSpec((tile, cols), lambda i: (i, unit))
    return pl.pallas_call(
        functools.partial(last_kernel, stamp),
        grid=(rows // tile,),
        in_specs=[block] * 4 + [pl.BlockSpec(memory_space=pl.ANY)] * len(before),
        out_specs=[spot] * 3,
        out_shape=[jax.ShapeDtypeStruct((rows, width), jnp.float32)] * 3,
        input_output_aliases={4 + i: i for i in range(len(before))},
        cost_estimate=pl.CostEstimate(
            flops=20 * rows * cols, bytes_accessed=28 * rows * cols, transcendentals=rows * cols
        ),
        compiler_params=pltpu.CompilerParams(vmem_limit_bytes=VMEM_BYTES),
    )(weight, first, second, grad, *before)


def by_rows(array):
    return with_layout_constraint(array, Layout(major_to_minor=(0, 1)))


def outer_update(total, anchor, momentum):
    average = total / lax.axis_size("replica")
    fresh_mom = outer_momentum * momentum + average
    fresh_anchor = anchor - outer_rate * (outer_momentum * fresh_mom + average)
    return (fresh_anchor, fresh_mom)


def ring_of(count):
    half = count // 2
    return [2 * p if p < half else 2 * (count - 1 - p) + 1 for p in range(count)]


def on_device(tokens, cotangent, params, adam_m, adam_v, anchor, momentum, delta, fragment):
    count = lax.axis_size("fsdp")
    half = count // 2
    ringed = count % 2 == 0 and count <= RING_MOST
    ring = ring_of(count)
    onward = [(ring[p], ring[(p + 1) % count]) for p in range(count)]
    back = [(ring[(p + 1) % count], ring[p]) for p in range(count)]
    index = lax.axis_index("fsdp")
    place = jnp.where(index % 2 == 0, index // 2, count - 1 - index // 2)

    cotan = cotangent[0]
    depth, width = params.shape[1:]
    unit_cols = UNIT_HEADS * HEAD_DIM
    units = width // unit_cols
    rows = tokens.shape[1] * count

    owns = [
        by_rows(params[0, :, u * unit_cols : (u + 1) * unit_cols].astype(jnp.bfloat16))
        for u in range(units)
    ]

    normed = norm_rows(tokens[0])
    normed_at = []
    for k in range(count if ringed else 0):
        spot = (place + k) % count
        owner = jnp.where(spot < half, 2 * spot, 2 * (count - 1 - spot) + 1)
        normed_at.append(lax.dynamic_slice_in_dim(normed, owner * depth, depth, 1))

    def gather_whole(current, after=None, beside=None):
        every = lax.all_gather(current, "fsdp", axis=0, tiled=True)
        return jnp.dot(normed, every, preferred_element_type=jnp.float32), every, beside

    def scatter_whole(key_grad):
        part = lax.dot_general(
            normed, key_grad, (((0,), (0,)), ((), ())), preferred_element_type=jnp.float32
        )
        return lax.psum_scatter(part, "fsdp", scatter_dimension=0, tiled=True)

    def add_rows(k, piece):
        return jnp.dot(normed_at[k], piece, preferred_element_type=jnp.float32)

    def gather_keys(current, after=None, beside=None):
        own = current
        if after is not None:
            own, _ = lax.optimization_barrier((own, after))
        keys = add_rows(0, own)
        left, right = own, own
        first_hop = None
        for k in range(1, half):
            left = lax.ppermute(left, "fsdp", onward)
            right = lax.ppermute(right, "fsdp", back)
            first_hop = first_hop or (left, right)
            keys = keys + add_rows(count - k, left) + add_rows(k, right)
            if k == 2 and beside is not None:
                keys, beside = lax.optimization_barrier((keys, beside))
        top = lax.ppermute(left[: depth // 2], "fsdp", onward)
        low = lax.ppermute(right[depth // 2 :], "fsdp", back)
        return keys + add_rows(half, jnp.concatenate([top, low], 0)), first_hop, beside

    def grad_part(k, key_grad):
        return lax.dot_general(
            normed_at[k], key_grad, (((0,), (0,)), ((), ())), preferred_element_type=jnp.float32
        )

    def scatter_grad(key_grad):
        far = by_rows((SCALE * grad_part(half, key_grad)).astype(SENT))
        right = lax.ppermute(far[: depth // 2], "fsdp", onward)
        left = lax.ppermute(far[depth // 2 :], "fsdp", back)
        zeros = jnp.zeros_like(right)
        right = jnp.concatenate([right, zeros], 0)
        left = jnp.concatenate([zeros, left], 0)
        for k in range(half - 1, 0, -1):
            right = SCALE * grad_part(k, key_grad) + right.astype(jnp.float32)
            left = SCALE * grad_part(count - k, key_grad) + left.astype(jnp.float32)
            right, left = by_rows(right.astype(SENT)), by_rows(left.astype(SENT))
            right = lax.ppermute(right, "fsdp", onward)
            left = lax.ppermute(left, "fsdp", back)
        return grad_part(0, key_grad) + (right.astype(jnp.float32) + left.astype(jnp.float32)) / SCALE

    gather, scatter = (gather_keys, scatter_grad) if ringed else (gather_whole, scatter_whole)
    total = lax.psum(delta[0], "replica")
    states, key_grads = [None] * units, [None] * units
    first_hop = None
    for u in range(units):
        keys, first_hop, total = gather(owns[u], first_hop, total if u == 0 else None)
        if u == 0:
            new_anchor, new_momentum = outer_update(total, anchor, momentum)
        key_grads[u] = key_gradient(keys, cotan, u, rows)
    for u in range(units):
        *states[u], owns[u] = first_update(
            1, u, fragment, new_anchor, params[0], adam_m[0], adam_v[0], scatter(key_grads[u])
        )
    results = ()
    for u in range(units):
        grad = scatter(key_gradient(gather(owns[u])[0], cotan, u, rows))
        results = last_update(2, u, width, *states[u], grad, results)

    return (*(out[None] for out in results), new_anchor, new_momentum)


def solution(mesh):
    return jax.shard_map(
        on_device,
        mesh=mesh,
        in_specs=(
            P("replica", "fsdp", None),
            P("replica", "fsdp", None),
            P("replica", "fsdp", None),
            P("replica", "fsdp", None),
            P("replica", "fsdp", None),
            P("fsdp", None),
            P("fsdp", None),
            P("replica", "fsdp", None),
            P(),
        ),
        out_specs=(
            P("replica", "fsdp", None),
            P("replica", "fsdp", None),
            P("replica", "fsdp", None),
            P("fsdp", None),
            P("fsdp", None),
        ),
        check_vma=False,
    )
```

```python
import functools

import jax
import jax.numpy as jnp
from jax import lax
from jax.experimental import pallas as pl
from jax.experimental.layout import Layout, with_layout_constraint
from jax.experimental.pallas import tpu as pltpu
from jax.sharding import PartitionSpec as P

HEAD_DIM = 128
KV_HEADS = 4
INNER_STEPS = 2
UNIT_HEADS = 2
RING_MOST = 8
NORM_TILE = 64
KEY_TILE = 256
ADAM_TILE = 256
VMEM_BYTES = 10 * 2**20
SENT = jnp.float16
SCALE = 1.0 / 128


beta_one = 0.9
beta_two = 0.95
adam_eps = 1e-08
learn_rate = 0.002
weight_decay = 0.1
outer_rate = 0.7
outer_momentum = 0.9
mixing = 0.5


def norm_kernel(values, out):
    floats = values[...].astype(jnp.float32)
    scale = lax.rsqrt(jnp.mean(floats * floats, axis=-1, keepdims=True) + 1e-05)
    out[...] = (floats * scale).astype(jnp.bfloat16)


def norm_rows(values):
    rows, width = values.shape
    tile = NORM_TILE if rows % NORM_TILE == 0 else rows
    block = pl.BlockSpec((tile, width), lambda i: (i, 0))
    return pl.pallas_call(
        norm_kernel,
        grid=(rows // tile,),
        in_specs=[block],
        out_specs=block,
        out_shape=jax.ShapeDtypeStruct(values.shape, jnp.bfloat16),
        cost_estimate=pl.CostEstimate(
            flops=8 * rows * width, bytes_accessed=4 * rows * width, transcendentals=rows
        ),
        compiler_params=pltpu.CompilerParams(vmem_limit_bytes=VMEM_BYTES),
    )(values)


def key_kernel(rows, keys, cotan, out):
    for h in range(keys.shape[1] // HEAD_DIM):
        spot = pl.ds(h * HEAD_DIM, HEAD_DIM)
        head = keys[:, spot]
        inverse = lax.rsqrt(jnp.mean(head * head, axis=-1, keepdims=True) + 1e-06)
        unit = head * inverse
        upstream = cotan[:, spot].astype(jnp.float32) / rows
        grads = inverse * (upstream - unit * jnp.mean(upstream * unit, axis=-1, keepdims=True))
        out[:, spot] = grads.astype(jnp.bfloat16)


def key_gradient(keys, cotan, unit, rows):
    count, cols = keys.shape
    tile = KEY_TILE if count % KEY_TILE == 0 else count
    block = pl.BlockSpec((tile, cols), lambda i: (i, 0))
    return pl.pallas_call(
        functools.partial(key_kernel, rows),
        grid=(count // tile,),
        in_specs=[block, pl.BlockSpec((tile, cols), lambda i: (i, unit))],
        out_specs=block,
        out_shape=jax.ShapeDtypeStruct(keys.shape, jnp.bfloat16),
        cost_estimate=pl.CostEstimate(
            flops=12 * count * cols, bytes_accessed=8 * count * cols, transcendentals=count
        ),
        compiler_params=pltpu.CompilerParams(vmem_limit_bytes=VMEM_BYTES),
    )(keys, cotan)


def adam_update(weight, first, second, grad, stamp):
    first = beta_one * first + (1.0 - beta_one) * grad
    second = beta_two * second + (1.0 - beta_two) * grad * grad
    fix_one = 1.0 - beta_one**stamp
    fix_two = 1.0 - beta_two**stamp
    ratio = first / fix_one / (jnp.sqrt(second / fix_two) + adam_eps)
    weight = weight - learn_rate * (ratio + weight_decay * weight)
    return (weight, first, second)


def first_kernel(stamp, unit, fragment, anchor, weight, first, second, grad, out_w, out_m, out_v, own):
    fresh, out_m[...], out_v[...] = adam_update(
        weight[...], first[...], second[...], grad[...], stamp
    )
    heads = fresh.shape[1] // HEAD_DIM
    for h in range(heads):
        head = fresh[:, h * HEAD_DIM : (h + 1) * HEAD_DIM]
        merged = mixing * head + (1.0 - mixing) * anchor[...]
        head = jnp.where(fragment[0] == unit * heads + h, merged, head)
        out_w[:, pl.ds(h * HEAD_DIM, HEAD_DIM)] = head
        own[:, pl.ds(h * HEAD_DIM, HEAD_DIM)] = head.astype(jnp.bfloat16)


def first_update(stamp, unit, fragment, anchor, weight, first, second, grad):
    rows, cols = grad.shape
    tile = min(rows, ADAM_TILE)
    block = pl.BlockSpec((tile, cols), lambda i: (i, 0))
    spot = pl.BlockSpec((tile, cols), lambda i: (i, unit))
    side = pl.BlockSpec((tile, HEAD_DIM), lambda i: (i, 0))
    return pl.pallas_call(
        functools.partial(first_kernel, stamp, unit),
        grid=(rows // tile,),
        in_specs=[pl.BlockSpec(memory_space=pltpu.SMEM), side, spot, spot, spot, block],
        out_specs=[block] * 4,
        out_shape=[jax.ShapeDtypeStruct((rows, cols), jnp.float32)] * 3
        + [jax.ShapeDtypeStruct((rows, cols), jnp.bfloat16)],
        cost_estimate=pl.CostEstimate(
            flops=24 * rows * cols, bytes_accessed=32 * rows * cols, transcendentals=rows * cols
        ),
        compiler_params=pltpu.CompilerParams(vmem_limit_bytes=VMEM_BYTES),
    )(fragment, anchor, weight, first, second, grad)


def last_kernel(stamp, weight, first, second, grad, *rest):
    for out, value in zip(
        rest[-3:], adam_update(weight[...], first[...], second[...], grad[...], stamp)
    ):
        out[...] = value


def last_update(stamp, unit, width, weight, first, second, grad, before):
    rows, cols = grad.shape
    tile = min(rows, ADAM_TILE)
    block = pl.BlockSpec((tile, cols), lambda i: (i, 0))
    spot = pl.BlockSpec((tile, cols), lambda i: (i, unit))
    return pl.pallas_call(
        functools.partial(last_kernel, stamp),
        grid=(rows // tile,),
        in_specs=[block] * 4 + [pl.BlockSpec(memory_space=pl.ANY)] * len(before),
        out_specs=[spot] * 3,
        out_shape=[jax.ShapeDtypeStruct((rows, width), jnp.float32)] * 3,
        input_output_aliases={4 + i: i for i in range(len(before))},
        cost_estimate=pl.CostEstimate(
            flops=20 * rows * cols, bytes_accessed=28 * rows * cols, transcendentals=rows * cols
        ),
        compiler_params=pltpu.CompilerParams(vmem_limit_bytes=VMEM_BYTES),
    )(weight, first, second, grad, *before)


def by_rows(array):
    return with_layout_constraint(array, Layout(major_to_minor=(0, 1)))


def outer_update(total, anchor, momentum):
    average = total / lax.axis_size("replica")
    fresh_mom = outer_momentum * momentum + average
    fresh_anchor = anchor - outer_rate * (outer_momentum * fresh_mom + average)
    return (fresh_anchor, fresh_mom)


def ring_of(count):
    half = count // 2
    return [2 * p if p < half else 2 * (count - 1 - p) + 1 for p in range(count)]


def on_device(tokens, cotangent, params, adam_m, adam_v, anchor, momentum, delta, fragment):
    count = lax.axis_size("fsdp")
    half = count // 2
    ringed = count % 2 == 0 and count <= RING_MOST
    ring = ring_of(count)
    onward = [(ring[p], ring[(p + 1) % count]) for p in range(count)]
    back = [(ring[(p + 1) % count], ring[p]) for p in range(count)]
    index = lax.axis_index("fsdp")
    place = jnp.where(index % 2 == 0, index // 2, count - 1 - index // 2)

    cotan = cotangent[0]
    depth, width = params.shape[1:]
    unit_cols = UNIT_HEADS * HEAD_DIM
    units = width // unit_cols
    rows = tokens.shape[1] * count

    owns = [
        by_rows(params[0, :, u * unit_cols : (u + 1) * unit_cols].astype(jnp.bfloat16))
        for u in range(units)
    ]

    normed = norm_rows(tokens[0])
    normed_at = []
    for k in range(count if ringed else 0):
        spot = (place + k) % count
        owner = jnp.where(spot < half, 2 * spot, 2 * (count - 1 - spot) + 1)
        normed_at.append(lax.dynamic_slice_in_dim(normed, owner * depth, depth, 1))

    def gather_whole(current, beside=None):
        every = lax.all_gather(current, "fsdp", axis=0, tiled=True)
        return jnp.dot(normed, every, preferred_element_type=jnp.float32), beside

    def scatter_whole(key_grad):
        part = lax.dot_general(
            normed, key_grad, (((0,), (0,)), ((), ())), preferred_element_type=jnp.float32
        )
        return lax.psum_scatter(part, "fsdp", scatter_dimension=0, tiled=True)

    def add_rows(k, piece):
        return jnp.dot(normed_at[k], piece, preferred_element_type=jnp.float32)

    def gather_keys(own, beside=None):
        keys = add_rows(0, own)
        left, right = own, own
        for k in range(1, half):
            left = lax.ppermute(left, "fsdp", onward)
            right = lax.ppermute(right, "fsdp", back)
            keys = keys + add_rows(count - k, left) + add_rows(k, right)
            if k == 2 and beside is not None:
                keys, beside = lax.optimization_barrier((keys, beside))
        top = lax.ppermute(left[: depth // 2], "fsdp", onward)
        low = lax.ppermute(right[depth // 2 :], "fsdp", back)
        return keys + add_rows(half, jnp.concatenate([top, low], 0)), beside

    def grad_part(k, key_grad):
        return lax.dot_general(
            normed_at[k], key_grad, (((0,), (0,)), ((), ())), preferred_element_type=jnp.float32
        )

    def scatter_grad(key_grad):
        far = by_rows((SCALE * grad_part(half, key_grad)).astype(SENT))
        right = lax.ppermute(far[: depth // 2], "fsdp", onward)
        left = lax.ppermute(far[depth // 2 :], "fsdp", back)
        key_grad, right, left = lax.optimization_barrier((key_grad, right, left))
        zeros = jnp.zeros_like(right)
        right = jnp.concatenate([right, zeros], 0)
        left = jnp.concatenate([zeros, left], 0)
        for k in range(half - 1, 0, -1):
            right = SCALE * grad_part(k, key_grad) + right.astype(jnp.float32)
            left = SCALE * grad_part(count - k, key_grad) + left.astype(jnp.float32)
            right, left = by_rows(right.astype(SENT)), by_rows(left.astype(SENT))
            right = lax.ppermute(right, "fsdp", onward)
            left = lax.ppermute(left, "fsdp", back)
        return grad_part(0, key_grad) + (right.astype(jnp.float32) + left.astype(jnp.float32)) / SCALE

    gather, scatter = (gather_keys, scatter_grad) if ringed else (gather_whole, scatter_whole)
    total = lax.psum(delta[0], "replica")
    states, key_grads = [None] * units, [None] * units
    for u in range(units):
        keys, done = gather(owns[u], total if u == 0 else None)
        if u == 0:
            total = done
            new_anchor, new_momentum = outer_update(total, anchor, momentum)
        key_grads[u] = key_gradient(keys, cotan, u, rows)
    for u in range(units):
        *states[u], owns[u] = first_update(
            1, u, fragment, new_anchor, params[0], adam_m[0], adam_v[0], scatter(key_grads[u])
        )
    results = ()
    for u in range(units):
        grad = scatter(key_gradient(gather(owns[u])[0], cotan, u, rows))
        results = last_update(2, u, width, *states[u], grad, results)

    return (*(out[None] for out in results), new_anchor, new_momentum)


def solution(mesh):
    return jax.shard_map(
        on_device,
        mesh=mesh,
        in_specs=(
            P("replica", "fsdp", None),
            P("replica", "fsdp", None),
            P("replica", "fsdp", None),
            P("replica", "fsdp", None),
            P("replica", "fsdp", None),
            P("fsdp", None),
            P("fsdp", None),
            P("replica", "fsdp", None),
            P(),
        ),
        out_specs=(
            P("replica", "fsdp", None),
            P("replica", "fsdp", None),
            P("replica", "fsdp", None),
            P("fsdp", None),
            P("fsdp", None),
        ),
        check_vma=False,
    )
```

```python
import functools

import jax
import jax.numpy as jnp
from jax import lax
from jax.experimental import pallas as pl
from jax.experimental.layout import Layout, with_layout_constraint
from jax.experimental.pallas import tpu as pltpu
from jax.sharding import PartitionSpec as P

HEAD_DIM = 128
KV_HEADS = 4
INNER_STEPS = 2
UNIT_HEADS = 2
RING_MOST = 8
NORM_TILE = 64
KEY_TILE = 256
ADAM_TILE = 256
VMEM_BYTES = 10 * 2**20
SENT = jnp.float16
SCALE = 1.0 / 128


beta_one = 0.9
beta_two = 0.95
adam_eps = 1e-08
learn_rate = 0.002
weight_decay = 0.1
outer_rate = 0.7
outer_momentum = 0.9
mixing = 0.5


def norm_kernel(values, out):
    floats = values[...].astype(jnp.float32)
    scale = lax.rsqrt(jnp.mean(floats * floats, axis=-1, keepdims=True) + 1e-05)
    out[...] = (floats * scale).astype(jnp.bfloat16)


def norm_rows(values):
    rows, width = values.shape
    tile = NORM_TILE if rows % NORM_TILE == 0 else rows
    block = pl.BlockSpec((tile, width), lambda i: (i, 0))
    return pl.pallas_call(
        norm_kernel,
        grid=(rows // tile,),
        in_specs=[block],
        out_specs=block,
        out_shape=jax.ShapeDtypeStruct(values.shape, jnp.bfloat16),
        cost_estimate=pl.CostEstimate(
            flops=8 * rows * width, bytes_accessed=4 * rows * width, transcendentals=rows
        ),
        compiler_params=pltpu.CompilerParams(vmem_limit_bytes=VMEM_BYTES),
    )(values)


def key_kernel(rows, keys, cotan, out):
    for h in range(keys.shape[1] // HEAD_DIM):
        spot = pl.ds(h * HEAD_DIM, HEAD_DIM)
        head = keys[:, spot]
        inverse = lax.rsqrt(jnp.mean(head * head, axis=-1, keepdims=True) + 1e-06)
        unit = head * inverse
        upstream = cotan[:, spot].astype(jnp.float32) / rows
        grads = inverse * (upstream - unit * jnp.mean(upstream * unit, axis=-1, keepdims=True))
        out[:, spot] = grads.astype(jnp.bfloat16)


def key_gradient(keys, cotan, unit, rows):
    count, cols = keys.shape
    tile = KEY_TILE if count % KEY_TILE == 0 else count
    block = pl.BlockSpec((tile, cols), lambda i: (i, 0))
    return pl.pallas_call(
        functools.partial(key_kernel, rows),
        grid=(count // tile,),
        in_specs=[block, pl.BlockSpec((tile, cols), lambda i: (i, unit))],
        out_specs=block,
        out_shape=jax.ShapeDtypeStruct(keys.shape, jnp.bfloat16),
        cost_estimate=pl.CostEstimate(
            flops=12 * count * cols, bytes_accessed=8 * count * cols, transcendentals=count
        ),
        compiler_params=pltpu.CompilerParams(vmem_limit_bytes=VMEM_BYTES),
    )(keys, cotan)


def adam_update(weight, first, second, grad, stamp):
    first = beta_one * first + (1.0 - beta_one) * grad
    second = beta_two * second + (1.0 - beta_two) * grad * grad
    fix_one = 1.0 - beta_one**stamp
    fix_two = 1.0 - beta_two**stamp
    ratio = first / fix_one / (jnp.sqrt(second / fix_two) + adam_eps)
    weight = weight - learn_rate * (ratio + weight_decay * weight)
    return (weight, first, second)


def first_kernel(stamp, unit, fragment, anchor, weight, first, second, grad, out_w, out_m, out_v, own):
    fresh, out_m[...], out_v[...] = adam_update(
        weight[...], first[...], second[...], grad[...], stamp
    )
    heads = fresh.shape[1] // HEAD_DIM
    for h in range(heads):
        head = fresh[:, h * HEAD_DIM : (h + 1) * HEAD_DIM]
        merged = mixing * head + (1.0 - mixing) * anchor[...]
        head = jnp.where(fragment[0] == unit * heads + h, merged, head)
        out_w[:, pl.ds(h * HEAD_DIM, HEAD_DIM)] = head
        own[:, pl.ds(h * HEAD_DIM, HEAD_DIM)] = head.astype(jnp.bfloat16)


def first_update(stamp, unit, fragment, anchor, weight, first, second, grad):
    rows, cols = grad.shape
    tile = min(rows, ADAM_TILE)
    block = pl.BlockSpec((tile, cols), lambda i: (i, 0))
    spot = pl.BlockSpec((tile, cols), lambda i: (i, unit))
    side = pl.BlockSpec((tile, HEAD_DIM), lambda i: (i, 0))
    return pl.pallas_call(
        functools.partial(first_kernel, stamp, unit),
        grid=(rows // tile,),
        in_specs=[pl.BlockSpec(memory_space=pltpu.SMEM), side, spot, spot, spot, block],
        out_specs=[block] * 4,
        out_shape=[jax.ShapeDtypeStruct((rows, cols), jnp.float32)] * 3
        + [jax.ShapeDtypeStruct((rows, cols), jnp.bfloat16)],
        cost_estimate=pl.CostEstimate(
            flops=24 * rows * cols, bytes_accessed=32 * rows * cols, transcendentals=rows * cols
        ),
        compiler_params=pltpu.CompilerParams(vmem_limit_bytes=VMEM_BYTES),
    )(fragment, anchor, weight, first, second, grad)


def last_kernel(stamp, weight, first, second, grad, *rest):
    for out, value in zip(
        rest[-3:], adam_update(weight[...], first[...], second[...], grad[...], stamp)
    ):
        out[...] = value


def last_update(stamp, unit, width, weight, first, second, grad, before):
    rows, cols = grad.shape
    tile = min(rows, ADAM_TILE)
    block = pl.BlockSpec((tile, cols), lambda i: (i, 0))
    spot = pl.BlockSpec((tile, cols), lambda i: (i, unit))
    return pl.pallas_call(
        functools.partial(last_kernel, stamp),
        grid=(rows // tile,),
        in_specs=[block] * 4 + [pl.BlockSpec(memory_space=pl.ANY)] * len(before),
        out_specs=[spot] * 3,
        out_shape=[jax.ShapeDtypeStruct((rows, width), jnp.float32)] * 3,
        input_output_aliases={4 + i: i for i in range(len(before))},
        cost_estimate=pl.CostEstimate(
            flops=20 * rows * cols, bytes_accessed=28 * rows * cols, transcendentals=rows * cols
        ),
        compiler_params=pltpu.CompilerParams(vmem_limit_bytes=VMEM_BYTES),
    )(weight, first, second, grad, *before)


def by_rows(array):
    return with_layout_constraint(array, Layout(major_to_minor=(0, 1)))


def sum_replicas(rows):
    count = lax.axis_size("replica")
    if count & (count - 1):
        return lax.psum(rows, "replica")
    step = 1
    while step < count:
        swaps = [(r, r ^ step) for r in range(count)]
        rows = rows + lax.ppermute(rows, "replica", swaps)
        step *= 2
    return rows


def outer_update(total, anchor, momentum):
    average = total / lax.axis_size("replica")
    fresh_mom = outer_momentum * momentum + average
    fresh_anchor = anchor - outer_rate * (outer_momentum * fresh_mom + average)
    return (fresh_anchor, fresh_mom)


def ring_of(count):
    half = count // 2
    return [2 * p if p < half else 2 * (count - 1 - p) + 1 for p in range(count)]


def on_device(tokens, cotangent, params, adam_m, adam_v, anchor, momentum, delta, fragment):
    count = lax.axis_size("fsdp")
    half = count // 2
    ringed = count % 2 == 0 and count <= RING_MOST
    ring = ring_of(count)
    onward = [(ring[p], ring[(p + 1) % count]) for p in range(count)]
    back = [(ring[(p + 1) % count], ring[p]) for p in range(count)]
    index = lax.axis_index("fsdp")
    place = jnp.where(index % 2 == 0, index // 2, count - 1 - index // 2)

    cotan = cotangent[0]
    depth, width = params.shape[1:]
    unit_cols = UNIT_HEADS * HEAD_DIM
    units = width // unit_cols
    rows = tokens.shape[1] * count

    owns = [
        by_rows(params[0, :, u * unit_cols : (u + 1) * unit_cols].astype(jnp.bfloat16))
        for u in range(units)
    ]

    normed = norm_rows(tokens[0])
    normed_at = []
    for k in range(count if ringed else 0):
        spot = (place + k) % count
        owner = jnp.where(spot < half, 2 * spot, 2 * (count - 1 - spot) + 1)
        normed_at.append(lax.dynamic_slice_in_dim(normed, owner * depth, depth, 1))

    def gather_whole(current, beside=None):
        every = lax.all_gather(current, "fsdp", axis=0, tiled=True)
        return jnp.dot(normed, every, preferred_element_type=jnp.float32), beside

    def scatter_whole(key_grad):
        part = lax.dot_general(
            normed, key_grad, (((0,), (0,)), ((), ())), preferred_element_type=jnp.float32
        )
        return lax.psum_scatter(part, "fsdp", scatter_dimension=0, tiled=True)

    def add_rows(k, piece):
        return jnp.dot(normed_at[k], piece, preferred_element_type=jnp.float32)

    def gather_keys(own, beside=None):
        keys = add_rows(0, own)
        left, right = own, own
        for k in range(1, half):
            left = lax.ppermute(left, "fsdp", onward)
            right = lax.ppermute(right, "fsdp", back)
            keys = keys + add_rows(count - k, left) + add_rows(k, right)
            if k == 3 and beside is not None:
                keys, beside = lax.optimization_barrier((keys, beside))
        top = lax.ppermute(left[: depth // 2], "fsdp", onward)
        low = lax.ppermute(right[depth // 2 :], "fsdp", back)
        return keys + add_rows(half, jnp.concatenate([top, low], 0)), beside

    def grad_part(k, key_grad):
        return lax.dot_general(
            normed_at[k], key_grad, (((0,), (0,)), ((), ())), preferred_element_type=jnp.float32
        )

    def scatter_grad(key_grad):
        far = by_rows((SCALE * grad_part(half, key_grad)).astype(SENT))
        right = lax.ppermute(far[: depth // 2], "fsdp", onward)
        left = lax.ppermute(far[depth // 2 :], "fsdp", back)
        key_grad, right, left = lax.optimization_barrier((key_grad, right, left))
        zeros = jnp.zeros_like(right)
        right = jnp.concatenate([right, zeros], 0)
        left = jnp.concatenate([zeros, left], 0)
        for k in range(half - 1, 0, -1):
            right = SCALE * grad_part(k, key_grad) + right.astype(jnp.float32)
            left = SCALE * grad_part(count - k, key_grad) + left.astype(jnp.float32)
            right, left = by_rows(right.astype(SENT)), by_rows(left.astype(SENT))
            right = lax.ppermute(right, "fsdp", onward)
            left = lax.ppermute(left, "fsdp", back)
        return grad_part(0, key_grad) + (right.astype(jnp.float32) + left.astype(jnp.float32)) / SCALE

    gather, scatter = (gather_keys, scatter_grad) if ringed else (gather_whole, scatter_whole)
    total = sum_replicas(delta[0])
    states, key_grads = [None] * units, [None] * units
    for u in range(units):
        keys, done = gather(owns[u], total if u == 0 else None)
        if u == 0:
            total = done
            new_anchor, new_momentum = outer_update(total, anchor, momentum)
        key_grads[u] = key_gradient(keys, cotan, u, rows)
    for u in range(units):
        *states[u], owns[u] = first_update(
            1, u, fragment, new_anchor, params[0], adam_m[0], adam_v[0], scatter(key_grads[u])
        )
    results = ()
    for u in range(units):
        grad = scatter(key_gradient(gather(owns[u])[0], cotan, u, rows))
        results = last_update(2, u, width, *states[u], grad, results)

    return (*(out[None] for out in results), new_anchor, new_momentum)


def solution(mesh):
    return jax.shard_map(
        on_device,
        mesh=mesh,
        in_specs=(
            P("replica", "fsdp", None),
            P("replica", "fsdp", None),
            P("replica", "fsdp", None),
            P("replica", "fsdp", None),
            P("replica", "fsdp", None),
            P("fsdp", None),
            P("fsdp", None),
            P("replica", "fsdp", None),
            P(),
        ),
        out_specs=(
            P("replica", "fsdp", None),
            P("replica", "fsdp", None),
            P("replica", "fsdp", None),
            P("fsdp", None),
            P("fsdp", None),
        ),
        check_vma=False,
    )
```

```python
import functools

import jax
import jax.numpy as jnp
from jax import lax
from jax.experimental import pallas as pl
from jax.experimental.layout import Layout, with_layout_constraint
from jax.experimental.pallas import tpu as pltpu
from jax.sharding import PartitionSpec as P

HEAD_DIM = 128
KV_HEADS = 4
INNER_STEPS = 2
UNIT_HEADS = 2
RING_MOST = 8
NORM_TILE = 64
CAST_TILE = 512
KEY_TILE = 256
ADAM_TILE = 256
VMEM_BYTES = 10 * 2**20
NORM_VMEM_BYTES = 36 * 2**20
SENT = jnp.float16
SCALE = 1.0 / 128


beta_one = 0.9
beta_two = 0.95
adam_eps = 1e-08
learn_rate = 0.002
weight_decay = 0.1
outer_rate = 0.7
outer_momentum = 0.9
mixing = 0.5


def norm_kernel(values, out):
    floats = values[...].astype(jnp.float32)
    scale = lax.rsqrt(jnp.mean(floats * floats, axis=-1, keepdims=True) + 1e-05)
    out[...] = (floats * scale).astype(jnp.bfloat16)


def norm_rows(values):
    rows, width = values.shape
    tile = NORM_TILE if rows % NORM_TILE == 0 else rows
    block = pl.BlockSpec((tile, width), lambda i: (i, 0))
    return pl.pallas_call(
        norm_kernel,
        grid=(rows // tile,),
        in_specs=[block],
        out_specs=block,
        out_shape=jax.ShapeDtypeStruct(values.shape, jnp.bfloat16),
        cost_estimate=pl.CostEstimate(
            flops=8 * rows * width, bytes_accessed=4 * rows * width, transcendentals=rows
        ),
        compiler_params=pltpu.CompilerParams(vmem_limit_bytes=NORM_VMEM_BYTES),
    )(values)


def cast_kernel(values, out):
    out[...] = values[...].astype(jnp.bfloat16)


def cast_columns(values, unit, cols):
    rows = values.shape[0]
    tile = min(rows, CAST_TILE)
    return pl.pallas_call(
        cast_kernel,
        grid=(rows // tile,),
        in_specs=[pl.BlockSpec((tile, cols), lambda i: (i, unit))],
        out_specs=pl.BlockSpec((tile, cols), lambda i: (i, 0)),
        out_shape=jax.ShapeDtypeStruct((rows, cols), jnp.bfloat16),
        cost_estimate=pl.CostEstimate(
            flops=rows * cols, bytes_accessed=6 * rows * cols, transcendentals=0
        ),
        compiler_params=pltpu.CompilerParams(vmem_limit_bytes=VMEM_BYTES),
    )(values)


def key_kernel(rows, keys, cotan, out):
    for h in range(keys.shape[1] // HEAD_DIM):
        spot = pl.ds(h * HEAD_DIM, HEAD_DIM)
        head = keys[:, spot]
        inverse = lax.rsqrt(jnp.mean(head * head, axis=-1, keepdims=True) + 1e-06)
        unit = head * inverse
        upstream = cotan[:, spot].astype(jnp.float32) / rows
        grads = inverse * (upstream - unit * jnp.mean(upstream * unit, axis=-1, keepdims=True))
        out[:, spot] = grads.astype(jnp.bfloat16)


def key_gradient(keys, cotan, unit, rows):
    count, cols = keys.shape
    tile = KEY_TILE if count % KEY_TILE == 0 else count
    block = pl.BlockSpec((tile, cols), lambda i: (i, 0))
    return pl.pallas_call(
        functools.partial(key_kernel, rows),
        grid=(count // tile,),
        in_specs=[block, pl.BlockSpec((tile, cols), lambda i: (i, unit))],
        out_specs=block,
        out_shape=jax.ShapeDtypeStruct(keys.shape, jnp.bfloat16),
        cost_estimate=pl.CostEstimate(
            flops=12 * count * cols, bytes_accessed=8 * count * cols, transcendentals=count
        ),
        compiler_params=pltpu.CompilerParams(vmem_limit_bytes=VMEM_BYTES),
    )(keys, cotan)


def adam_update(weight, first, second, grad, stamp):
    first = beta_one * first + (1.0 - beta_one) * grad
    second = beta_two * second + (1.0 - beta_two) * grad * grad
    fix_one = 1.0 - beta_one**stamp
    fix_two = 1.0 - beta_two**stamp
    ratio = first / fix_one / (jnp.sqrt(second / fix_two) + adam_eps)
    weight = weight - learn_rate * (ratio + weight_decay * weight)
    return (weight, first, second)


def first_kernel(stamp, unit, fragment, anchor, weight, first, second, grad, out_w, out_m, out_v, own):
    fresh, out_m[...], out_v[...] = adam_update(
        weight[...], first[...], second[...], grad[...], stamp
    )
    heads = fresh.shape[1] // HEAD_DIM
    for h in range(heads):
        head = fresh[:, h * HEAD_DIM : (h + 1) * HEAD_DIM]
        merged = mixing * head + (1.0 - mixing) * anchor[...]
        head = jnp.where(fragment[0] == unit * heads + h, merged, head)
        out_w[:, pl.ds(h * HEAD_DIM, HEAD_DIM)] = head
        own[:, pl.ds(h * HEAD_DIM, HEAD_DIM)] = head.astype(jnp.bfloat16)


def first_update(stamp, unit, fragment, anchor, weight, first, second, grad):
    rows, cols = grad.shape
    tile = min(rows, ADAM_TILE)
    block = pl.BlockSpec((tile, cols), lambda i: (i, 0))
    spot = pl.BlockSpec((tile, cols), lambda i: (i, unit))
    side = pl.BlockSpec((tile, HEAD_DIM), lambda i: (i, 0))
    return pl.pallas_call(
        functools.partial(first_kernel, stamp, unit),
        grid=(rows // tile,),
        in_specs=[pl.BlockSpec(memory_space=pltpu.SMEM), side, spot, spot, spot, block],
        out_specs=[block] * 4,
        out_shape=[jax.ShapeDtypeStruct((rows, cols), jnp.float32)] * 3
        + [jax.ShapeDtypeStruct((rows, cols), jnp.bfloat16)],
        cost_estimate=pl.CostEstimate(
            flops=24 * rows * cols, bytes_accessed=32 * rows * cols, transcendentals=rows * cols
        ),
        compiler_params=pltpu.CompilerParams(vmem_limit_bytes=VMEM_BYTES),
    )(fragment, anchor, weight, first, second, grad)


def last_kernel(stamp, weight, first, second, grad, *rest):
    for out, value in zip(
        rest[-3:], adam_update(weight[...], first[...], second[...], grad[...], stamp)
    ):
        out[...] = value


def last_update(stamp, unit, width, weight, first, second, grad, before):
    rows, cols = grad.shape
    tile = min(rows, ADAM_TILE)
    block = pl.BlockSpec((tile, cols), lambda i: (i, 0))
    spot = pl.BlockSpec((tile, cols), lambda i: (i, unit))
    return pl.pallas_call(
        functools.partial(last_kernel, stamp),
        grid=(rows // tile,),
        in_specs=[block] * 4 + [pl.BlockSpec(memory_space=pl.ANY)] * len(before),
        out_specs=[spot] * 3,
        out_shape=[jax.ShapeDtypeStruct((rows, width), jnp.float32)] * 3,
        input_output_aliases={4 + i: i for i in range(len(before))},
        cost_estimate=pl.CostEstimate(
            flops=20 * rows * cols, bytes_accessed=28 * rows * cols, transcendentals=rows * cols
        ),
        compiler_params=pltpu.CompilerParams(vmem_limit_bytes=VMEM_BYTES),
    )(weight, first, second, grad, *before)


def by_rows(array):
    return with_layout_constraint(array, Layout(major_to_minor=(0, 1)))


def sum_replicas(rows):
    count = lax.axis_size("replica")
    if count & (count - 1):
        return lax.psum(rows, "replica")
    step = 1
    while step < count:
        swaps = [(r, r ^ step) for r in range(count)]
        rows = rows + lax.ppermute(rows, "replica", swaps)
        step *= 2
    return rows


def outer_update(total, anchor, momentum):
    average = total / lax.axis_size("replica")
    fresh_mom = outer_momentum * momentum + average
    fresh_anchor = anchor - outer_rate * (outer_momentum * fresh_mom + average)
    return (fresh_anchor, fresh_mom)


def ring_of(count):
    half = count // 2
    return [2 * p if p < half else 2 * (count - 1 - p) + 1 for p in range(count)]


def on_device(tokens, cotangent, params, adam_m, adam_v, anchor, momentum, delta, fragment):
    count = lax.axis_size("fsdp")
    half = count // 2
    ringed = count % 2 == 0 and count <= RING_MOST
    ring = ring_of(count)
    onward = [(ring[p], ring[(p + 1) % count]) for p in range(count)]
    back = [(ring[(p + 1) % count], ring[p]) for p in range(count)]
    index = lax.axis_index("fsdp")
    place = jnp.where(index % 2 == 0, index // 2, count - 1 - index // 2)

    cotan = cotangent[0]
    depth, width = params.shape[1:]
    unit_cols = UNIT_HEADS * HEAD_DIM
    units = width // unit_cols
    rows = tokens.shape[1] * count

    owns = [cast_columns(params[0], u, unit_cols) for u in range(units)]

    normed = norm_rows(tokens[0])
    normed_at = []
    for k in range(count if ringed else 0):
        spot = (place + k) % count
        owner = jnp.where(spot < half, 2 * spot, 2 * (count - 1 - spot) + 1)
        normed_at.append(lax.dynamic_slice_in_dim(normed, owner * depth, depth, 1))

    def gather_whole(current):
        every = lax.all_gather(current, "fsdp", axis=0, tiled=True)
        return jnp.dot(normed, every, preferred_element_type=jnp.float32), every

    def scatter_whole(key_grad):
        part = lax.dot_general(
            normed, key_grad, (((0,), (0,)), ((), ())), preferred_element_type=jnp.float32
        )
        return lax.psum_scatter(part, "fsdp", scatter_dimension=0, tiled=True)

    def add_rows(k, piece):
        return jnp.dot(normed_at[k], piece, preferred_element_type=jnp.float32)

    def gather_keys(own):
        keys = add_rows(0, own)
        left, right = own, own
        for k in range(1, half):
            left = lax.ppermute(left, "fsdp", onward)
            right = lax.ppermute(right, "fsdp", back)
            keys = keys + add_rows(count - k, left) + add_rows(k, right)
            if k == 2:
                second = (left, right)
        top = lax.ppermute(left[: depth // 2], "fsdp", onward)
        low = lax.ppermute(right[depth // 2 :], "fsdp", back)
        return keys + add_rows(half, jnp.concatenate([top, low], 0)), second

    def grad_part(k, key_grad):
        return lax.dot_general(
            normed_at[k], key_grad, (((0,), (0,)), ((), ())), preferred_element_type=jnp.float32
        )

    def scatter_grad(key_grad):
        far = by_rows((SCALE * grad_part(half, key_grad)).astype(SENT))
        right = lax.ppermute(far[: depth // 2], "fsdp", onward)
        left = lax.ppermute(far[depth // 2 :], "fsdp", back)
        key_grad, right, left = lax.optimization_barrier((key_grad, right, left))
        zeros = jnp.zeros_like(right)
        right = jnp.concatenate([right, zeros], 0)
        left = jnp.concatenate([zeros, left], 0)
        for k in range(half - 1, 0, -1):
            right = SCALE * grad_part(k, key_grad) + right.astype(jnp.float32)
            left = SCALE * grad_part(count - k, key_grad) + left.astype(jnp.float32)
            right, left = by_rows(right.astype(SENT)), by_rows(left.astype(SENT))
            right = lax.ppermute(right, "fsdp", onward)
            left = lax.ppermute(left, "fsdp", back)
        return grad_part(0, key_grad) + (right.astype(jnp.float32) + left.astype(jnp.float32)) / SCALE

    gather, scatter = (gather_keys, scatter_grad) if ringed else (gather_whole, scatter_whole)
    states, key_grads = [None] * units, [None] * units
    for u in range(units):
        keys, arrived = gather(owns[u])
        if u == 0:
            rows_of_delta, _ = lax.optimization_barrier((delta[0], arrived))
            new_anchor, new_momentum = outer_update(sum_replicas(rows_of_delta), anchor, momentum)
        key_grads[u] = key_gradient(keys, cotan, u, rows)
    for u in range(units):
        *states[u], owns[u] = first_update(
            1, u, fragment, new_anchor, params[0], adam_m[0], adam_v[0], scatter(key_grads[u])
        )
    results = ()
    for u in range(units):
        grad = scatter(key_gradient(gather(owns[u])[0], cotan, u, rows))
        results = last_update(2, u, width, *states[u], grad, results)

    return (*(out[None] for out in results), new_anchor, new_momentum)


def solution(mesh):
    return jax.shard_map(
        on_device,
        mesh=mesh,
        in_specs=(
            P("replica", "fsdp", None),
            P("replica", "fsdp", None),
            P("replica", "fsdp", None),
            P("replica", "fsdp", None),
            P("replica", "fsdp", None),
            P("fsdp", None),
            P("fsdp", None),
            P("replica", "fsdp", None),
            P(),
        ),
        out_specs=(
            P("replica", "fsdp", None),
            P("replica", "fsdp", None),
            P("replica", "fsdp", None),
            P("fsdp", None),
            P("fsdp", None),
        ),
        check_vma=False,
    )
```

```python
import functools

import jax
import jax.numpy as jnp
from jax import lax
from jax.experimental import pallas as pl
from jax.experimental.layout import Layout, with_layout_constraint
from jax.experimental.pallas import tpu as pltpu
from jax.sharding import PartitionSpec as P

HEAD_DIM = 128
KV_HEADS = 4
INNER_STEPS = 2
UNIT_HEADS = 1
RING_MOST = 8
NORM_TILE = 64
CAST_TILE = 512
KEY_TILE = 256
ADAM_TILE = 256
VMEM_BYTES = 10 * 2**20
NORM_VMEM_BYTES = 36 * 2**20
SENT = jnp.float16
SCALE = 1.0 / 128


beta_one = 0.9
beta_two = 0.95
adam_eps = 1e-08
learn_rate = 0.002
weight_decay = 0.1
outer_rate = 0.7
outer_momentum = 0.9
mixing = 0.5


def norm_kernel(values, out):
    floats = values[...].astype(jnp.float32)
    scale = lax.rsqrt(jnp.mean(floats * floats, axis=-1, keepdims=True) + 1e-05)
    out[...] = (floats * scale).astype(jnp.bfloat16)


def norm_rows(values):
    rows, width = values.shape
    tile = NORM_TILE if rows % NORM_TILE == 0 else rows
    block = pl.BlockSpec((tile, width), lambda i: (i, 0))
    return pl.pallas_call(
        norm_kernel,
        grid=(rows // tile,),
        in_specs=[block],
        out_specs=block,
        out_shape=jax.ShapeDtypeStruct(values.shape, jnp.bfloat16),
        cost_estimate=pl.CostEstimate(
            flops=8 * rows * width, bytes_accessed=4 * rows * width, transcendentals=rows
        ),
        compiler_params=pltpu.CompilerParams(vmem_limit_bytes=NORM_VMEM_BYTES),
    )(values)


def cast_kernel(values, out):
    out[...] = values[...].astype(jnp.bfloat16)


def cast_columns(values, unit, cols):
    rows = values.shape[0]
    tile = min(rows, CAST_TILE)
    return pl.pallas_call(
        cast_kernel,
        grid=(rows // tile,),
        in_specs=[pl.BlockSpec((tile, cols), lambda i: (i, unit))],
        out_specs=pl.BlockSpec((tile, cols), lambda i: (i, 0)),
        out_shape=jax.ShapeDtypeStruct((rows, cols), jnp.bfloat16),
        cost_estimate=pl.CostEstimate(
            flops=rows * cols, bytes_accessed=6 * rows * cols, transcendentals=0
        ),
        compiler_params=pltpu.CompilerParams(vmem_limit_bytes=VMEM_BYTES),
    )(values)


def key_kernel(rows, keys, cotan, out):
    for h in range(keys.shape[1] // HEAD_DIM):
        spot = pl.ds(h * HEAD_DIM, HEAD_DIM)
        head = keys[:, spot]
        inverse = lax.rsqrt(jnp.mean(head * head, axis=-1, keepdims=True) + 1e-06)
        unit = head * inverse
        upstream = cotan[:, spot].astype(jnp.float32) / rows
        grads = inverse * (upstream - unit * jnp.mean(upstream * unit, axis=-1, keepdims=True))
        out[:, spot] = grads.astype(jnp.bfloat16)


def key_gradient(keys, cotan, unit, rows):
    count, cols = keys.shape
    tile = KEY_TILE if count % KEY_TILE == 0 else count
    block = pl.BlockSpec((tile, cols), lambda i: (i, 0))
    return pl.pallas_call(
        functools.partial(key_kernel, rows),
        grid=(count // tile,),
        in_specs=[block, pl.BlockSpec((tile, cols), lambda i: (i, unit))],
        out_specs=block,
        out_shape=jax.ShapeDtypeStruct(keys.shape, jnp.bfloat16),
        cost_estimate=pl.CostEstimate(
            flops=12 * count * cols, bytes_accessed=8 * count * cols, transcendentals=count
        ),
        compiler_params=pltpu.CompilerParams(vmem_limit_bytes=VMEM_BYTES),
    )(keys, cotan)


def adam_update(weight, first, second, grad, stamp):
    first = beta_one * first + (1.0 - beta_one) * grad
    second = beta_two * second + (1.0 - beta_two) * grad * grad
    fix_one = 1.0 - beta_one**stamp
    fix_two = 1.0 - beta_two**stamp
    ratio = first / fix_one / (jnp.sqrt(second / fix_two) + adam_eps)
    weight = weight - learn_rate * (ratio + weight_decay * weight)
    return (weight, first, second)


def first_kernel(stamp, unit, fragment, anchor, weight, first, second, grad, out_w, out_m, out_v, own):
    fresh, out_m[...], out_v[...] = adam_update(
        weight[...], first[...], second[...], grad[...], stamp
    )
    heads = fresh.shape[1] // HEAD_DIM
    for h in range(heads):
        head = fresh[:, h * HEAD_DIM : (h + 1) * HEAD_DIM]
        merged = mixing * head + (1.0 - mixing) * anchor[...]
        head = jnp.where(fragment[0] == unit * heads + h, merged, head)
        out_w[:, pl.ds(h * HEAD_DIM, HEAD_DIM)] = head
        own[:, pl.ds(h * HEAD_DIM, HEAD_DIM)] = head.astype(jnp.bfloat16)


def first_update(stamp, unit, fragment, anchor, weight, first, second, grad):
    rows, cols = grad.shape
    tile = min(rows, ADAM_TILE)
    block = pl.BlockSpec((tile, cols), lambda i: (i, 0))
    spot = pl.BlockSpec((tile, cols), lambda i: (i, unit))
    side = pl.BlockSpec((tile, HEAD_DIM), lambda i: (i, 0))
    return pl.pallas_call(
        functools.partial(first_kernel, stamp, unit),
        grid=(rows // tile,),
        in_specs=[pl.BlockSpec(memory_space=pltpu.SMEM), side, spot, spot, spot, block],
        out_specs=[block] * 4,
        out_shape=[jax.ShapeDtypeStruct((rows, cols), jnp.float32)] * 3
        + [jax.ShapeDtypeStruct((rows, cols), jnp.bfloat16)],
        cost_estimate=pl.CostEstimate(
            flops=24 * rows * cols, bytes_accessed=32 * rows * cols, transcendentals=rows * cols
        ),
        compiler_params=pltpu.CompilerParams(vmem_limit_bytes=VMEM_BYTES),
    )(fragment, anchor, weight, first, second, grad)


def last_kernel(stamp, weight, first, second, grad, *rest):
    for out, value in zip(
        rest[-3:], adam_update(weight[...], first[...], second[...], grad[...], stamp)
    ):
        out[...] = value


def last_update(stamp, unit, width, weight, first, second, grad, before):
    rows, cols = grad.shape
    tile = min(rows, ADAM_TILE)
    block = pl.BlockSpec((tile, cols), lambda i: (i, 0))
    spot = pl.BlockSpec((tile, cols), lambda i: (i, unit))
    return pl.pallas_call(
        functools.partial(last_kernel, stamp),
        grid=(rows // tile,),
        in_specs=[block] * 4 + [pl.BlockSpec(memory_space=pl.ANY)] * len(before),
        out_specs=[spot] * 3,
        out_shape=[jax.ShapeDtypeStruct((rows, width), jnp.float32)] * 3,
        input_output_aliases={4 + i: i for i in range(len(before))},
        cost_estimate=pl.CostEstimate(
            flops=20 * rows * cols, bytes_accessed=28 * rows * cols, transcendentals=rows * cols
        ),
        compiler_params=pltpu.CompilerParams(vmem_limit_bytes=VMEM_BYTES),
    )(weight, first, second, grad, *before)


def by_rows(array):
    return with_layout_constraint(array, Layout(major_to_minor=(0, 1)))


def sum_replicas(rows):
    count = lax.axis_size("replica")
    if count & (count - 1):
        return lax.psum(rows, "replica")
    step = 1
    while step < count:
        swaps = [(r, r ^ step) for r in range(count)]
        rows = rows + lax.ppermute(rows, "replica", swaps)
        step *= 2
    return rows


def outer_update(total, anchor, momentum):
    average = total / lax.axis_size("replica")
    fresh_mom = outer_momentum * momentum + average
    fresh_anchor = anchor - outer_rate * (outer_momentum * fresh_mom + average)
    return (fresh_anchor, fresh_mom)


def ring_of(count):
    half = count // 2
    return [2 * p if p < half else 2 * (count - 1 - p) + 1 for p in range(count)]


def on_device(tokens, cotangent, params, adam_m, adam_v, anchor, momentum, delta, fragment):
    count = lax.axis_size("fsdp")
    half = count // 2
    ringed = count % 2 == 0 and count <= RING_MOST
    ring = ring_of(count)
    onward = [(ring[p], ring[(p + 1) % count]) for p in range(count)]
    back = [(ring[(p + 1) % count], ring[p]) for p in range(count)]
    index = lax.axis_index("fsdp")
    place = jnp.where(index % 2 == 0, index // 2, count - 1 - index // 2)

    cotan = cotangent[0]
    depth, width = params.shape[1:]
    unit_cols = UNIT_HEADS * HEAD_DIM
    units = width // unit_cols
    rows = tokens.shape[1] * count

    owns = [cast_columns(params[0], u, unit_cols) for u in range(units)]

    normed = norm_rows(tokens[0])
    normed_at = []
    for k in range(count if ringed else 0):
        spot = (place + k) % count
        owner = jnp.where(spot < half, 2 * spot, 2 * (count - 1 - spot) + 1)
        normed_at.append(lax.dynamic_slice_in_dim(normed, owner * depth, depth, 1))

    def gather_whole(current):
        every = lax.all_gather(current, "fsdp", axis=0, tiled=True)
        return jnp.dot(normed, every, preferred_element_type=jnp.float32), every

    def scatter_whole(key_grad):
        part = lax.dot_general(
            normed, key_grad, (((0,), (0,)), ((), ())), preferred_element_type=jnp.float32
        )
        return lax.psum_scatter(part, "fsdp", scatter_dimension=0, tiled=True)

    def add_rows(k, piece):
        return jnp.dot(normed_at[k], piece, preferred_element_type=jnp.float32)

    def gather_keys(own):
        keys = add_rows(0, own)
        left, right = own, own
        for k in range(1, half):
            left = lax.ppermute(left, "fsdp", onward)
            right = lax.ppermute(right, "fsdp", back)
            keys = keys + add_rows(count - k, left) + add_rows(k, right)
            if k == 2:
                second = (left, right)
        top = lax.ppermute(left[: depth // 2], "fsdp", onward)
        low = lax.ppermute(right[depth // 2 :], "fsdp", back)
        return keys + add_rows(half, jnp.concatenate([top, low], 0)), second

    def grad_part(k, key_grad):
        return lax.dot_general(
            normed_at[k], key_grad, (((0,), (0,)), ((), ())), preferred_element_type=jnp.float32
        )

    def scatter_grad(key_grad):
        far = by_rows((SCALE * grad_part(half, key_grad)).astype(SENT))
        right = lax.ppermute(far[: depth // 2], "fsdp", onward)
        left = lax.ppermute(far[depth // 2 :], "fsdp", back)
        key_grad, right, left = lax.optimization_barrier((key_grad, right, left))
        zeros = jnp.zeros_like(right)
        right = jnp.concatenate([right, zeros], 0)
        left = jnp.concatenate([zeros, left], 0)
        for k in range(half - 1, 0, -1):
            right = SCALE * grad_part(k, key_grad) + right.astype(jnp.float32)
            left = SCALE * grad_part(count - k, key_grad) + left.astype(jnp.float32)
            right, left = by_rows(right.astype(SENT)), by_rows(left.astype(SENT))
            right = lax.ppermute(right, "fsdp", onward)
            left = lax.ppermute(left, "fsdp", back)
        return grad_part(0, key_grad) + (right.astype(jnp.float32) + left.astype(jnp.float32)) / SCALE

    gather, scatter = (gather_keys, scatter_grad) if ringed else (gather_whole, scatter_whole)
    states, key_grads = [None] * units, [None] * units
    for u in range(units):
        keys, arrived = gather(owns[u])
        if u == 0:
            rows_of_delta, _ = lax.optimization_barrier((delta[0], arrived))
            new_anchor, new_momentum = outer_update(sum_replicas(rows_of_delta), anchor, momentum)
        key_grads[u] = key_gradient(keys, cotan, u, rows)
    for u in range(units):
        *states[u], owns[u] = first_update(
            1, u, fragment, new_anchor, params[0], adam_m[0], adam_v[0], scatter(key_grads[u])
        )
    results = ()
    for u in range(units):
        grad = scatter(key_gradient(gather(owns[u])[0], cotan, u, rows))
        results = last_update(2, u, width, *states[u], grad, results)

    return (*(out[None] for out in results), new_anchor, new_momentum)


def solution(mesh):
    return jax.shard_map(
        on_device,
        mesh=mesh,
        in_specs=(
            P("replica", "fsdp", None),
            P("replica", "fsdp", None),
            P("replica", "fsdp", None),
            P("replica", "fsdp", None),
            P("replica", "fsdp", None),
            P("fsdp", None),
            P("fsdp", None),
            P("replica", "fsdp", None),
            P(),
        ),
        out_specs=(
            P("replica", "fsdp", None),
            P("replica", "fsdp", None),
            P("replica", "fsdp", None),
            P("fsdp", None),
            P("fsdp", None),
        ),
        check_vma=False,
    )
```

```python
import functools

import jax
import jax.numpy as jnp
from jax import lax
from jax.experimental import pallas as pl
from jax.experimental.layout import Layout, with_layout_constraint
from jax.experimental.pallas import tpu as pltpu
from jax.sharding import PartitionSpec as P

HEAD_DIM = 128
KV_HEADS = 4
INNER_STEPS = 2
UNIT_HEADS = 2
RING_MOST = 8
NORM_TILE = 64
CAST_TILE = 512
KEY_TILE = 256
OWN_TILE = 256
ADAM_TILE = 256
VMEM_BYTES = 10 * 2**20
NORM_VMEM_BYTES = 36 * 2**20
CAST_VMEM_BYTES = 62 * 2**20
SENT = jnp.float16
SCALE = 1.0 / 128


beta_one = 0.9
beta_two = 0.95
adam_eps = 1e-08
learn_rate = 0.002
weight_decay = 0.1
outer_rate = 0.7
outer_momentum = 0.9
mixing = 0.5


def norm_kernel(values, out):
    floats = values[...].astype(jnp.float32)
    scale = lax.rsqrt(jnp.mean(floats * floats, axis=-1, keepdims=True) + 1e-05)
    out[...] = (floats * scale).astype(jnp.bfloat16)


def norm_rows(values):
    rows, width = values.shape
    tile = NORM_TILE if rows % NORM_TILE == 0 else rows
    block = pl.BlockSpec((tile, width), lambda i: (i, 0))
    return pl.pallas_call(
        norm_kernel,
        grid=(rows // tile,),
        in_specs=[block],
        out_specs=block,
        out_shape=jax.ShapeDtypeStruct(values.shape, jnp.bfloat16),
        cost_estimate=pl.CostEstimate(
            flops=8 * rows * width, bytes_accessed=4 * rows * width, transcendentals=rows
        ),
        compiler_params=pltpu.CompilerParams(vmem_limit_bytes=NORM_VMEM_BYTES),
    )(values)


def cast_kernel(values, out):
    out[...] = values[...].astype(jnp.bfloat16)


def cast_columns(values, unit, cols):
    rows = values.shape[0]
    tile = min(rows, CAST_TILE)
    return pl.pallas_call(
        cast_kernel,
        grid=(rows // tile,),
        in_specs=[pl.BlockSpec((tile, cols), lambda i: (i, unit))],
        out_specs=pl.BlockSpec((tile, cols), lambda i: (i, 0)),
        out_shape=jax.ShapeDtypeStruct((rows, cols), jnp.bfloat16),
        cost_estimate=pl.CostEstimate(
            flops=rows * cols, bytes_accessed=6 * rows * cols, transcendentals=0
        ),
        compiler_params=pltpu.CompilerParams(vmem_limit_bytes=CAST_VMEM_BYTES),
    )(values)


def key_kernel(rows, keys, cotan, out):
    for h in range(keys.shape[1] // HEAD_DIM):
        spot = pl.ds(h * HEAD_DIM, HEAD_DIM)
        head = keys[:, spot]
        inverse = lax.rsqrt(jnp.mean(head * head, axis=-1, keepdims=True) + 1e-06)
        unit = head * inverse
        upstream = cotan[:, spot].astype(jnp.float32) / rows
        grads = inverse * (upstream - unit * jnp.mean(upstream * unit, axis=-1, keepdims=True))
        out[:, spot] = grads.astype(jnp.bfloat16)


def key_gradient(keys, cotan, unit, rows):
    count, cols = keys.shape
    tile = KEY_TILE if count % KEY_TILE == 0 else count
    block = pl.BlockSpec((tile, cols), lambda i: (i, 0))
    return pl.pallas_call(
        functools.partial(key_kernel, rows),
        grid=(count // tile,),
        in_specs=[block, pl.BlockSpec((tile, cols), lambda i: (i, unit))],
        out_specs=block,
        out_shape=jax.ShapeDtypeStruct(keys.shape, jnp.bfloat16),
        cost_estimate=pl.CostEstimate(
            flops=12 * count * cols, bytes_accessed=8 * count * cols, transcendentals=count
        ),
        compiler_params=pltpu.CompilerParams(vmem_limit_bytes=VMEM_BYTES),
    )(keys, cotan)


def own_kernel(spot, normed, key_grad, out):
    out[...] = lax.dot_general(
        normed[...], key_grad[...], (((0,), (0,)), ((), ())), preferred_element_type=jnp.float32
    )


def own_term(normed, spot, key_grad, depth):
    count, cols = key_grad.shape
    tile = min(depth, OWN_TILE)
    tiles = depth // tile
    return pl.pallas_call(
        own_kernel,
        grid_spec=pltpu.PrefetchScalarGridSpec(
            num_scalar_prefetch=1,
            grid=(tiles,),
            in_specs=[
                pl.BlockSpec((count, tile), lambda i, place: (0, place[0] * tiles + i)),
                pl.BlockSpec((count, cols), lambda i, place: (0, 0)),
            ],
            out_specs=pl.BlockSpec((tile, cols), lambda i, place: (i, 0)),
        ),
        out_shape=jax.ShapeDtypeStruct((depth, cols), jnp.float32),
        cost_estimate=pl.CostEstimate(
            flops=2 * count * cols * depth,
            bytes_accessed=2 * count * depth + 2 * count * cols + 4 * depth * cols,
            transcendentals=0,
        ),
        compiler_params=pltpu.CompilerParams(vmem_limit_bytes=VMEM_BYTES),
    )(spot, normed, key_grad)


def adam_update(weight, first, second, grad, stamp):
    first = beta_one * first + (1.0 - beta_one) * grad
    second = beta_two * second + (1.0 - beta_two) * grad * grad
    fix_one = 1.0 - beta_one**stamp
    fix_two = 1.0 - beta_two**stamp
    ratio = first / fix_one / (jnp.sqrt(second / fix_two) + adam_eps)
    weight = weight - learn_rate * (ratio + weight_decay * weight)
    return (weight, first, second)


def first_kernel(stamp, unit, fragment, anchor, weight, first, second, grad, out_w, out_m, out_v, own):
    fresh, out_m[...], out_v[...] = adam_update(
        weight[...], first[...], second[...], grad[...], stamp
    )
    heads = fresh.shape[1] // HEAD_DIM
    for h in range(heads):
        head = fresh[:, h * HEAD_DIM : (h + 1) * HEAD_DIM]
        merged = mixing * head + (1.0 - mixing) * anchor[...]
        head = jnp.where(fragment[0] == unit * heads + h, merged, head)
        out_w[:, pl.ds(h * HEAD_DIM, HEAD_DIM)] = head
        own[:, pl.ds(h * HEAD_DIM, HEAD_DIM)] = head.astype(jnp.bfloat16)


def first_update(stamp, unit, fragment, anchor, weight, first, second, grad):
    rows, cols = grad.shape
    tile = min(rows, ADAM_TILE)
    block = pl.BlockSpec((tile, cols), lambda i: (i, 0))
    spot = pl.BlockSpec((tile, cols), lambda i: (i, unit))
    side = pl.BlockSpec((tile, HEAD_DIM), lambda i: (i, 0))
    return pl.pallas_call(
        functools.partial(first_kernel, stamp, unit),
        grid=(rows // tile,),
        in_specs=[pl.BlockSpec(memory_space=pltpu.SMEM), side, spot, spot, spot, block],
        out_specs=[block] * 4,
        out_shape=[jax.ShapeDtypeStruct((rows, cols), jnp.float32)] * 3
        + [jax.ShapeDtypeStruct((rows, cols), jnp.bfloat16)],
        cost_estimate=pl.CostEstimate(
            flops=24 * rows * cols, bytes_accessed=32 * rows * cols, transcendentals=rows * cols
        ),
        compiler_params=pltpu.CompilerParams(vmem_limit_bytes=VMEM_BYTES),
    )(fragment, anchor, weight, first, second, grad)


def last_kernel(stamp, weight, first, second, grad, *rest):
    for out, value in zip(
        rest[-3:], adam_update(weight[...], first[...], second[...], grad[...], stamp)
    ):
        out[...] = value


def last_update(stamp, unit, width, weight, first, second, grad, before):
    rows, cols = grad.shape
    tile = min(rows, ADAM_TILE)
    block = pl.BlockSpec((tile, cols), lambda i: (i, 0))
    spot = pl.BlockSpec((tile, cols), lambda i: (i, unit))
    return pl.pallas_call(
        functools.partial(last_kernel, stamp),
        grid=(rows // tile,),
        in_specs=[block] * 4 + [pl.BlockSpec(memory_space=pl.ANY)] * len(before),
        out_specs=[spot] * 3,
        out_shape=[jax.ShapeDtypeStruct((rows, width), jnp.float32)] * 3,
        input_output_aliases={4 + i: i for i in range(len(before))},
        cost_estimate=pl.CostEstimate(
            flops=20 * rows * cols, bytes_accessed=28 * rows * cols, transcendentals=rows * cols
        ),
        compiler_params=pltpu.CompilerParams(vmem_limit_bytes=VMEM_BYTES),
    )(weight, first, second, grad, *before)


def by_rows(array):
    return with_layout_constraint(array, Layout(major_to_minor=(0, 1)))


def sum_replicas(rows):
    count = lax.axis_size("replica")
    if count & (count - 1):
        return lax.psum(rows, "replica")
    step = 1
    while step < count:
        swaps = [(r, r ^ step) for r in range(count)]
        rows = rows + lax.ppermute(rows, "replica", swaps)
        step *= 2
    return rows


def outer_update(total, anchor, momentum):
    average = total / lax.axis_size("replica")
    fresh_mom = outer_momentum * momentum + average
    fresh_anchor = anchor - outer_rate * (outer_momentum * fresh_mom + average)
    return (fresh_anchor, fresh_mom)


def ring_of(count):
    half = count // 2
    return [2 * p if p < half else 2 * (count - 1 - p) + 1 for p in range(count)]


def on_device(tokens, cotangent, params, adam_m, adam_v, anchor, momentum, delta, fragment):
    count = lax.axis_size("fsdp")
    half = count // 2
    ringed = count % 2 == 0 and count <= RING_MOST
    ring = ring_of(count)
    onward = [(ring[p], ring[(p + 1) % count]) for p in range(count)]
    back = [(ring[(p + 1) % count], ring[p]) for p in range(count)]
    index = lax.axis_index("fsdp")
    place = jnp.where(index % 2 == 0, index // 2, count - 1 - index // 2)

    cotan = cotangent[0]
    depth, width = params.shape[1:]
    unit_cols = UNIT_HEADS * HEAD_DIM
    units = width // unit_cols
    rows = tokens.shape[1] * count

    owns = [cast_columns(params[0], u, unit_cols) for u in range(units)]

    normed = norm_rows(tokens[0])
    normed_at, places = [], []
    for k in range(count if ringed else 0):
        spot = (place + k) % count
        owner = jnp.where(spot < half, 2 * spot, 2 * (count - 1 - spot) + 1)
        normed_at.append(lax.dynamic_slice_in_dim(normed, owner * depth, depth, 1))
        places.append(owner.astype(jnp.int32).reshape(1))

    def gather_whole(current):
        every = lax.all_gather(current, "fsdp", axis=0, tiled=True)
        return jnp.dot(normed, every, preferred_element_type=jnp.float32), every

    def scatter_whole(key_grad, last=False):
        part = lax.dot_general(
            normed, key_grad, (((0,), (0,)), ((), ())), preferred_element_type=jnp.float32
        )
        return lax.psum_scatter(part, "fsdp", scatter_dimension=0, tiled=True)

    def add_rows(k, piece):
        return jnp.dot(normed_at[k], piece, preferred_element_type=jnp.float32)

    def gather_keys(own):
        keys = add_rows(0, own)
        left, right = own, own
        for k in range(1, half):
            left = lax.ppermute(left, "fsdp", onward)
            right = lax.ppermute(right, "fsdp", back)
            keys = keys + add_rows(count - k, left) + add_rows(k, right)
            if k == 2:
                second = (left, right)
        top = lax.ppermute(left[: depth // 2], "fsdp", onward)
        low = lax.ppermute(right[depth // 2 :], "fsdp", back)
        return keys + add_rows(half, jnp.concatenate([top, low], 0)), second

    def grad_part(k, key_grad):
        return lax.dot_general(
            normed_at[k], key_grad, (((0,), (0,)), ((), ())), preferred_element_type=jnp.float32
        )

    def scatter_grad(key_grad, last=False):
        far = by_rows((SCALE * grad_part(half, key_grad)).astype(SENT))
        right = lax.ppermute(far[: depth // 2], "fsdp", onward)
        left = lax.ppermute(far[depth // 2 :], "fsdp", back)
        key_grad, right, left = lax.optimization_barrier((key_grad, right, left))
        zeros = jnp.zeros_like(right)
        right = jnp.concatenate([right, zeros], 0)
        left = jnp.concatenate([zeros, left], 0)
        for k in range(half - 1, 0, -1):
            right = SCALE * grad_part(k, key_grad) + right.astype(jnp.float32)
            left = SCALE * grad_part(count - k, key_grad) + left.astype(jnp.float32)
            right, left = by_rows(right.astype(SENT)), by_rows(left.astype(SENT))
            right = lax.ppermute(right, "fsdp", onward)
            left = lax.ppermute(left, "fsdp", back)
        own = own_term(normed, places[0], key_grad, depth) if last else grad_part(0, key_grad)
        return own + (right.astype(jnp.float32) + left.astype(jnp.float32)) / SCALE

    gather, scatter = (gather_keys, scatter_grad) if ringed else (gather_whole, scatter_whole)
    states, key_grads = [None] * units, [None] * units
    for u in range(units):
        keys, arrived = gather(owns[u])
        if u == 0:
            rows_of_delta, _ = lax.optimization_barrier((delta[0], arrived))
            new_anchor, new_momentum = outer_update(sum_replicas(rows_of_delta), anchor, momentum)
        key_grads[u] = key_gradient(keys, cotan, u, rows)
    for u in range(units):
        *states[u], owns[u] = first_update(
            1, u, fragment, new_anchor, params[0], adam_m[0], adam_v[0], scatter(key_grads[u])
        )
    results = ()
    for u in range(units):
        grad = scatter(key_gradient(gather(owns[u])[0], cotan, u, rows), u == units - 1)
        results = last_update(2, u, width, *states[u], grad, results)

    return (*(out[None] for out in results), new_anchor, new_momentum)


def solution(mesh):
    return jax.shard_map(
        on_device,
        mesh=mesh,
        in_specs=(
            P("replica", "fsdp", None),
            P("replica", "fsdp", None),
            P("replica", "fsdp", None),
            P("replica", "fsdp", None),
            P("replica", "fsdp", None),
            P("fsdp", None),
            P("fsdp", None),
            P("replica", "fsdp", None),
            P(),
        ),
        out_specs=(
            P("replica", "fsdp", None),
            P("replica", "fsdp", None),
            P("replica", "fsdp", None),
            P("fsdp", None),
            P("fsdp", None),
        ),
        check_vma=False,
    )
```

```python
import functools

import jax
import jax.numpy as jnp
from jax import lax
from jax.experimental import pallas as pl
from jax.experimental.layout import Layout, with_layout_constraint
from jax.experimental.pallas import tpu as pltpu
from jax.sharding import PartitionSpec as P

HEAD_DIM = 128
KV_HEADS = 4
INNER_STEPS = 2
UNIT_HEADS = 2
RING_MOST = 8
NORM_TILE = 128
CAST_TILE = 512
KEY_TILE = 256
OWN_TILE = 256
ADAM_TILE = 512
VMEM_BYTES = 14 * 2**20
NORM_VMEM_BYTES = 36 * 2**20
SENT = jnp.float16
SCALE = 1.0 / 128


beta_one = 0.9
beta_two = 0.95
adam_eps = 1e-08
learn_rate = 0.002
weight_decay = 0.1
outer_rate = 0.7
outer_momentum = 0.9
mixing = 0.5


def norm_kernel(values, out):
    floats = values[...].astype(jnp.float32)
    scale = lax.rsqrt(jnp.mean(floats * floats, axis=-1, keepdims=True) + 1e-05)
    out[...] = (floats * scale).astype(jnp.bfloat16)


def norm_rows(values):
    rows, width = values.shape
    tile = NORM_TILE if rows % NORM_TILE == 0 else rows
    block = pl.BlockSpec((tile, width), lambda i: (i, 0))
    return pl.pallas_call(
        norm_kernel,
        grid=(rows // tile,),
        in_specs=[block],
        out_specs=block,
        out_shape=jax.ShapeDtypeStruct(values.shape, jnp.bfloat16),
        cost_estimate=pl.CostEstimate(
            flops=8 * rows * width, bytes_accessed=4 * rows * width, transcendentals=rows
        ),
        compiler_params=pltpu.CompilerParams(vmem_limit_bytes=NORM_VMEM_BYTES),
    )(values)


def cast_kernel(values, out):
    out[...] = values[...].astype(jnp.bfloat16)


def cast_columns(values, unit, cols):
    rows = values.shape[0]
    tile = min(rows, CAST_TILE)
    return pl.pallas_call(
        cast_kernel,
        grid=(rows // tile,),
        in_specs=[pl.BlockSpec((tile, cols), lambda i: (i, unit))],
        out_specs=pl.BlockSpec((tile, cols), lambda i: (i, 0)),
        out_shape=jax.ShapeDtypeStruct((rows, cols), jnp.bfloat16),
        cost_estimate=pl.CostEstimate(
            flops=rows * cols, bytes_accessed=6 * rows * cols, transcendentals=0
        ),
        compiler_params=pltpu.CompilerParams(vmem_limit_bytes=VMEM_BYTES),
    )(values)


def key_kernel(rows, keys, cotan, out):
    for h in range(keys.shape[1] // HEAD_DIM):
        spot = pl.ds(h * HEAD_DIM, HEAD_DIM)
        head = keys[:, spot]
        inverse = lax.rsqrt(jnp.mean(head * head, axis=-1, keepdims=True) + 1e-06)
        unit = head * inverse
        upstream = cotan[:, spot].astype(jnp.float32) / rows
        grads = inverse * (upstream - unit * jnp.mean(upstream * unit, axis=-1, keepdims=True))
        out[:, spot] = grads.astype(jnp.bfloat16)


def key_gradient(keys, cotan, unit, rows):
    count, cols = keys.shape
    tile = KEY_TILE if count % KEY_TILE == 0 else count
    block = pl.BlockSpec((tile, cols), lambda i: (i, 0))
    return pl.pallas_call(
        functools.partial(key_kernel, rows),
        grid=(count // tile,),
        in_specs=[block, pl.BlockSpec((tile, cols), lambda i: (i, unit))],
        out_specs=block,
        out_shape=jax.ShapeDtypeStruct(keys.shape, jnp.bfloat16),
        cost_estimate=pl.CostEstimate(
            flops=12 * count * cols, bytes_accessed=8 * count * cols, transcendentals=count
        ),
        compiler_params=pltpu.CompilerParams(vmem_limit_bytes=VMEM_BYTES),
    )(keys, cotan)


def own_kernel(spot, normed, key_grad, out):
    out[...] = lax.dot_general(
        normed[...], key_grad[...], (((0,), (0,)), ((), ())), preferred_element_type=jnp.float32
    )


def own_term(normed, spot, key_grad, depth):
    count, cols = key_grad.shape
    tile = min(depth, OWN_TILE)
    tiles = depth // tile
    return pl.pallas_call(
        own_kernel,
        grid_spec=pltpu.PrefetchScalarGridSpec(
            num_scalar_prefetch=1,
            grid=(tiles,),
            in_specs=[
                pl.BlockSpec((count, tile), lambda i, place: (0, place[0] * tiles + i)),
                pl.BlockSpec((count, cols), lambda i, place: (0, 0)),
            ],
            out_specs=pl.BlockSpec((tile, cols), lambda i, place: (i, 0)),
        ),
        out_shape=jax.ShapeDtypeStruct((depth, cols), jnp.float32),
        cost_estimate=pl.CostEstimate(
            flops=2 * count * cols * depth,
            bytes_accessed=2 * count * depth + 2 * count * cols + 4 * depth * cols,
            transcendentals=0,
        ),
        compiler_params=pltpu.CompilerParams(vmem_limit_bytes=VMEM_BYTES),
    )(spot, normed, key_grad)


def adam_update(weight, first, second, grad, stamp):
    first = beta_one * first + (1.0 - beta_one) * grad
    second = beta_two * second + (1.0 - beta_two) * grad * grad
    fix_one = 1.0 - beta_one**stamp
    fix_two = 1.0 - beta_two**stamp
    ratio = first / fix_one / (jnp.sqrt(second / fix_two) + adam_eps)
    weight = weight - learn_rate * (ratio + weight_decay * weight)
    return (weight, first, second)


def first_kernel(stamp, unit, fragment, anchor, weight, first, second, grad, out_w, out_m, out_v, own):
    fresh, out_m[...], out_v[...] = adam_update(
        weight[...], first[...], second[...], grad[...], stamp
    )
    heads = fresh.shape[1] // HEAD_DIM
    for h in range(heads):
        head = fresh[:, h * HEAD_DIM : (h + 1) * HEAD_DIM]
        merged = mixing * head + (1.0 - mixing) * anchor[...]
        head = jnp.where(fragment[0] == unit * heads + h, merged, head)
        out_w[:, pl.ds(h * HEAD_DIM, HEAD_DIM)] = head
        own[:, pl.ds(h * HEAD_DIM, HEAD_DIM)] = head.astype(jnp.bfloat16)


def first_update(stamp, unit, fragment, anchor, weight, first, second, grad):
    rows, cols = grad.shape
    tile = min(rows, ADAM_TILE)
    block = pl.BlockSpec((tile, cols), lambda i: (i, 0))
    spot = pl.BlockSpec((tile, cols), lambda i: (i, unit))
    side = pl.BlockSpec((tile, HEAD_DIM), lambda i: (i, 0))
    return pl.pallas_call(
        functools.partial(first_kernel, stamp, unit),
        grid=(rows // tile,),
        in_specs=[pl.BlockSpec(memory_space=pltpu.SMEM), side, spot, spot, spot, block],
        out_specs=[block] * 4,
        out_shape=[jax.ShapeDtypeStruct((rows, cols), jnp.float32)] * 3
        + [jax.ShapeDtypeStruct((rows, cols), jnp.bfloat16)],
        cost_estimate=pl.CostEstimate(
            flops=24 * rows * cols, bytes_accessed=32 * rows * cols, transcendentals=rows * cols
        ),
        compiler_params=pltpu.CompilerParams(vmem_limit_bytes=VMEM_BYTES),
    )(fragment, anchor, weight, first, second, grad)


def last_kernel(stamp, weight, first, second, grad, *rest):
    for out, value in zip(
        rest[-3:], adam_update(weight[...], first[...], second[...], grad[...], stamp)
    ):
        out[...] = value


def last_update(stamp, unit, width, weight, first, second, grad, before):
    rows, cols = grad.shape
    tile = min(rows, ADAM_TILE)
    block = pl.BlockSpec((tile, cols), lambda i: (i, 0))
    spot = pl.BlockSpec((tile, cols), lambda i: (i, unit))
    return pl.pallas_call(
        functools.partial(last_kernel, stamp),
        grid=(rows // tile,),
        in_specs=[block] * 4 + [pl.BlockSpec(memory_space=pl.ANY)] * len(before),
        out_specs=[spot] * 3,
        out_shape=[jax.ShapeDtypeStruct((rows, width), jnp.float32)] * 3,
        input_output_aliases={4 + i: i for i in range(len(before))},
        cost_estimate=pl.CostEstimate(
            flops=20 * rows * cols, bytes_accessed=28 * rows * cols, transcendentals=rows * cols
        ),
        compiler_params=pltpu.CompilerParams(vmem_limit_bytes=VMEM_BYTES),
    )(weight, first, second, grad, *before)


def by_rows(array):
    return with_layout_constraint(array, Layout(major_to_minor=(0, 1)))


def sum_replicas(rows):
    count = lax.axis_size("replica")
    if count & (count - 1):
        return lax.psum(rows, "replica")
    step = 1
    while step < count:
        swaps = [(r, r ^ step) for r in range(count)]
        rows = rows + lax.ppermute(rows, "replica", swaps)
        step *= 2
    return rows


def outer_update(total, anchor, momentum):
    average = total / lax.axis_size("replica")
    fresh_mom = outer_momentum * momentum + average
    fresh_anchor = anchor - outer_rate * (outer_momentum * fresh_mom + average)
    return (fresh_anchor, fresh_mom)


def ring_of(count):
    half = count // 2
    return [2 * p if p < half else 2 * (count - 1 - p) + 1 for p in range(count)]


def on_device(tokens, cotangent, params, adam_m, adam_v, anchor, momentum, delta, fragment):
    count = lax.axis_size("fsdp")
    half = count // 2
    ringed = count % 2 == 0 and count <= RING_MOST
    ring = ring_of(count)
    onward = [(ring[p], ring[(p + 1) % count]) for p in range(count)]
    back = [(ring[(p + 1) % count], ring[p]) for p in range(count)]
    index = lax.axis_index("fsdp")
    place = jnp.where(index % 2 == 0, index // 2, count - 1 - index // 2)

    cotan = cotangent[0]
    depth, width = params.shape[1:]
    unit_cols = UNIT_HEADS * HEAD_DIM
    units = width // unit_cols
    rows = tokens.shape[1] * count

    owns = [cast_columns(params[0], u, unit_cols) for u in range(units)]

    normed = norm_rows(tokens[0])
    normed_at, places = [], []
    for k in range(count if ringed else 0):
        spot = (place + k) % count
        owner = jnp.where(spot < half, 2 * spot, 2 * (count - 1 - spot) + 1)
        normed_at.append(lax.dynamic_slice_in_dim(normed, owner * depth, depth, 1))
        places.append(owner.astype(jnp.int32).reshape(1))

    def gather_whole(current):
        every = lax.all_gather(current, "fsdp", axis=0, tiled=True)
        return jnp.dot(normed, every, preferred_element_type=jnp.float32), every

    def scatter_whole(key_grad, last=False):
        part = lax.dot_general(
            normed, key_grad, (((0,), (0,)), ((), ())), preferred_element_type=jnp.float32
        )
        return lax.psum_scatter(part, "fsdp", scatter_dimension=0, tiled=True)

    def add_rows(k, piece):
        return jnp.dot(normed_at[k], piece, preferred_element_type=jnp.float32)

    def gather_keys(own):
        keys = add_rows(0, own)
        left, right = own, own
        for k in range(1, half):
            left = lax.ppermute(left, "fsdp", onward)
            right = lax.ppermute(right, "fsdp", back)
            keys = keys + add_rows(count - k, left) + add_rows(k, right)
            if k == 2:
                second = (left, right)
        top = lax.ppermute(left[: depth // 2], "fsdp", onward)
        low = lax.ppermute(right[depth // 2 :], "fsdp", back)
        return keys + add_rows(half, jnp.concatenate([top, low], 0)), second

    def grad_part(k, key_grad):
        return lax.dot_general(
            normed_at[k], key_grad, (((0,), (0,)), ((), ())), preferred_element_type=jnp.float32
        )

    def scatter_grad(key_grad, last=False):
        far = by_rows((SCALE * grad_part(half, key_grad)).astype(SENT))
        right = lax.ppermute(far[: depth // 2], "fsdp", onward)
        left = lax.ppermute(far[depth // 2 :], "fsdp", back)
        key_grad, right, left = lax.optimization_barrier((key_grad, right, left))
        zeros = jnp.zeros_like(right)
        right = jnp.concatenate([right, zeros], 0)
        left = jnp.concatenate([zeros, left], 0)
        for k in range(half - 1, 0, -1):
            right = SCALE * grad_part(k, key_grad) + right.astype(jnp.float32)
            left = SCALE * grad_part(count - k, key_grad) + left.astype(jnp.float32)
            right, left = by_rows(right.astype(SENT)), by_rows(left.astype(SENT))
            right = lax.ppermute(right, "fsdp", onward)
            left = lax.ppermute(left, "fsdp", back)
        own = own_term(normed, places[0], key_grad, depth) if last else grad_part(0, key_grad)
        return own + (right.astype(jnp.float32) + left.astype(jnp.float32)) / SCALE

    gather, scatter = (gather_keys, scatter_grad) if ringed else (gather_whole, scatter_whole)
    states, key_grads = [None] * units, [None] * units
    for u in range(units):
        keys, arrived = gather(owns[u])
        if u == 0:
            rows_of_delta, _ = lax.optimization_barrier((delta[0], arrived))
            new_anchor, new_momentum = outer_update(sum_replicas(rows_of_delta), anchor, momentum)
        key_grads[u] = key_gradient(keys, cotan, u, rows)
    for u in range(units):
        *states[u], owns[u] = first_update(
            1, u, fragment, new_anchor, params[0], adam_m[0], adam_v[0], scatter(key_grads[u])
        )
    results = ()
    for u in range(units):
        grad = scatter(key_gradient(gather(owns[u])[0], cotan, u, rows), u == units - 1)
        results = last_update(2, u, width, *states[u], grad, results)

    return (*(out[None] for out in results), new_anchor, new_momentum)


def solution(mesh):
    return jax.shard_map(
        on_device,
        mesh=mesh,
        in_specs=(
            P("replica", "fsdp", None),
            P("replica", "fsdp", None),
            P("replica", "fsdp", None),
            P("replica", "fsdp", None),
            P("replica", "fsdp", None),
            P("fsdp", None),
            P("fsdp", None),
            P("replica", "fsdp", None),
            P(),
        ),
        out_specs=(
            P("replica", "fsdp", None),
            P("replica", "fsdp", None),
            P("replica", "fsdp", None),
            P("fsdp", None),
            P("fsdp", None),
        ),
        check_vma=False,
    )
```

```python
import functools

import jax
import jax.numpy as jnp
from jax import lax
from jax.experimental import pallas as pl
from jax.experimental.layout import Layout, with_layout_constraint
from jax.experimental.pallas import tpu as pltpu
from jax.sharding import PartitionSpec as P

HEAD_DIM = 128
KV_HEADS = 4
INNER_STEPS = 2
UNIT_HEADS = 2
RING_MOST = 8
NORM_TILE = 128
CAST_TILE = 512
KEY_TILE = 256
OWN_TILE = 256
ADAM_TILE = 512
VMEM_BYTES = 14 * 2**20
NORM_VMEM_BYTES = 36 * 2**20
SENT = jnp.float16
SCALE = 1.0 / 128


beta_one = 0.9
beta_two = 0.95
adam_eps = 1e-08
learn_rate = 0.002
weight_decay = 0.1
outer_rate = 0.7
outer_momentum = 0.9
mixing = 0.5


def norm_kernel(values, out):
    floats = values[...].astype(jnp.float32)
    scale = lax.rsqrt(jnp.mean(floats * floats, axis=-1, keepdims=True) + 1e-05)
    out[...] = (floats * scale).astype(jnp.bfloat16)


def norm_rows(values):
    rows, width = values.shape
    tile = NORM_TILE if rows % NORM_TILE == 0 else rows
    block = pl.BlockSpec((tile, width), lambda i: (i, 0))
    return pl.pallas_call(
        norm_kernel,
        grid=(rows // tile,),
        in_specs=[block],
        out_specs=block,
        out_shape=jax.ShapeDtypeStruct(values.shape, jnp.bfloat16),
        cost_estimate=pl.CostEstimate(
            flops=8 * rows * width, bytes_accessed=4 * rows * width, transcendentals=rows
        ),
        compiler_params=pltpu.CompilerParams(vmem_limit_bytes=NORM_VMEM_BYTES),
    )(values)


def cast_kernel(values, out):
    out[...] = values[...].astype(jnp.bfloat16)


def cast_columns(values, unit, cols):
    rows = values.shape[0]
    tile = min(rows, CAST_TILE)
    return pl.pallas_call(
        cast_kernel,
        grid=(rows // tile,),
        in_specs=[pl.BlockSpec((tile, cols), lambda i: (i, unit))],
        out_specs=pl.BlockSpec((tile, cols), lambda i: (i, 0)),
        out_shape=jax.ShapeDtypeStruct((rows, cols), jnp.bfloat16),
        cost_estimate=pl.CostEstimate(
            flops=rows * cols, bytes_accessed=6 * rows * cols, transcendentals=0
        ),
        compiler_params=pltpu.CompilerParams(vmem_limit_bytes=VMEM_BYTES),
    )(values)


def head_gradients(rows, keys, cotan, out):
    for h in range(keys.shape[1] // HEAD_DIM):
        spot = pl.ds(h * HEAD_DIM, HEAD_DIM)
        head = keys[:, h * HEAD_DIM : (h + 1) * HEAD_DIM]
        inverse = lax.rsqrt(jnp.mean(head * head, axis=-1, keepdims=True) + 1e-06)
        unit = head * inverse
        upstream = cotan[:, spot].astype(jnp.float32) / rows
        grads = inverse * (upstream - unit * jnp.mean(upstream * unit, axis=-1, keepdims=True))
        out[:, spot] = grads.astype(jnp.bfloat16)


def key_kernel(rows, keys, cotan, out):
    head_gradients(rows, keys[...], cotan, out)


def last_key_kernel(rows, spot, keys, top, low, normed, cotan, out):
    half = top.shape[0]
    total = keys[...]
    for part, piece in enumerate((top, low)):
        features = normed[:, pl.ds(part * half, half)]
        total = total + jnp.dot(features, piece[...], preferred_element_type=jnp.float32)
    head_gradients(rows, total, cotan, out)


def key_gradient(keys, cotan, unit, rows, rest=None):
    count, cols = keys.shape
    tile = KEY_TILE if count % KEY_TILE == 0 else count
    block = pl.BlockSpec((tile, cols), lambda i, *_: (i, 0))
    cotan_block = pl.BlockSpec((tile, cols), lambda i, *_: (i, unit))
    options = dict(
        out_shape=jax.ShapeDtypeStruct(keys.shape, jnp.bfloat16),
        compiler_params=pltpu.CompilerParams(vmem_limit_bytes=VMEM_BYTES),
    )
    if rest is None:
        return pl.pallas_call(
            functools.partial(key_kernel, rows),
            grid=(count // tile,),
            in_specs=[block, cotan_block],
            out_specs=block,
            cost_estimate=pl.CostEstimate(
                flops=12 * count * cols, bytes_accessed=8 * count * cols, transcendentals=count
            ),
            **options,
        )(keys, cotan)
    top, low, normed, spot = rest
    half = top.shape[0]
    piece = pl.BlockSpec((half, cols), lambda i, *_: (0, 0))
    features = pl.BlockSpec((tile, 2 * half), lambda i, place: (i, place[0]))
    return pl.pallas_call(
        functools.partial(last_key_kernel, rows),
        grid_spec=pltpu.PrefetchScalarGridSpec(
            num_scalar_prefetch=1,
            grid=(count // tile,),
            in_specs=[block, piece, piece, features, cotan_block],
            out_specs=block,
        ),
        cost_estimate=pl.CostEstimate(
            flops=4 * count * cols * half,
            bytes_accessed=8 * count * cols + 4 * half * (cols + count),
            transcendentals=count,
        ),
        **options,
    )(spot, keys, top, low, normed, cotan)


def own_kernel(spot, normed, key_grad, out):
    out[...] = lax.dot_general(
        normed[...], key_grad[...], (((0,), (0,)), ((), ())), preferred_element_type=jnp.float32
    )


def own_term(normed, spot, key_grad, depth):
    count, cols = key_grad.shape
    tile = min(depth, OWN_TILE)
    tiles = depth // tile
    return pl.pallas_call(
        own_kernel,
        grid_spec=pltpu.PrefetchScalarGridSpec(
            num_scalar_prefetch=1,
            grid=(tiles,),
            in_specs=[
                pl.BlockSpec((count, tile), lambda i, place: (0, place[0] * tiles + i)),
                pl.BlockSpec((count, cols), lambda i, place: (0, 0)),
            ],
            out_specs=pl.BlockSpec((tile, cols), lambda i, place: (i, 0)),
        ),
        out_shape=jax.ShapeDtypeStruct((depth, cols), jnp.float32),
        cost_estimate=pl.CostEstimate(
            flops=2 * count * cols * depth,
            bytes_accessed=2 * count * depth + 2 * count * cols + 4 * depth * cols,
            transcendentals=0,
        ),
        compiler_params=pltpu.CompilerParams(vmem_limit_bytes=VMEM_BYTES),
    )(spot, normed, key_grad)


def adam_update(weight, first, second, grad, stamp):
    first = beta_one * first + (1.0 - beta_one) * grad
    second = beta_two * second + (1.0 - beta_two) * grad * grad
    fix_one = 1.0 - beta_one**stamp
    fix_two = 1.0 - beta_two**stamp
    ratio = first / fix_one / (jnp.sqrt(second / fix_two) + adam_eps)
    weight = weight - learn_rate * (ratio + weight_decay * weight)
    return (weight, first, second)


def first_kernel(stamp, unit, fragment, anchor, weight, first, second, grad, out_w, out_m, out_v, own):
    fresh, out_m[...], out_v[...] = adam_update(
        weight[...], first[...], second[...], grad[...], stamp
    )
    heads = fresh.shape[1] // HEAD_DIM
    for h in range(heads):
        head = fresh[:, h * HEAD_DIM : (h + 1) * HEAD_DIM]
        merged = mixing * head + (1.0 - mixing) * anchor[...]
        head = jnp.where(fragment[0] == unit * heads + h, merged, head)
        out_w[:, pl.ds(h * HEAD_DIM, HEAD_DIM)] = head
        own[:, pl.ds(h * HEAD_DIM, HEAD_DIM)] = head.astype(jnp.bfloat16)


def first_update(stamp, unit, fragment, anchor, weight, first, second, grad):
    rows, cols = grad.shape
    tile = min(rows, ADAM_TILE)
    block = pl.BlockSpec((tile, cols), lambda i: (i, 0))
    spot = pl.BlockSpec((tile, cols), lambda i: (i, unit))
    side = pl.BlockSpec((tile, HEAD_DIM), lambda i: (i, 0))
    return pl.pallas_call(
        functools.partial(first_kernel, stamp, unit),
        grid=(rows // tile,),
        in_specs=[pl.BlockSpec(memory_space=pltpu.SMEM), side, spot, spot, spot, block],
        out_specs=[block] * 4,
        out_shape=[jax.ShapeDtypeStruct((rows, cols), jnp.float32)] * 3
        + [jax.ShapeDtypeStruct((rows, cols), jnp.bfloat16)],
        cost_estimate=pl.CostEstimate(
            flops=24 * rows * cols, bytes_accessed=32 * rows * cols, transcendentals=rows * cols
        ),
        compiler_params=pltpu.CompilerParams(vmem_limit_bytes=VMEM_BYTES),
    )(fragment, anchor, weight, first, second, grad)


def last_kernel(stamp, weight, first, second, grad, *rest):
    for out, value in zip(
        rest[-3:], adam_update(weight[...], first[...], second[...], grad[...], stamp)
    ):
        out[...] = value


def last_update(stamp, unit, width, weight, first, second, grad, before):
    rows, cols = grad.shape
    tile = min(rows, ADAM_TILE)
    block = pl.BlockSpec((tile, cols), lambda i: (i, 0))
    spot = pl.BlockSpec((tile, cols), lambda i: (i, unit))
    return pl.pallas_call(
        functools.partial(last_kernel, stamp),
        grid=(rows // tile,),
        in_specs=[block] * 4 + [pl.BlockSpec(memory_space=pl.ANY)] * len(before),
        out_specs=[spot] * 3,
        out_shape=[jax.ShapeDtypeStruct((rows, width), jnp.float32)] * 3,
        input_output_aliases={4 + i: i for i in range(len(before))},
        cost_estimate=pl.CostEstimate(
            flops=20 * rows * cols, bytes_accessed=28 * rows * cols, transcendentals=rows * cols
        ),
        compiler_params=pltpu.CompilerParams(vmem_limit_bytes=VMEM_BYTES),
    )(weight, first, second, grad, *before)


def by_rows(array):
    return with_layout_constraint(array, Layout(major_to_minor=(0, 1)))


def sum_replicas(rows):
    count = lax.axis_size("replica")
    if count & (count - 1):
        return lax.psum(rows, "replica")
    step = 1
    while step < count:
        swaps = [(r, r ^ step) for r in range(count)]
        rows = rows + lax.ppermute(rows, "replica", swaps)
        step *= 2
    return rows


def outer_update(total, anchor, momentum):
    average = total / lax.axis_size("replica")
    fresh_mom = outer_momentum * momentum + average
    fresh_anchor = anchor - outer_rate * (outer_momentum * fresh_mom + average)
    return (fresh_anchor, fresh_mom)


def ring_of(count):
    half = count // 2
    return [2 * p if p < half else 2 * (count - 1 - p) + 1 for p in range(count)]


def on_device(tokens, cotangent, params, adam_m, adam_v, anchor, momentum, delta, fragment):
    count = lax.axis_size("fsdp")
    half = count // 2
    ringed = count % 2 == 0 and count <= RING_MOST
    ring = ring_of(count)
    onward = [(ring[p], ring[(p + 1) % count]) for p in range(count)]
    back = [(ring[(p + 1) % count], ring[p]) for p in range(count)]
    index = lax.axis_index("fsdp")
    place = jnp.where(index % 2 == 0, index // 2, count - 1 - index // 2)

    cotan = cotangent[0]
    depth, width = params.shape[1:]
    unit_cols = UNIT_HEADS * HEAD_DIM
    units = width // unit_cols
    rows = tokens.shape[1] * count

    owns = [cast_columns(params[0], u, unit_cols) for u in range(units)]

    normed = norm_rows(tokens[0])
    normed_at, places = [], []
    for k in range(count if ringed else 0):
        spot = (place + k) % count
        owner = jnp.where(spot < half, 2 * spot, 2 * (count - 1 - spot) + 1)
        normed_at.append(lax.dynamic_slice_in_dim(normed, owner * depth, depth, 1))
        places.append(owner.astype(jnp.int32).reshape(1))

    def gather_whole(current):
        every = lax.all_gather(current, "fsdp", axis=0, tiled=True)
        return (jnp.dot(normed, every, preferred_element_type=jnp.float32), None), every

    def scatter_whole(key_grad, last=False):
        part = lax.dot_general(
            normed, key_grad, (((0,), (0,)), ((), ())), preferred_element_type=jnp.float32
        )
        return lax.psum_scatter(part, "fsdp", scatter_dimension=0, tiled=True)

    def add_rows(k, piece):
        return jnp.dot(normed_at[k], piece, preferred_element_type=jnp.float32)

    def gather_keys(own):
        keys = add_rows(0, own)
        left, right = own, own
        for k in range(1, half):
            left = lax.ppermute(left, "fsdp", onward)
            right = lax.ppermute(right, "fsdp", back)
            keys = keys + add_rows(count - k, left) + add_rows(k, right)
            if k == 2:
                second = (left, right)
        top = lax.ppermute(left[: depth // 2], "fsdp", onward)
        low = lax.ppermute(right[depth // 2 :], "fsdp", back)
        return (keys, (top, low, normed, places[half])), second

    def grad_part(k, key_grad):
        return lax.dot_general(
            normed_at[k], key_grad, (((0,), (0,)), ((), ())), preferred_element_type=jnp.float32
        )

    def scatter_grad(key_grad, last=False):
        far = by_rows((SCALE * grad_part(half, key_grad)).astype(SENT))
        right = lax.ppermute(far[: depth // 2], "fsdp", onward)
        left = lax.ppermute(far[depth // 2 :], "fsdp", back)
        key_grad, right, left = lax.optimization_barrier((key_grad, right, left))
        zeros = jnp.zeros_like(right)
        right = jnp.concatenate([right, zeros], 0)
        left = jnp.concatenate([zeros, left], 0)
        for k in range(half - 1, 0, -1):
            right = SCALE * grad_part(k, key_grad) + right.astype(jnp.float32)
            left = SCALE * grad_part(count - k, key_grad) + left.astype(jnp.float32)
            right, left = by_rows(right.astype(SENT)), by_rows(left.astype(SENT))
            right = lax.ppermute(right, "fsdp", onward)
            left = lax.ppermute(left, "fsdp", back)
        own = own_term(normed, places[0], key_grad, depth) if last else grad_part(0, key_grad)
        return own + (right.astype(jnp.float32) + left.astype(jnp.float32)) / SCALE

    gather, scatter = (gather_keys, scatter_grad) if ringed else (gather_whole, scatter_whole)
    states, key_grads = [None] * units, [None] * units
    for u in range(units):
        (keys, rest), arrived = gather(owns[u])
        if u == 0:
            rows_of_delta, _ = lax.optimization_barrier((delta[0], arrived))
            new_anchor, new_momentum = outer_update(sum_replicas(rows_of_delta), anchor, momentum)
        key_grads[u] = key_gradient(keys, cotan, u, rows, rest)
    for u in range(units):
        *states[u], owns[u] = first_update(
            1, u, fragment, new_anchor, params[0], adam_m[0], adam_v[0], scatter(key_grads[u])
        )
    results = ()
    for u in range(units):
        keys, rest = gather(owns[u])[0]
        grad = scatter(key_gradient(keys, cotan, u, rows, rest), u == units - 1)
        results = last_update(2, u, width, *states[u], grad, results)

    return (*(out[None] for out in results), new_anchor, new_momentum)


def solution(mesh):
    return jax.shard_map(
        on_device,
        mesh=mesh,
        in_specs=(
            P("replica", "fsdp", None),
            P("replica", "fsdp", None),
            P("replica", "fsdp", None),
            P("replica", "fsdp", None),
            P("replica", "fsdp", None),
            P("fsdp", None),
            P("fsdp", None),
            P("replica", "fsdp", None),
            P(),
        ),
        out_specs=(
            P("replica", "fsdp", None),
            P("replica", "fsdp", None),
            P("replica", "fsdp", None),
            P("fsdp", None),
            P("fsdp", None),
        ),
        check_vma=False,
    )
```

```python
import functools

import jax
import jax.numpy as jnp
from jax import lax
from jax.experimental import pallas as pl
from jax.experimental.layout import Layout, with_layout_constraint
from jax.experimental.pallas import tpu as pltpu
from jax.sharding import PartitionSpec as P

HEAD_DIM = 128
KV_HEADS = 4
INNER_STEPS = 2
UNIT_HEADS = 2
RING_MOST = 8
NORM_TILE = 128
CAST_TILE = 512
KEY_TILE = 256
OWN_TILE = 256
ADAM_TILE = 512
VMEM_BYTES = 14 * 2**20
NORM_VMEM_BYTES = 36 * 2**20
SENT = jnp.float16
SCALE = 1.0 / 128


beta_one = 0.9
beta_two = 0.95
adam_eps = 1e-08
learn_rate = 0.002
weight_decay = 0.1
outer_rate = 0.7
outer_momentum = 0.9
mixing = 0.5


def norm_kernel(values, out):
    floats = values[...].astype(jnp.float32)
    scale = lax.rsqrt(jnp.mean(floats * floats, axis=-1, keepdims=True) + 1e-05)
    out[...] = (floats * scale).astype(jnp.bfloat16)


def norm_rows(values):
    rows, width = values.shape
    tile = NORM_TILE if rows % NORM_TILE == 0 else rows
    block = pl.BlockSpec((tile, width), lambda i: (i, 0))
    return pl.pallas_call(
        norm_kernel,
        grid=(rows // tile,),
        in_specs=[block],
        out_specs=block,
        out_shape=jax.ShapeDtypeStruct(values.shape, jnp.bfloat16),
        cost_estimate=pl.CostEstimate(
            flops=8 * rows * width, bytes_accessed=4 * rows * width, transcendentals=rows
        ),
        compiler_params=pltpu.CompilerParams(vmem_limit_bytes=NORM_VMEM_BYTES),
    )(values)


def cast_kernel(values, out):
    out[...] = values[...].astype(jnp.bfloat16)


def cast_columns(values, unit, cols):
    rows = values.shape[0]
    tile = min(rows, CAST_TILE)
    return pl.pallas_call(
        cast_kernel,
        grid=(rows // tile,),
        in_specs=[pl.BlockSpec((tile, cols), lambda i: (i, unit))],
        out_specs=pl.BlockSpec((tile, cols), lambda i: (i, 0)),
        out_shape=jax.ShapeDtypeStruct((rows, cols), jnp.bfloat16),
        cost_estimate=pl.CostEstimate(
            flops=rows * cols, bytes_accessed=6 * rows * cols, transcendentals=0
        ),
        compiler_params=pltpu.CompilerParams(vmem_limit_bytes=VMEM_BYTES),
    )(values)


def key_kernel(rows, keys, cotan, out):
    for h in range(keys.shape[1] // HEAD_DIM):
        spot = pl.ds(h * HEAD_DIM, HEAD_DIM)
        head = keys[:, spot]
        inverse = lax.rsqrt(jnp.mean(head * head, axis=-1, keepdims=True) + 1e-06)
        unit = head * inverse
        upstream = cotan[:, spot].astype(jnp.float32) / rows
        grads = inverse * (upstream - unit * jnp.mean(upstream * unit, axis=-1, keepdims=True))
        out[:, spot] = grads.astype(jnp.bfloat16)


def key_gradient(keys, cotan, unit, rows):
    count, cols = keys.shape
    tile = KEY_TILE if count % KEY_TILE == 0 else count
    block = pl.BlockSpec((tile, cols), lambda i: (i, 0))
    return pl.pallas_call(
        functools.partial(key_kernel, rows),
        grid=(count // tile,),
        in_specs=[block, pl.BlockSpec((tile, cols), lambda i: (i, unit))],
        out_specs=block,
        out_shape=jax.ShapeDtypeStruct(keys.shape, jnp.bfloat16),
        cost_estimate=pl.CostEstimate(
            flops=12 * count * cols, bytes_accessed=8 * count * cols, transcendentals=count
        ),
        compiler_params=pltpu.CompilerParams(vmem_limit_bytes=VMEM_BYTES),
    )(keys, cotan)


def own_kernel(spot, normed, key_grad, out):
    out[...] = lax.dot_general(
        normed[...], key_grad[...], (((0,), (0,)), ((), ())), preferred_element_type=jnp.float32
    )


def own_term(normed, spot, key_grad, depth):
    count, cols = key_grad.shape
    tile = min(depth, OWN_TILE)
    tiles = depth // tile
    return pl.pallas_call(
        own_kernel,
        grid_spec=pltpu.PrefetchScalarGridSpec(
            num_scalar_prefetch=1,
            grid=(tiles,),
            in_specs=[
                pl.BlockSpec((count, tile), lambda i, place: (0, place[0] * tiles + i)),
                pl.BlockSpec((count, cols), lambda i, place: (0, 0)),
            ],
            out_specs=pl.BlockSpec((tile, cols), lambda i, place: (i, 0)),
        ),
        out_shape=jax.ShapeDtypeStruct((depth, cols), jnp.float32),
        cost_estimate=pl.CostEstimate(
            flops=2 * count * cols * depth,
            bytes_accessed=2 * count * depth + 2 * count * cols + 4 * depth * cols,
            transcendentals=0,
        ),
        compiler_params=pltpu.CompilerParams(vmem_limit_bytes=VMEM_BYTES),
    )(spot, normed, key_grad)


def adam_update(weight, first, second, grad, stamp):
    first = beta_one * first + (1.0 - beta_one) * grad
    second = beta_two * second + (1.0 - beta_two) * grad * grad
    fix_one = 1.0 - beta_one**stamp
    fix_two = 1.0 - beta_two**stamp
    ratio = first / fix_one / (jnp.sqrt(second / fix_two) + adam_eps)
    weight = weight - learn_rate * (ratio + weight_decay * weight)
    return (weight, first, second)


def first_kernel(stamp, unit, fragment, anchor, weight, first, second, grad, out_w, out_m, out_v, own):
    fresh, out_m[...], out_v[...] = adam_update(
        weight[...], first[...], second[...], grad[...], stamp
    )
    heads = fresh.shape[1] // HEAD_DIM
    for h in range(heads):
        head = fresh[:, h * HEAD_DIM : (h + 1) * HEAD_DIM]
        merged = mixing * head + (1.0 - mixing) * anchor[...]
        head = jnp.where(fragment[0] == unit * heads + h, merged, head)
        out_w[:, pl.ds(h * HEAD_DIM, HEAD_DIM)] = head
        own[:, pl.ds(h * HEAD_DIM, HEAD_DIM)] = head.astype(jnp.bfloat16)


def first_update(stamp, unit, fragment, anchor, weight, first, second, grad):
    rows, cols = grad.shape
    tile = min(rows, ADAM_TILE)
    block = pl.BlockSpec((tile, cols), lambda i: (i, 0))
    spot = pl.BlockSpec((tile, cols), lambda i: (i, unit))
    side = pl.BlockSpec((tile, HEAD_DIM), lambda i: (i, 0))
    return pl.pallas_call(
        functools.partial(first_kernel, stamp, unit),
        grid=(rows // tile,),
        in_specs=[pl.BlockSpec(memory_space=pltpu.SMEM), side, spot, spot, spot, block],
        out_specs=[block] * 4,
        out_shape=[jax.ShapeDtypeStruct((rows, cols), jnp.float32)] * 3
        + [jax.ShapeDtypeStruct((rows, cols), jnp.bfloat16)],
        cost_estimate=pl.CostEstimate(
            flops=24 * rows * cols, bytes_accessed=32 * rows * cols, transcendentals=rows * cols
        ),
        compiler_params=pltpu.CompilerParams(vmem_limit_bytes=VMEM_BYTES),
    )(fragment, anchor, weight, first, second, grad)


def last_kernel(stamp, weight, first, second, grad, *rest):
    for out, value in zip(
        rest[-3:], adam_update(weight[...], first[...], second[...], grad[...], stamp)
    ):
        out[...] = value


def last_update(stamp, unit, width, weight, first, second, grad, before):
    rows, cols = grad.shape
    tile = min(rows, ADAM_TILE)
    block = pl.BlockSpec((tile, cols), lambda i: (i, 0))
    spot = pl.BlockSpec((tile, cols), lambda i: (i, unit))
    return pl.pallas_call(
        functools.partial(last_kernel, stamp),
        grid=(rows // tile,),
        in_specs=[block] * 4 + [pl.BlockSpec(memory_space=pl.ANY)] * len(before),
        out_specs=[spot] * 3,
        out_shape=[jax.ShapeDtypeStruct((rows, width), jnp.float32)] * 3,
        input_output_aliases={4 + i: i for i in range(len(before))},
        cost_estimate=pl.CostEstimate(
            flops=20 * rows * cols, bytes_accessed=28 * rows * cols, transcendentals=rows * cols
        ),
        compiler_params=pltpu.CompilerParams(vmem_limit_bytes=VMEM_BYTES),
    )(weight, first, second, grad, *before)


def by_rows(array):
    return with_layout_constraint(array, Layout(major_to_minor=(0, 1)))


def sum_replicas(rows):
    count = lax.axis_size("replica")
    if count & (count - 1):
        return lax.psum(rows, "replica")
    step = 1
    while step < count:
        swaps = [(r, r ^ step) for r in range(count)]
        rows = rows + lax.ppermute(rows, "replica", swaps)
        step *= 2
    return rows


def outer_update(total, anchor, momentum):
    average = total / lax.axis_size("replica")
    fresh_mom = outer_momentum * momentum + average
    fresh_anchor = anchor - outer_rate * (outer_momentum * fresh_mom + average)
    return (fresh_anchor, fresh_mom)


def ring_of(count):
    half = count // 2
    return [2 * p if p < half else 2 * (count - 1 - p) + 1 for p in range(count)]


def on_device(tokens, cotangent, params, adam_m, adam_v, anchor, momentum, delta, fragment):
    count = lax.axis_size("fsdp")
    half = count // 2
    ringed = count % 2 == 0 and count <= RING_MOST
    ring = ring_of(count)
    onward = [(ring[p], ring[(p + 1) % count]) for p in range(count)]
    back = [(ring[(p + 1) % count], ring[p]) for p in range(count)]
    index = lax.axis_index("fsdp")
    place = jnp.where(index % 2 == 0, index // 2, count - 1 - index // 2)

    cotan = cotangent[0]
    depth, width = params.shape[1:]
    unit_cols = UNIT_HEADS * HEAD_DIM
    units = width // unit_cols
    rows = tokens.shape[1] * count

    owns = [cast_columns(params[0], u, unit_cols) for u in range(units)]

    normed = norm_rows(tokens[0])
    normed_at, places = [], []
    for k in range(count if ringed else 0):
        spot = (place + k) % count
        owner = jnp.where(spot < half, 2 * spot, 2 * (count - 1 - spot) + 1)
        normed_at.append(lax.dynamic_slice_in_dim(normed, owner * depth, depth, 1))
        places.append(owner.astype(jnp.int32).reshape(1))

    def gather_whole(current):
        every = lax.all_gather(current, "fsdp", axis=0, tiled=True)
        return jnp.dot(normed, every, preferred_element_type=jnp.float32), every

    def scatter_whole(key_grad, last=False):
        part = lax.dot_general(
            normed, key_grad, (((0,), (0,)), ((), ())), preferred_element_type=jnp.float32
        )
        return lax.psum_scatter(part, "fsdp", scatter_dimension=0, tiled=True)

    def add_rows(k, piece):
        return jnp.dot(normed_at[k], piece, preferred_element_type=jnp.float32)

    def gather_keys(own):
        keys = add_rows(0, own)
        left, right = own, own
        for k in range(1, half):
            left = lax.ppermute(left, "fsdp", onward)
            right = lax.ppermute(right, "fsdp", back)
            keys = keys + add_rows(count - k, left) + add_rows(k, right)
            if k == 2:
                second = (left, right)
        top = lax.ppermute(left[: depth // 2], "fsdp", onward)
        low = lax.ppermute(right[depth // 2 :], "fsdp", back)
        return keys + add_rows(half, jnp.concatenate([top, low], 0)), second

    def grad_part(k, key_grad):
        return lax.dot_general(
            normed_at[k], key_grad, (((0,), (0,)), ((), ())), preferred_element_type=jnp.float32
        )

    def scatter_grad(key_grad, last=False):
        far = by_rows((SCALE * grad_part(half, key_grad)).astype(SENT))
        right = lax.ppermute(far[: depth // 2], "fsdp", onward)
        left = lax.ppermute(far[depth // 2 :], "fsdp", back)
        with_right, right = lax.optimization_barrier((key_grad, right))
        with_left, left = lax.optimization_barrier((key_grad, left))
        zeros = jnp.zeros_like(right)
        right = jnp.concatenate([right, zeros], 0)
        left = jnp.concatenate([zeros, left], 0)
        for k in range(half - 1, 0, -1):
            right = SCALE * grad_part(k, with_right) + right.astype(jnp.float32)
            left = SCALE * grad_part(count - k, with_left) + left.astype(jnp.float32)
            right, left = by_rows(right.astype(SENT)), by_rows(left.astype(SENT))
            right = lax.ppermute(right, "fsdp", onward)
            left = lax.ppermute(left, "fsdp", back)
        own = own_term(normed, places[0], with_left, depth) if last else grad_part(0, with_left)
        return own + (right.astype(jnp.float32) + left.astype(jnp.float32)) / SCALE

    gather, scatter = (gather_keys, scatter_grad) if ringed else (gather_whole, scatter_whole)
    states, key_grads = [None] * units, [None] * units
    for u in range(units):
        keys, arrived = gather(owns[u])
        if u == 0:
            rows_of_delta, _ = lax.optimization_barrier((delta[0], arrived))
            new_anchor, new_momentum = outer_update(sum_replicas(rows_of_delta), anchor, momentum)
        key_grads[u] = key_gradient(keys, cotan, u, rows)
    for u in range(units):
        *states[u], owns[u] = first_update(
            1, u, fragment, new_anchor, params[0], adam_m[0], adam_v[0], scatter(key_grads[u])
        )
    results = ()
    for u in range(units):
        grad = scatter(key_gradient(gather(owns[u])[0], cotan, u, rows), u == units - 1)
        results = last_update(2, u, width, *states[u], grad, results)

    return (*(out[None] for out in results), new_anchor, new_momentum)


def solution(mesh):
    return jax.shard_map(
        on_device,
        mesh=mesh,
        in_specs=(
            P("replica", "fsdp", None),
            P("replica", "fsdp", None),
            P("replica", "fsdp", None),
            P("replica", "fsdp", None),
            P("replica", "fsdp", None),
            P("fsdp", None),
            P("fsdp", None),
            P("replica", "fsdp", None),
            P(),
        ),
        out_specs=(
            P("replica", "fsdp", None),
            P("replica", "fsdp", None),
            P("replica", "fsdp", None),
            P("fsdp", None),
            P("fsdp", None),
        ),
        check_vma=False,
    )
```

```python
import functools

import jax
import jax.numpy as jnp
from jax import lax
from jax.experimental import pallas as pl
from jax.experimental.layout import Layout, with_layout_constraint
from jax.experimental.pallas import tpu as pltpu
from jax.sharding import PartitionSpec as P

HEAD_DIM = 128
KV_HEADS = 4
INNER_STEPS = 2
UNIT_HEADS = 2
RING_SIZE = 8
NORM_TILE = 128
CAST_TILE = 512
KEY_TILE = 256
OWN_TILE = 256
ADAM_TILE = 512
VMEM_BYTES = 14 * 2**20
NORM_VMEM_BYTES = 36 * 2**20
SENT = jnp.float16
SCALE = 1.0 / 128


beta_one = 0.9
beta_two = 0.95
adam_eps = 1e-08
learn_rate = 0.002
weight_decay = 0.1
outer_rate = 0.7
outer_momentum = 0.9
mixing = 0.5


def norm_kernel(values, out):
    floats = values[...].astype(jnp.float32)
    scale = lax.rsqrt(jnp.mean(floats * floats, axis=-1, keepdims=True) + 1e-05)
    out[...] = (floats * scale).astype(jnp.bfloat16)


def norm_rows(values):
    rows, width = values.shape
    tile = NORM_TILE if rows % NORM_TILE == 0 else rows
    block = pl.BlockSpec((tile, width), lambda i: (i, 0))
    return pl.pallas_call(
        norm_kernel,
        grid=(rows // tile,),
        in_specs=[block],
        out_specs=block,
        out_shape=jax.ShapeDtypeStruct(values.shape, jnp.bfloat16),
        cost_estimate=pl.CostEstimate(
            flops=8 * rows * width, bytes_accessed=4 * rows * width, transcendentals=rows
        ),
        compiler_params=pltpu.CompilerParams(vmem_limit_bytes=NORM_VMEM_BYTES),
    )(values)


def cast_kernel(values, out):
    out[...] = values[...].astype(jnp.bfloat16)


def cast_columns(values, unit, cols):
    rows = values.shape[0]
    tile = min(rows, CAST_TILE)
    return pl.pallas_call(
        cast_kernel,
        grid=(rows // tile,),
        in_specs=[pl.BlockSpec((tile, cols), lambda i: (i, unit))],
        out_specs=pl.BlockSpec((tile, cols), lambda i: (i, 0)),
        out_shape=jax.ShapeDtypeStruct((rows, cols), jnp.bfloat16),
        cost_estimate=pl.CostEstimate(
            flops=rows * cols, bytes_accessed=6 * rows * cols, transcendentals=0
        ),
        compiler_params=pltpu.CompilerParams(vmem_limit_bytes=VMEM_BYTES),
    )(values)


def key_kernel(rows, keys, cotan, out):
    for h in range(keys.shape[1] // HEAD_DIM):
        spot = pl.ds(h * HEAD_DIM, HEAD_DIM)
        head = keys[:, spot]
        inverse = lax.rsqrt(jnp.mean(head * head, axis=-1, keepdims=True) + 1e-06)
        unit = head * inverse
        upstream = cotan[:, spot].astype(jnp.float32) / rows
        grads = inverse * (upstream - unit * jnp.mean(upstream * unit, axis=-1, keepdims=True))
        out[:, spot] = grads.astype(jnp.bfloat16)


def key_gradient(keys, cotan, unit, rows):
    count, cols = keys.shape
    tile = KEY_TILE if count % KEY_TILE == 0 else count
    block = pl.BlockSpec((tile, cols), lambda i: (i, 0))
    return pl.pallas_call(
        functools.partial(key_kernel, rows),
        grid=(count // tile,),
        in_specs=[block, pl.BlockSpec((tile, cols), lambda i: (i, unit))],
        out_specs=block,
        out_shape=jax.ShapeDtypeStruct(keys.shape, jnp.bfloat16),
        cost_estimate=pl.CostEstimate(
            flops=12 * count * cols, bytes_accessed=8 * count * cols, transcendentals=count
        ),
        compiler_params=pltpu.CompilerParams(vmem_limit_bytes=VMEM_BYTES),
    )(keys, cotan)


def own_kernel(spot, normed, key_grad, out):
    out[...] = lax.dot_general(
        normed[...], key_grad[...], (((0,), (0,)), ((), ())), preferred_element_type=jnp.float32
    )


def own_term(normed, spot, key_grad, depth):
    count, cols = key_grad.shape
    tile = min(depth, OWN_TILE)
    tiles = depth // tile
    return pl.pallas_call(
        own_kernel,
        grid_spec=pltpu.PrefetchScalarGridSpec(
            num_scalar_prefetch=1,
            grid=(tiles,),
            in_specs=[
                pl.BlockSpec((count, tile), lambda i, place: (0, place[0] * tiles + i)),
                pl.BlockSpec((count, cols), lambda i, place: (0, 0)),
            ],
            out_specs=pl.BlockSpec((tile, cols), lambda i, place: (i, 0)),
        ),
        out_shape=jax.ShapeDtypeStruct((depth, cols), jnp.float32),
        cost_estimate=pl.CostEstimate(
            flops=2 * count * cols * depth,
            bytes_accessed=2 * count * depth + 2 * count * cols + 4 * depth * cols,
            transcendentals=0,
        ),
        compiler_params=pltpu.CompilerParams(vmem_limit_bytes=VMEM_BYTES),
    )(spot, normed, key_grad)


def adam_update(weight, first, second, grad, stamp):
    first = beta_one * first + (1.0 - beta_one) * grad
    second = beta_two * second + (1.0 - beta_two) * grad * grad
    fix_one = 1.0 - beta_one**stamp
    fix_two = 1.0 - beta_two**stamp
    ratio = first / fix_one / (jnp.sqrt(second / fix_two) + adam_eps)
    weight = weight - learn_rate * (ratio + weight_decay * weight)
    return (weight, first, second)


def first_kernel(stamp, unit, fragment, anchor, weight, first, second, grad, out_w, out_m, out_v, own):
    fresh, out_m[...], out_v[...] = adam_update(
        weight[...], first[...], second[...], grad[...], stamp
    )
    heads = fresh.shape[1] // HEAD_DIM
    for h in range(heads):
        head = fresh[:, h * HEAD_DIM : (h + 1) * HEAD_DIM]
        merged = mixing * head + (1.0 - mixing) * anchor[...]
        head = jnp.where(fragment[0] == unit * heads + h, merged, head)
        out_w[:, pl.ds(h * HEAD_DIM, HEAD_DIM)] = head
        own[:, pl.ds(h * HEAD_DIM, HEAD_DIM)] = head.astype(jnp.bfloat16)


def first_update(stamp, unit, fragment, anchor, weight, first, second, grad):
    rows, cols = grad.shape
    tile = min(rows, ADAM_TILE)
    block = pl.BlockSpec((tile, cols), lambda i: (i, 0))
    spot = pl.BlockSpec((tile, cols), lambda i: (i, unit))
    side = pl.BlockSpec((tile, HEAD_DIM), lambda i: (i, 0))
    return pl.pallas_call(
        functools.partial(first_kernel, stamp, unit),
        grid=(rows // tile,),
        in_specs=[pl.BlockSpec(memory_space=pltpu.SMEM), side, spot, spot, spot, block],
        out_specs=[block] * 4,
        out_shape=[jax.ShapeDtypeStruct((rows, cols), jnp.float32)] * 3
        + [jax.ShapeDtypeStruct((rows, cols), jnp.bfloat16)],
        cost_estimate=pl.CostEstimate(
            flops=24 * rows * cols, bytes_accessed=32 * rows * cols, transcendentals=rows * cols
        ),
        compiler_params=pltpu.CompilerParams(vmem_limit_bytes=VMEM_BYTES),
    )(fragment, anchor, weight, first, second, grad)


def last_kernel(stamp, weight, first, second, grad, *rest):
    for out, value in zip(
        rest[-3:], adam_update(weight[...], first[...], second[...], grad[...], stamp)
    ):
        out[...] = value


def last_update(stamp, unit, width, weight, first, second, grad, before):
    rows, cols = grad.shape
    tile = min(rows, ADAM_TILE)
    block = pl.BlockSpec((tile, cols), lambda i: (i, 0))
    spot = pl.BlockSpec((tile, cols), lambda i: (i, unit))
    return pl.pallas_call(
        functools.partial(last_kernel, stamp),
        grid=(rows // tile,),
        in_specs=[block] * 4 + [pl.BlockSpec(memory_space=pl.ANY)] * len(before),
        out_specs=[spot] * 3,
        out_shape=[jax.ShapeDtypeStruct((rows, width), jnp.float32)] * 3,
        input_output_aliases={4 + i: i for i in range(len(before))},
        cost_estimate=pl.CostEstimate(
            flops=20 * rows * cols, bytes_accessed=28 * rows * cols, transcendentals=rows * cols
        ),
        compiler_params=pltpu.CompilerParams(vmem_limit_bytes=VMEM_BYTES),
    )(weight, first, second, grad, *before)


def by_rows(array):
    return with_layout_constraint(array, Layout(major_to_minor=(0, 1)))


def sum_replicas(rows):
    count = lax.axis_size("replica")
    if count & (count - 1):
        return lax.psum(rows, "replica")
    step = 1
    while step < count:
        swaps = [(r, r ^ step) for r in range(count)]
        rows = rows + lax.ppermute(rows, "replica", swaps)
        step *= 2
    return rows


def outer_update(total, anchor, momentum):
    average = total / lax.axis_size("replica")
    fresh_mom = outer_momentum * momentum + average
    fresh_anchor = anchor - outer_rate * (outer_momentum * fresh_mom + average)
    return (fresh_anchor, fresh_mom)


def ring_of(count):
    half = count // 2
    return [2 * p if p < half else 2 * (count - 1 - p) + 1 for p in range(count)]


def on_device(tokens, cotangent, params, adam_m, adam_v, anchor, momentum, delta, fragment):
    count = lax.axis_size("fsdp")
    half = count // 2
    ringed = count == RING_SIZE
    ring = ring_of(count)
    onward = [(ring[p], ring[(p + 1) % count]) for p in range(count)]
    back = [(ring[(p + 1) % count], ring[p]) for p in range(count)]
    across = [(ring[p], ring[count - 1 - p]) for p in (1, 2, 5, 6)]
    to_end = [(ring[p], ring[q]) for p, q in ((1, 0), (2, 3), (5, 4), (6, 7))]
    from_end = [(q, p) for p, q in to_end]
    end_pair = [(ring[p], ring[count - 1 - p]) for p in (0, 3, 4, 7)]
    index = lax.axis_index("fsdp")
    place = jnp.where(index % 2 == 0, index // 2, count - 1 - index // 2)

    cotan = cotangent[0]
    depth, width = params.shape[1:]
    unit_cols = UNIT_HEADS * HEAD_DIM
    units = width // unit_cols
    rows = tokens.shape[1] * count

    cut = depth * 5 // 8
    low_side = place % 4 < 2

    owns = [cast_columns(params[0], u, unit_cols) for u in range(units)]

    normed = norm_rows(tokens[0])
    normed_at, places = [], []
    for k in range(count if ringed else 0):
        spot = (place + k) % count
        owner = jnp.where(spot < half, 2 * spot, 2 * (count - 1 - spot) + 1)
        normed_at.append(lax.dynamic_slice_in_dim(normed, owner * depth, depth, 1))
        places.append(owner.astype(jnp.int32).reshape(1))

    def gather_whole(current):
        every = lax.all_gather(current, "fsdp", axis=0, tiled=True)
        return jnp.dot(normed, every, preferred_element_type=jnp.float32), every

    def scatter_whole(key_grad, last=False):
        part = lax.dot_general(
            normed, key_grad, (((0,), (0,)), ((), ())), preferred_element_type=jnp.float32
        )
        return lax.psum_scatter(part, "fsdp", scatter_dimension=0, tiled=True)

    def add_rows(k, piece):
        return jnp.dot(normed_at[k], piece, preferred_element_type=jnp.float32)

    def gather_keys(own):
        keys = add_rows(0, own)
        left, right = own, own
        for k in range(1, half):
            left = lax.ppermute(left, "fsdp", onward)
            right = lax.ppermute(right, "fsdp", back)
            keys = keys + add_rows(count - k, left) + add_rows(k, right)
            if k == 1:
                far_across = lax.ppermute(jnp.where(low_side, right, left), "fsdp", across)
            if k == 2:
                second = (left, right)
        near = jnp.where(low_side, right, left)
        top = lax.ppermute(near[:cut], "fsdp", to_end)
        low = lax.ppermute(near[cut:], "fsdp", end_pair)
        farthest = jnp.concatenate([top, low], 0) + far_across
        return keys + add_rows(half, farthest), second

    def grad_part(k, key_grad):
        return lax.dot_general(
            normed_at[k], key_grad, (((0,), (0,)), ((), ())), preferred_element_type=jnp.float32
        )

    def scatter_grad(key_grad, last=False):
        far = by_rows((SCALE * grad_part(half, key_grad)).astype(SENT))
        top = lax.ppermute(far[:cut], "fsdp", from_end)
        low = lax.ppermute(far[cut:], "fsdp", end_pair)
        far_across = lax.ppermute(far, "fsdp", across)
        key_grad, top, low = lax.optimization_barrier((key_grad, top, low))
        arrived = jnp.concatenate([top, low], 0).astype(jnp.float32)
        right, left = jnp.where(low_side, arrived, 0.0), jnp.where(low_side, 0.0, arrived)
        for k in range(half - 1, 0, -1):
            right = SCALE * grad_part(k, key_grad) + right.astype(jnp.float32)
            left = SCALE * grad_part(count - k, key_grad) + left.astype(jnp.float32)
            if k == 1:
                right = right + jnp.where(low_side, far_across.astype(jnp.float32), 0.0)
                left = left + jnp.where(low_side, 0.0, far_across.astype(jnp.float32))
            right, left = by_rows(right.astype(SENT)), by_rows(left.astype(SENT))
            right = lax.ppermute(right, "fsdp", onward)
            left = lax.ppermute(left, "fsdp", back)
        own = own_term(normed, places[0], key_grad, depth) if last else grad_part(0, key_grad)
        return own + (right.astype(jnp.float32) + left.astype(jnp.float32)) / SCALE

    gather, scatter = (gather_keys, scatter_grad) if ringed else (gather_whole, scatter_whole)
    states, key_grads = [None] * units, [None] * units
    for u in range(units):
        keys, arrived = gather(owns[u])
        if u == 0:
            rows_of_delta, _ = lax.optimization_barrier((delta[0], arrived))
            new_anchor, new_momentum = outer_update(sum_replicas(rows_of_delta), anchor, momentum)
        key_grads[u] = key_gradient(keys, cotan, u, rows)
    for u in range(units):
        *states[u], owns[u] = first_update(
            1, u, fragment, new_anchor, params[0], adam_m[0], adam_v[0], scatter(key_grads[u])
        )
    results = ()
    for u in range(units):
        grad = scatter(key_gradient(gather(owns[u])[0], cotan, u, rows), u == units - 1)
        results = last_update(2, u, width, *states[u], grad, results)

    return (*(out[None] for out in results), new_anchor, new_momentum)


def solution(mesh):
    return jax.shard_map(
        on_device,
        mesh=mesh,
        in_specs=(
            P("replica", "fsdp", None),
            P("replica", "fsdp", None),
            P("replica", "fsdp", None),
            P("replica", "fsdp", None),
            P("replica", "fsdp", None),
            P("fsdp", None),
            P("fsdp", None),
            P("replica", "fsdp", None),
            P(),
        ),
        out_specs=(
            P("replica", "fsdp", None),
            P("replica", "fsdp", None),
            P("replica", "fsdp", None),
            P("fsdp", None),
            P("fsdp", None),
        ),
        check_vma=False,
    )
```

```python
import functools

import jax
import jax.numpy as jnp
from jax import lax
from jax.experimental import pallas as pl
from jax.experimental.layout import Layout, with_layout_constraint
from jax.experimental.pallas import tpu as pltpu
from jax.sharding import PartitionSpec as P

HEAD_DIM = 128
KV_HEADS = 4
INNER_STEPS = 2
UNIT_HEADS = 2
RING_MOST = 8
NORM_TILE = 128
CAST_TILE = 512
KEY_TILE = 384
OWN_TILE = 256
ADAM_TILE = 512
VMEM_BYTES = 14 * 2**20
NORM_VMEM_BYTES = 36 * 2**20
SENT = jnp.float16
SCALE = 1.0 / 128


beta_one = 0.9
beta_two = 0.95
adam_eps = 1e-08
learn_rate = 0.002
weight_decay = 0.1
outer_rate = 0.7
outer_momentum = 0.9
mixing = 0.5


def norm_kernel(values, out):
    floats = values[...].astype(jnp.float32)
    scale = lax.rsqrt(jnp.mean(floats * floats, axis=-1, keepdims=True) + 1e-05)
    out[...] = (floats * scale).astype(jnp.bfloat16)


def norm_rows(values):
    rows, width = values.shape
    tile = NORM_TILE if rows % NORM_TILE == 0 else rows
    block = pl.BlockSpec((tile, width), lambda i: (i, 0))
    return pl.pallas_call(
        norm_kernel,
        grid=(rows // tile,),
        in_specs=[block],
        out_specs=block,
        out_shape=jax.ShapeDtypeStruct(values.shape, jnp.bfloat16),
        cost_estimate=pl.CostEstimate(
            flops=8 * rows * width, bytes_accessed=4 * rows * width, transcendentals=rows
        ),
        compiler_params=pltpu.CompilerParams(vmem_limit_bytes=NORM_VMEM_BYTES),
    )(values)


def cast_kernel(values, out):
    out[...] = values[...].astype(jnp.bfloat16)


def cast_columns(values, unit, cols):
    rows = values.shape[0]
    tile = min(rows, CAST_TILE)
    return pl.pallas_call(
        cast_kernel,
        grid=(rows // tile,),
        in_specs=[pl.BlockSpec((tile, cols), lambda i: (i, unit))],
        out_specs=pl.BlockSpec((tile, cols), lambda i: (i, 0)),
        out_shape=jax.ShapeDtypeStruct((rows, cols), jnp.bfloat16),
        cost_estimate=pl.CostEstimate(
            flops=rows * cols, bytes_accessed=6 * rows * cols, transcendentals=0
        ),
        compiler_params=pltpu.CompilerParams(vmem_limit_bytes=VMEM_BYTES),
    )(values)


def key_kernel(rows, keys, cotan, out):
    for h in range(keys.shape[1] // HEAD_DIM):
        spot = pl.ds(h * HEAD_DIM, HEAD_DIM)
        head = keys[:, spot]
        inverse = lax.rsqrt(jnp.mean(head * head, axis=-1, keepdims=True) + 1e-06)
        unit = head * inverse
        upstream = cotan[:, spot].astype(jnp.float32) / rows
        grads = inverse * (upstream - unit * jnp.mean(upstream * unit, axis=-1, keepdims=True))
        out[:, spot] = grads.astype(jnp.bfloat16)


def key_gradient(keys, cotan, unit, rows):
    count, cols = keys.shape
    tile = KEY_TILE if count % KEY_TILE == 0 else count
    block = pl.BlockSpec((tile, cols), lambda i: (i, 0))
    return pl.pallas_call(
        functools.partial(key_kernel, rows),
        grid=(count // tile,),
        in_specs=[block, pl.BlockSpec((tile, cols), lambda i: (i, unit))],
        out_specs=block,
        out_shape=jax.ShapeDtypeStruct(keys.shape, jnp.bfloat16),
        cost_estimate=pl.CostEstimate(
            flops=12 * count * cols, bytes_accessed=8 * count * cols, transcendentals=count
        ),
        compiler_params=pltpu.CompilerParams(vmem_limit_bytes=VMEM_BYTES),
    )(keys, cotan)


def own_kernel(spot, normed, key_grad, out):
    out[...] = lax.dot_general(
        normed[...], key_grad[...], (((0,), (0,)), ((), ())), preferred_element_type=jnp.float32
    )


def own_term(normed, spot, key_grad, depth):
    count, cols = key_grad.shape
    tile = min(depth, OWN_TILE)
    tiles = depth // tile
    return pl.pallas_call(
        own_kernel,
        grid_spec=pltpu.PrefetchScalarGridSpec(
            num_scalar_prefetch=1,
            grid=(tiles,),
            in_specs=[
                pl.BlockSpec((count, tile), lambda i, place: (0, place[0] * tiles + i)),
                pl.BlockSpec((count, cols), lambda i, place: (0, 0)),
            ],
            out_specs=pl.BlockSpec((tile, cols), lambda i, place: (i, 0)),
        ),
        out_shape=jax.ShapeDtypeStruct((depth, cols), jnp.float32),
        cost_estimate=pl.CostEstimate(
            flops=2 * count * cols * depth,
            bytes_accessed=2 * count * depth + 2 * count * cols + 4 * depth * cols,
            transcendentals=0,
        ),
        compiler_params=pltpu.CompilerParams(vmem_limit_bytes=VMEM_BYTES),
    )(spot, normed, key_grad)


def adam_update(weight, first, second, grad, stamp):
    first = beta_one * first + (1.0 - beta_one) * grad
    second = beta_two * second + (1.0 - beta_two) * grad * grad
    fix_one = 1.0 - beta_one**stamp
    fix_two = 1.0 - beta_two**stamp
    ratio = first / fix_one / (jnp.sqrt(second / fix_two) + adam_eps)
    weight = weight - learn_rate * (ratio + weight_decay * weight)
    return (weight, first, second)


def first_kernel(stamp, unit, fragment, anchor, weight, first, second, grad, out_w, out_m, out_v, own):
    fresh, out_m[...], out_v[...] = adam_update(
        weight[...], first[...], second[...], grad[...], stamp
    )
    heads = fresh.shape[1] // HEAD_DIM
    for h in range(heads):
        head = fresh[:, h * HEAD_DIM : (h + 1) * HEAD_DIM]
        merged = mixing * head + (1.0 - mixing) * anchor[...]
        head = jnp.where(fragment[0] == unit * heads + h, merged, head)
        out_w[:, pl.ds(h * HEAD_DIM, HEAD_DIM)] = head
        own[:, pl.ds(h * HEAD_DIM, HEAD_DIM)] = head.astype(jnp.bfloat16)


def first_update(stamp, unit, fragment, anchor, weight, first, second, grad):
    rows, cols = grad.shape
    tile = min(rows, ADAM_TILE)
    block = pl.BlockSpec((tile, cols), lambda i: (i, 0))
    spot = pl.BlockSpec((tile, cols), lambda i: (i, unit))
    side = pl.BlockSpec((tile, HEAD_DIM), lambda i: (i, 0))
    return pl.pallas_call(
        functools.partial(first_kernel, stamp, unit),
        grid=(rows // tile,),
        in_specs=[pl.BlockSpec(memory_space=pltpu.SMEM), side, spot, spot, spot, block],
        out_specs=[block] * 4,
        out_shape=[jax.ShapeDtypeStruct((rows, cols), jnp.float32)] * 3
        + [jax.ShapeDtypeStruct((rows, cols), jnp.bfloat16)],
        cost_estimate=pl.CostEstimate(
            flops=24 * rows * cols, bytes_accessed=32 * rows * cols, transcendentals=rows * cols
        ),
        compiler_params=pltpu.CompilerParams(vmem_limit_bytes=VMEM_BYTES),
    )(fragment, anchor, weight, first, second, grad)


def last_kernel(stamp, weight, first, second, grad, *rest):
    for out, value in zip(
        rest[-3:], adam_update(weight[...], first[...], second[...], grad[...], stamp)
    ):
        out[...] = value


def last_update(stamp, unit, width, weight, first, second, grad, before):
    rows, cols = grad.shape
    tile = min(rows, ADAM_TILE)
    block = pl.BlockSpec((tile, cols), lambda i: (i, 0))
    spot = pl.BlockSpec((tile, cols), lambda i: (i, unit))
    return pl.pallas_call(
        functools.partial(last_kernel, stamp),
        grid=(rows // tile,),
        in_specs=[block] * 4 + [pl.BlockSpec(memory_space=pl.ANY)] * len(before),
        out_specs=[spot] * 3,
        out_shape=[jax.ShapeDtypeStruct((rows, width), jnp.float32)] * 3,
        input_output_aliases={4 + i: i for i in range(len(before))},
        cost_estimate=pl.CostEstimate(
            flops=20 * rows * cols, bytes_accessed=28 * rows * cols, transcendentals=rows * cols
        ),
        compiler_params=pltpu.CompilerParams(vmem_limit_bytes=VMEM_BYTES),
    )(weight, first, second, grad, *before)


def by_rows(array):
    return with_layout_constraint(array, Layout(major_to_minor=(0, 1)))


def sum_replicas(rows):
    count = lax.axis_size("replica")
    if count & (count - 1):
        return lax.psum(rows, "replica")
    step = 1
    while step < count:
        swaps = [(r, r ^ step) for r in range(count)]
        rows = rows + lax.ppermute(rows, "replica", swaps)
        step *= 2
    return rows


def outer_update(total, anchor, momentum):
    average = total / lax.axis_size("replica")
    fresh_mom = outer_momentum * momentum + average
    fresh_anchor = anchor - outer_rate * (outer_momentum * fresh_mom + average)
    return (fresh_anchor, fresh_mom)


def ring_of(count):
    half = count // 2
    return [2 * p if p < half else 2 * (count - 1 - p) + 1 for p in range(count)]


def on_device(tokens, cotangent, params, adam_m, adam_v, anchor, momentum, delta, fragment):
    count = lax.axis_size("fsdp")
    half = count // 2
    ringed = count % 2 == 0 and count <= RING_MOST
    ring = ring_of(count)
    onward = [(ring[p], ring[(p + 1) % count]) for p in range(count)]
    back = [(ring[(p + 1) % count], ring[p]) for p in range(count)]
    index = lax.axis_index("fsdp")
    place = jnp.where(index % 2 == 0, index // 2, count - 1 - index // 2)

    cotan = cotangent[0]
    depth, width = params.shape[1:]
    unit_cols = UNIT_HEADS * HEAD_DIM
    units = width // unit_cols
    rows = tokens.shape[1] * count

    owns = [by_rows(params[0, :, :unit_cols].astype(jnp.bfloat16))]
    owns += [cast_columns(params[0], u, unit_cols) for u in range(1, units)]

    normed = norm_rows(tokens[0])
    normed_at, places = [], []
    for k in range(count if ringed else 0):
        spot = (place + k) % count
        owner = jnp.where(spot < half, 2 * spot, 2 * (count - 1 - spot) + 1)
        normed_at.append(lax.dynamic_slice_in_dim(normed, owner * depth, depth, 1))
        places.append(owner.astype(jnp.int32).reshape(1))

    def gather_whole(current):
        every = lax.all_gather(current, "fsdp", axis=0, tiled=True)
        return jnp.dot(normed, every, preferred_element_type=jnp.float32), every

    def scatter_whole(key_grad, last=False):
        part = lax.dot_general(
            normed, key_grad, (((0,), (0,)), ((), ())), preferred_element_type=jnp.float32
        )
        return lax.psum_scatter(part, "fsdp", scatter_dimension=0, tiled=True)

    def add_rows(k, piece):
        return jnp.dot(normed_at[k], piece, preferred_element_type=jnp.float32)

    def gather_keys(own):
        keys = add_rows(0, own)
        left, right = own, own
        for k in range(1, half):
            left = lax.ppermute(left, "fsdp", onward)
            right = lax.ppermute(right, "fsdp", back)
            keys = keys + add_rows(count - k, left) + add_rows(k, right)
            if k == 2:
                second = (left, right)
        top = lax.ppermute(left[: depth // 2], "fsdp", onward)
        low = lax.ppermute(right[depth // 2 :], "fsdp", back)
        return keys + add_rows(half, jnp.concatenate([top, low], 0)), second

    def grad_part(k, key_grad):
        return lax.dot_general(
            normed_at[k], key_grad, (((0,), (0,)), ((), ())), preferred_element_type=jnp.float32
        )

    def scatter_grad(key_grad, last=False):
        far = by_rows((SCALE * grad_part(half, key_grad)).astype(SENT))
        right = lax.ppermute(far[: depth // 2], "fsdp", onward)
        left = lax.ppermute(far[depth // 2 :], "fsdp", back)
        with_right, right = lax.optimization_barrier((key_grad, right))
        with_left, left = lax.optimization_barrier((key_grad, left))
        zeros = jnp.zeros_like(right)
        right = jnp.concatenate([right, zeros], 0)
        left = jnp.concatenate([zeros, left], 0)
        for k in range(half - 1, 0, -1):
            right = SCALE * grad_part(k, with_right) + right.astype(jnp.float32)
            left = SCALE * grad_part(count - k, with_left) + left.astype(jnp.float32)
            right, left = by_rows(right.astype(SENT)), by_rows(left.astype(SENT))
            right = lax.ppermute(right, "fsdp", onward)
            left = lax.ppermute(left, "fsdp", back)
        own = own_term(normed, places[0], with_left, depth) if last else grad_part(0, with_left)
        return own + (right.astype(jnp.float32) + left.astype(jnp.float32)) / SCALE

    gather, scatter = (gather_keys, scatter_grad) if ringed else (gather_whole, scatter_whole)
    states, key_grads = [None] * units, [None] * units
    for u in range(units):
        keys, arrived = gather(owns[u])
        if u == 0:
            rows_of_delta, _ = lax.optimization_barrier((delta[0], arrived))
            new_anchor, new_momentum = outer_update(sum_replicas(rows_of_delta), anchor, momentum)
        key_grads[u] = key_gradient(keys, cotan, u, rows)
    for u in range(units):
        *states[u], owns[u] = first_update(
            1, u, fragment, new_anchor, params[0], adam_m[0], adam_v[0], scatter(key_grads[u])
        )
    results = ()
    for u in range(units):
        grad = scatter(key_gradient(gather(owns[u])[0], cotan, u, rows), u == units - 1)
        results = last_update(2, u, width, *states[u], grad, results)

    return (*(out[None] for out in results), new_anchor, new_momentum)


def solution(mesh):
    return jax.shard_map(
        on_device,
        mesh=mesh,
        in_specs=(
            P("replica", "fsdp", None),
            P("replica", "fsdp", None),
            P("replica", "fsdp", None),
            P("replica", "fsdp", None),
            P("replica", "fsdp", None),
            P("fsdp", None),
            P("fsdp", None),
            P("replica", "fsdp", None),
            P(),
        ),
        out_specs=(
            P("replica", "fsdp", None),
            P("replica", "fsdp", None),
            P("replica", "fsdp", None),
            P("fsdp", None),
            P("fsdp", None),
        ),
        check_vma=False,
    )
```

```python
import functools

import jax
import jax.numpy as jnp
from jax import lax
from jax.experimental import pallas as pl
from jax.experimental.layout import Layout, with_layout_constraint
from jax.experimental.pallas import tpu as pltpu
from jax.sharding import PartitionSpec as P

HEAD_DIM = 128
KV_HEADS = 4
INNER_STEPS = 2
UNIT_HEADS = 2
RING_MOST = 8
NORM_TILE = 128
CAST_TILE = 512
KEY_TILE = 384
OWN_TILE = 256
ADAM_TILE = 512
VMEM_BYTES = 14 * 2**20
NORM_VMEM_BYTES = 33 * 2**20
SENT = jnp.float16
SCALE = 1.0 / 128


beta_one = 0.9
beta_two = 0.95
adam_eps = 1e-08
learn_rate = 0.002
weight_decay = 0.1
outer_rate = 0.7
outer_momentum = 0.9
mixing = 0.5


def norm_kernel(values, out):
    floats = values[...].astype(jnp.float32)
    scale = lax.rsqrt(jnp.mean(floats * floats, axis=-1, keepdims=True) + 1e-05)
    out[...] = (floats * scale).astype(jnp.bfloat16)


def norm_rows(values):
    rows, width = values.shape
    tile = NORM_TILE if rows % NORM_TILE == 0 else rows
    block = pl.BlockSpec((tile, width), lambda i: (i, 0))
    return pl.pallas_call(
        norm_kernel,
        grid=(rows // tile,),
        in_specs=[block],
        out_specs=block,
        out_shape=jax.ShapeDtypeStruct(values.shape, jnp.bfloat16),
        cost_estimate=pl.CostEstimate(
            flops=8 * rows * width, bytes_accessed=4 * rows * width, transcendentals=rows
        ),
        compiler_params=pltpu.CompilerParams(vmem_limit_bytes=NORM_VMEM_BYTES),
    )(values)


def cast_kernel(values, out):
    out[...] = values[...].astype(jnp.bfloat16)


def cast_columns(values, unit, cols):
    rows = values.shape[0]
    tile = min(rows, CAST_TILE)
    return pl.pallas_call(
        cast_kernel,
        grid=(rows // tile,),
        in_specs=[pl.BlockSpec((tile, cols), lambda i: (i, unit))],
        out_specs=pl.BlockSpec((tile, cols), lambda i: (i, 0)),
        out_shape=jax.ShapeDtypeStruct((rows, cols), jnp.bfloat16),
        cost_estimate=pl.CostEstimate(
            flops=rows * cols, bytes_accessed=6 * rows * cols, transcendentals=0
        ),
        compiler_params=pltpu.CompilerParams(vmem_limit_bytes=VMEM_BYTES),
    )(values)


def key_kernel(rows, keys, cotan, out):
    for h in range(keys.shape[1] // HEAD_DIM):
        spot = pl.ds(h * HEAD_DIM, HEAD_DIM)
        head = keys[:, spot]
        inverse = lax.rsqrt(jnp.mean(head * head, axis=-1, keepdims=True) + 1e-06)
        unit = head * inverse
        upstream = cotan[:, spot].astype(jnp.float32) / rows
        grads = inverse * (upstream - unit * jnp.mean(upstream * unit, axis=-1, keepdims=True))
        out[:, spot] = grads.astype(jnp.bfloat16)


def key_gradient(keys, cotan, unit, rows):
    count, cols = keys.shape
    tile = KEY_TILE if count % KEY_TILE == 0 else count
    block = pl.BlockSpec((tile, cols), lambda i: (i, 0))
    return pl.pallas_call(
        functools.partial(key_kernel, rows),
        grid=(count // tile,),
        in_specs=[block, pl.BlockSpec((tile, cols), lambda i: (i, unit))],
        out_specs=block,
        out_shape=jax.ShapeDtypeStruct(keys.shape, jnp.bfloat16),
        cost_estimate=pl.CostEstimate(
            flops=12 * count * cols, bytes_accessed=8 * count * cols, transcendentals=count
        ),
        compiler_params=pltpu.CompilerParams(vmem_limit_bytes=VMEM_BYTES),
    )(keys, cotan)


def own_kernel(spot, normed, key_grad, out):
    out[...] = lax.dot_general(
        normed[...], key_grad[...], (((0,), (0,)), ((), ())), preferred_element_type=jnp.float32
    )


def own_term(normed, spot, key_grad, depth):
    count, cols = key_grad.shape
    tile = min(depth, OWN_TILE)
    tiles = depth // tile
    return pl.pallas_call(
        own_kernel,
        grid_spec=pltpu.PrefetchScalarGridSpec(
            num_scalar_prefetch=1,
            grid=(tiles,),
            in_specs=[
                pl.BlockSpec((count, tile), lambda i, place: (0, place[0] * tiles + i)),
                pl.BlockSpec((count, cols), lambda i, place: (0, 0)),
            ],
            out_specs=pl.BlockSpec((tile, cols), lambda i, place: (i, 0)),
        ),
        out_shape=jax.ShapeDtypeStruct((depth, cols), jnp.float32),
        cost_estimate=pl.CostEstimate(
            flops=2 * count * cols * depth,
            bytes_accessed=2 * count * depth + 2 * count * cols + 4 * depth * cols,
            transcendentals=0,
        ),
        compiler_params=pltpu.CompilerParams(vmem_limit_bytes=VMEM_BYTES),
    )(spot, normed, key_grad)


def adam_update(weight, first, second, grad, stamp):
    first = beta_one * first + (1.0 - beta_one) * grad
    second = beta_two * second + (1.0 - beta_two) * grad * grad
    fix_one = 1.0 - beta_one**stamp
    fix_two = 1.0 - beta_two**stamp
    ratio = first / fix_one / (jnp.sqrt(second / fix_two) + adam_eps)
    weight = weight - learn_rate * (ratio + weight_decay * weight)
    return (weight, first, second)


def first_kernel(stamp, unit, fragment, anchor, weight, first, second, grad, out_w, out_m, out_v, own):
    fresh, out_m[...], out_v[...] = adam_update(
        weight[...], first[...], second[...], grad[...], stamp
    )
    heads = fresh.shape[1] // HEAD_DIM
    for h in range(heads):
        head = fresh[:, h * HEAD_DIM : (h + 1) * HEAD_DIM]
        merged = mixing * head + (1.0 - mixing) * anchor[...]
        head = jnp.where(fragment[0] == unit * heads + h, merged, head)
        out_w[:, pl.ds(h * HEAD_DIM, HEAD_DIM)] = head
        own[:, pl.ds(h * HEAD_DIM, HEAD_DIM)] = head.astype(jnp.bfloat16)


def first_update(stamp, unit, fragment, anchor, weight, first, second, grad):
    rows, cols = grad.shape
    tile = min(rows, ADAM_TILE)
    block = pl.BlockSpec((tile, cols), lambda i: (i, 0))
    spot = pl.BlockSpec((tile, cols), lambda i: (i, unit))
    side = pl.BlockSpec((tile, HEAD_DIM), lambda i: (i, 0))
    return pl.pallas_call(
        functools.partial(first_kernel, stamp, unit),
        grid=(rows // tile,),
        in_specs=[pl.BlockSpec(memory_space=pltpu.SMEM), side, spot, spot, spot, block],
        out_specs=[block] * 4,
        out_shape=[jax.ShapeDtypeStruct((rows, cols), jnp.float32)] * 3
        + [jax.ShapeDtypeStruct((rows, cols), jnp.bfloat16)],
        cost_estimate=pl.CostEstimate(
            flops=24 * rows * cols, bytes_accessed=32 * rows * cols, transcendentals=rows * cols
        ),
        compiler_params=pltpu.CompilerParams(vmem_limit_bytes=VMEM_BYTES),
    )(fragment, anchor, weight, first, second, grad)


def last_kernel(stamp, weight, first, second, grad, *rest):
    for out, value in zip(
        rest[-3:], adam_update(weight[...], first[...], second[...], grad[...], stamp)
    ):
        out[...] = value


def last_update(stamp, unit, width, weight, first, second, grad, before):
    rows, cols = grad.shape
    tile = min(rows, ADAM_TILE)
    block = pl.BlockSpec((tile, cols), lambda i: (i, 0))
    spot = pl.BlockSpec((tile, cols), lambda i: (i, unit))
    return pl.pallas_call(
        functools.partial(last_kernel, stamp),
        grid=(rows // tile,),
        in_specs=[block] * 4 + [pl.BlockSpec(memory_space=pl.ANY)] * len(before),
        out_specs=[spot] * 3,
        out_shape=[jax.ShapeDtypeStruct((rows, width), jnp.float32)] * 3,
        input_output_aliases={4 + i: i for i in range(len(before))},
        cost_estimate=pl.CostEstimate(
            flops=20 * rows * cols, bytes_accessed=28 * rows * cols, transcendentals=rows * cols
        ),
        compiler_params=pltpu.CompilerParams(vmem_limit_bytes=VMEM_BYTES),
    )(weight, first, second, grad, *before)


def by_rows(array):
    return with_layout_constraint(array, Layout(major_to_minor=(0, 1)))


def sum_replicas(rows):
    count = lax.axis_size("replica")
    if count & (count - 1):
        return lax.psum(rows, "replica")
    step = 1
    while step < count:
        swaps = [(r, r ^ step) for r in range(count)]
        rows = rows + lax.ppermute(rows, "replica", swaps)
        step *= 2
    return rows


def outer_update(total, anchor, momentum):
    average = total / lax.axis_size("replica")
    fresh_mom = outer_momentum * momentum + average
    fresh_anchor = anchor - outer_rate * (outer_momentum * fresh_mom + average)
    return (fresh_anchor, fresh_mom)


def ring_of(count):
    half = count // 2
    return [2 * p if p < half else 2 * (count - 1 - p) + 1 for p in range(count)]


def on_device(tokens, cotangent, params, adam_m, adam_v, anchor, momentum, delta, fragment):
    count = lax.axis_size("fsdp")
    half = count // 2
    ringed = count % 2 == 0 and count <= RING_MOST
    ring = ring_of(count)
    onward = [(ring[p], ring[(p + 1) % count]) for p in range(count)]
    back = [(ring[(p + 1) % count], ring[p]) for p in range(count)]
    index = lax.axis_index("fsdp")
    place = jnp.where(index % 2 == 0, index // 2, count - 1 - index // 2)

    cotan = cotangent[0]
    depth, width = params.shape[1:]
    unit_cols = UNIT_HEADS * HEAD_DIM
    units = width // unit_cols
    rows = tokens.shape[1] * count

    owns = [by_rows(params[0, :, :unit_cols].astype(jnp.bfloat16))]
    owns += [cast_columns(params[0], u, unit_cols) for u in range(1, units)]

    normed = norm_rows(tokens[0])
    normed_at, places = [], []
    for k in range(count if ringed else 0):
        spot = (place + k) % count
        owner = jnp.where(spot < half, 2 * spot, 2 * (count - 1 - spot) + 1)
        normed_at.append(lax.dynamic_slice_in_dim(normed, owner * depth, depth, 1))
        places.append(owner.astype(jnp.int32).reshape(1))

    def gather_whole(current):
        every = lax.all_gather(current, "fsdp", axis=0, tiled=True)
        return jnp.dot(normed, every, preferred_element_type=jnp.float32), every

    def scatter_whole(key_grad, last=False):
        part = lax.dot_general(
            normed, key_grad, (((0,), (0,)), ((), ())), preferred_element_type=jnp.float32
        )
        return lax.psum_scatter(part, "fsdp", scatter_dimension=0, tiled=True)

    def add_rows(k, piece):
        return jnp.dot(normed_at[k], piece, preferred_element_type=jnp.float32)

    def gather_keys(own):
        keys = add_rows(0, own)
        left, right = own, own
        for k in range(1, half):
            left = lax.ppermute(left, "fsdp", onward)
            right = lax.ppermute(right, "fsdp", back)
            keys = keys + add_rows(count - k, left) + add_rows(k, right)
            if k == 2:
                second = (left, right)
        top = lax.ppermute(left[: depth // 2], "fsdp", onward)
        low = lax.ppermute(right[depth // 2 :], "fsdp", back)
        return keys + add_rows(half, jnp.concatenate([top, low], 0)), second

    def grad_part(k, key_grad):
        return lax.dot_general(
            normed_at[k], key_grad, (((0,), (0,)), ((), ())), preferred_element_type=jnp.float32
        )

    def scatter_grad(key_grad, last=False):
        far = by_rows((SCALE * grad_part(half, key_grad)).astype(SENT))
        right = lax.ppermute(far[: depth // 2], "fsdp", onward)
        left = lax.ppermute(far[depth // 2 :], "fsdp", back)
        with_right, right = lax.optimization_barrier((key_grad, right))
        with_left, left = lax.optimization_barrier((key_grad, left))
        zeros = jnp.zeros_like(right)
        right = jnp.concatenate([right, zeros], 0)
        left = jnp.concatenate([zeros, left], 0)
        for k in range(half - 1, 0, -1):
            right = SCALE * grad_part(k, with_right) + right.astype(jnp.float32)
            left = SCALE * grad_part(count - k, with_left) + left.astype(jnp.float32)
            right, left = by_rows(right.astype(SENT)), by_rows(left.astype(SENT))
            right = lax.ppermute(right, "fsdp", onward)
            left = lax.ppermute(left, "fsdp", back)
        own = own_term(normed, places[0], with_left, depth) if last else grad_part(0, with_left)
        return own + (right.astype(jnp.float32) + left.astype(jnp.float32)) / SCALE

    gather, scatter = (gather_keys, scatter_grad) if ringed else (gather_whole, scatter_whole)
    states, key_grads = [None] * units, [None] * units
    for u in range(units):
        keys, arrived = gather(owns[u])
        if u == 0:
            rows_of_delta, _ = lax.optimization_barrier((delta[0], arrived))
            new_anchor, new_momentum = outer_update(sum_replicas(rows_of_delta), anchor, momentum)
        key_grads[u] = key_gradient(keys, cotan, u, rows)
    for u in range(units):
        *states[u], owns[u] = first_update(
            1, u, fragment, new_anchor, params[0], adam_m[0], adam_v[0], scatter(key_grads[u])
        )
    results = ()
    for u in range(units):
        grad = scatter(key_gradient(gather(owns[u])[0], cotan, u, rows), u == units - 1)
        results = last_update(2, u, width, *states[u], grad, results)

    return (*(out[None] for out in results), new_anchor, new_momentum)


def solution(mesh):
    return jax.shard_map(
        on_device,
        mesh=mesh,
        in_specs=(
            P("replica", "fsdp", None),
            P("replica", "fsdp", None),
            P("replica", "fsdp", None),
            P("replica", "fsdp", None),
            P("replica", "fsdp", None),
            P("fsdp", None),
            P("fsdp", None),
            P("replica", "fsdp", None),
            P(),
        ),
        out_specs=(
            P("replica", "fsdp", None),
            P("replica", "fsdp", None),
            P("replica", "fsdp", None),
            P("fsdp", None),
            P("fsdp", None),
        ),
        check_vma=False,
    )
```
